512 devices in a mesh: row: 16 (over z), col: 32 (over x, y, core).
Axes of the slice: x: 4, y: 4, z: 16, core: 2. Of those that a mesh axis runs over, the one named last changes fastest.
Arguments:
- activations: bfloat16 [2048, 6144], P('row', 'col'), may hold values from -6 to 6
- out_grad: bfloat16 [2048, 49152], P('row', 'col'), may hold values from -6 to 6
- weight_slots: bfloat16 [32, 16, 512, 512], P('col', 'row'), may hold values from -0.15625 to 0.15625
- block_mask: int32 [96, 12], replicated, may hold values from 0 to 1, as said below
- block_owner: int32 [96, 12], replicated, may hold values from 0 to 15, as said below
Outputs:
- outputs: bfloat16 [2048, 49152], P('row', 'col')
- in_grad: bfloat16 [2048, 6144], P('row', 'col')
- weight_grad: bfloat16 [32, 16, 512, 512], P('col', 'row')
The draws below stay inside these ranges and needn't reach their ends.
Inputs may be any that keep to these rules, and one draw needn't show every extreme that they name: `block_mask`: in each group of block rows (3 rows of 12 blocks) exactly a quarter of the blocks are nonzero. `block_owner`: among the nonzero blocks of one group, no index of row owns more than 1, and some index owns exactly 1.
All inputs are finite; a program needn't handle non-finite values.
Results may differ from the reference program's by a relative error of at most 0.005.
Values may be sent and summed in bfloat16 or wider, within the bound.
No kernel may reach another device: no remote copies, remote signals or barrier semaphores. Data moves between devices by JAX's collectives and lax.ppermute only.
A program may use at most 64 MiB of HBM per device.

```python
import math
import jax
import jax.numpy as jnp
from jax import lax

D = 6144
FF = 49152
BLK = 512
TOKENS = 2048
SLOTS = 1
N_ROW = 16
N_COL = 32


def shared_layout(key):
    group_rows = FF // BLK // N_COL
    model_blocks = D // BLK
    group_size = group_rows * model_blocks
    nonzero_count = group_size // 4
    group_keys = jax.random.split(key, N_COL)

    def one_group(group_key):
        split_keys = jax.random.split(group_key, 5)
        shuffle = jax.random.permutation(split_keys[0], group_size).astype(jnp.int32)
        placing = jnp.zeros((group_size,), jnp.int32).at[shuffle].set(jnp.arange(group_size, dtype=jnp.int32))
        chosen = (placing < nonzero_count).astype(jnp.int32)
        busiest = jax.random.randint(split_keys[1], (), 0, N_ROW).astype(jnp.int32)
        others = (jax.random.permutation(split_keys[2], (N_ROW - 1) * SLOTS) // SLOTS).astype(jnp.int32)
        others = others + (others >= busiest).astype(jnp.int32)
        tickets = jnp.concatenate([jnp.full((SLOTS,), busiest, jnp.int32), others])[:nonzero_count]
        tickets = jax.random.permutation(split_keys[3], tickets)
        rank_list = jnp.cumsum(chosen) - 1
        assigned = tickets[jnp.clip(rank_list, 0, nonzero_count - 1)]
        spare_owner = jax.random.randint(split_keys[4], (group_size,), 0, N_ROW).astype(jnp.int32)
        owner_map = jnp.where(chosen == 1, assigned, spare_owner).astype(jnp.int32)
        return (chosen, owner_map)
    chosen, owner_map = jax.vmap(one_group)(group_keys)
    return (chosen.reshape(FF // BLK, model_blocks), owner_map.reshape(FF // BLK, model_blocks))


def draw_block_mask(key, part):
    layout = shared_layout(key)
    return layout[0].astype(jnp.int32)


def draw_block_owner(key, part):
    layout = shared_layout(key)
    return layout[1].astype(jnp.int32)


def levels(rng, shape, cuts, least, high):
    level = 1.0
    for position, blocks in cuts:
        steps = jax.random.uniform(jax.random.fold_in(jax.random.fold_in(rng, 6), position), (blocks,), jnp.float32, least / len(cuts), high / len(cuts))
        level = level * jnp.repeat(jnp.exp(steps), shape[position] // blocks).reshape((-1,) + (1,) * (len(shape) - 1 - position))
    return level


def noise(stream_key, dims, deviation, reach, pieces=(), kind=jnp.bfloat16):
    factor_of = levels(stream_key, dims, pieces, -0.22, 0.18) if pieces else 1.0
    drawn = jax.random.normal(stream_key, dims, jnp.float32) * deviation * factor_of
    return jnp.minimum(jnp.maximum(drawn, -reach), reach).astype(kind)


def setup_inputs(seed: int = 0) -> dict:
    key_list = jax.random.split(jax.random.key(seed), 6)
    activations = noise(key_list[0], (TOKENS, D), 1.0, 6.0, ((0, 16), (1, 32)))
    out_grad = noise(key_list[1], (TOKENS, FF), 1.0, 6.0, ((0, 16), (1, 32)))
    weight_slots = noise(key_list[2], (N_COL, N_ROW * SLOTS, BLK, BLK), (D // 4) ** -0.5, 0.15625, ((0, 32), (1, 16)))
    block_mask = draw_block_mask(jax.random.fold_in(key_list[5], 71), 0)
    block_owner = draw_block_owner(jax.random.fold_in(key_list[5], 71), 0)
    return dict(activations=activations, out_grad=out_grad, weight_slots=weight_slots, block_mask=block_mask, block_owner=block_owner)


def slot_table(block_mask, block_owner):
    group_rows = FF // BLK // N_COL
    model_blocks = D // BLK
    group_size = group_rows * model_blocks
    mask_rows = block_mask.reshape(N_COL, group_size)
    owner_rows = block_owner.reshape(N_COL, group_size)
    owner_ids = jnp.arange(N_ROW, dtype=jnp.int32)
    chosen = ((mask_rows[:, None, :] == 1) & (owner_rows[:, None, :] == owner_ids[None, :, None])).astype(jnp.int32)
    rank_list = (jnp.cumsum(chosen, axis=2) - 1).astype(jnp.int32)
    slot_index = lax.optimization_barrier(jnp.sum(chosen * rank_list, axis=1)).astype(jnp.int32)
    return (owner_rows * SLOTS + slot_index).reshape(FF // BLK, model_blocks).astype(jnp.int32)

def reference(activations, out_grad, weight_slots, block_mask, block_owner):
    group_rows = FF // BLK // N_COL
    model_blocks = D // BLK
    hidden_blocks = FF // BLK
    nonzero_count = hidden_blocks * model_blocks // 4
    slot_ids = slot_table(block_mask, block_owner)
    listed = jnp.nonzero(block_mask.reshape(-1), size=nonzero_count)[0].astype(jnp.int32)
    act_blocks = activations.reshape(TOKENS, model_blocks, BLK)
    grad_blocks = out_grad.reshape(TOKENS, hidden_blocks, BLK)
    grad_scale = 1.0 / math.sqrt(TOKENS)

    def accumulate(carry_pair, block_id):
        out_sum, in_sum = carry_pair
        hidden_row = (block_id // model_blocks).astype(jnp.int32)
        model_col = (block_id % model_blocks).astype(jnp.int32)
        slot_here = slot_ids[hidden_row, model_col]
        weight_block = weight_slots[hidden_row // group_rows, slot_here]
        act_panel = lax.dynamic_index_in_dim(act_blocks, model_col, 1, keepdims=False)
        grad_panel = lax.dynamic_index_in_dim(grad_blocks, hidden_row, 1, keepdims=False)
        partial_out = jnp.dot(act_panel, weight_block.T, preferred_element_type=jnp.float32).astype(jnp.bfloat16)
        partial_in = jnp.dot(grad_panel, weight_block, preferred_element_type=jnp.float32).astype(jnp.bfloat16)
        block_grad = (jnp.dot(grad_panel.T, act_panel, preferred_element_type=jnp.float32) * grad_scale).astype(jnp.bfloat16)
        out_sum = out_sum.at[:, hidden_row].add(partial_out.astype(jnp.float32))
        in_sum = in_sum.at[:, model_col].add(partial_in.astype(jnp.float32))
        return ((out_sum, in_sum), block_grad)
    start_pair = (jnp.zeros((TOKENS, hidden_blocks, BLK), jnp.float32), jnp.zeros((TOKENS, model_blocks, BLK), jnp.float32))
    (out_sum, in_sum), grads = lax.scan(accumulate, start_pair, listed)
    group_of = (listed // model_blocks // group_rows).astype(jnp.int32)
    slot_of = slot_ids.reshape(-1)[listed].astype(jnp.int32)
    weight_grad = jnp.zeros(weight_slots.shape, jnp.bfloat16).at[group_of, slot_of].set(grads)
    outputs = out_sum.reshape(TOKENS, FF).astype(jnp.bfloat16)
    in_grad = in_sum.reshape(TOKENS, D).astype(jnp.bfloat16)
    return (outputs, in_grad, weight_grad)
```

```python
import functools
import math

import jax
import jax.numpy as jnp
from jax import lax
from jax.experimental import pallas as pl
from jax.experimental.pallas import tpu as pltpu
from jax.sharding import PartitionSpec as P

BF = jnp.bfloat16
F32 = jnp.float32
NX, NY, NC = 4, 4, 2
VMEM_BYTES = 48 * 1024 * 1024


def col_of(x, y, c):
    return (x * NY + y) * NC + c


X_GROUPS = [[col_of(x, y, c) for x in range(NX)] for y in range(NY) for c in range(NC)]
Y_GROUPS = [[col_of(x, y, c) for y in range(NY)] for x in range(NX) for c in range(NC)]
CORE_SWAP = [(i, i ^ 1) for i in range(NX * NY * NC)]


def tokens_kernel(meta, act_ref, grad_ref, w_ref, out_ref, in_ref, out_acc, in_acc, *, blk):
    step = pl.program_id(0)

    @pl.when(step == 0)
    def _():
        out_acc[...] = jnp.zeros_like(out_acc)
        in_acc[...] = jnp.zeros_like(in_acc)

    hid = pl.ds(pl.multiple_of(meta[1, step] * blk, blk), blk)
    mod = pl.ds(pl.multiple_of(meta[2, step] * blk, blk), blk)
    w = w_ref[0]
    out_acc[hid, :] += jnp.dot(w, act_ref[mod, :], preferred_element_type=F32)
    in_acc[:, mod] += jnp.dot(grad_ref[:, hid], w, preferred_element_type=F32)

    @pl.when(step == pl.num_programs(0) - 1)
    def _():
        out_ref[...] = out_acc[...].T.astype(BF)
        in_ref[...] = in_acc[...].T.astype(BF)


def tokens_step(meta, act_t, grad, w_all):
    blk = w_all.shape[1]
    feats, toks = act_t.shape
    hidden = grad.shape[1]
    whole = lambda k, m: (0, 0)
    return pl.pallas_call(
        functools.partial(tokens_kernel, blk=blk),
        grid_spec=pltpu.PrefetchScalarGridSpec(
            num_scalar_prefetch=1,
            grid=(meta.shape[1],),
            in_specs=[
                pl.BlockSpec((feats, toks), whole),
                pl.BlockSpec((toks, hidden), whole),
                pl.BlockSpec((1, blk, blk), lambda k, m: (m[0, k], 0, 0)),
            ],
            out_specs=[
                pl.BlockSpec((toks, hidden), whole),
                pl.BlockSpec((feats, toks), whole),
            ],
            scratch_shapes=[pltpu.VMEM((hidden, toks), F32), pltpu.VMEM((toks, feats), F32)],
        ),
        out_shape=[
            jax.ShapeDtypeStruct((toks, hidden), BF),
            jax.ShapeDtypeStruct((feats, toks), BF),
        ],
        compiler_params=pltpu.CompilerParams(vmem_limit_bytes=VMEM_BYTES),
        name="tokens_step",
    )(meta, act_t, grad, w_all)


def wgrad_kernel(core, grad_ref, own_ref, oth_ref, out_ref, a_buf, b_buf, *, scale):
    n_x, n_z, rows, toks = grad_ref.shape
    piece = own_ref.shape[2]

    @pl.when(pl.program_id(0) == 0)
    def _():
        for x in range(n_x):
            for z in range(n_z):
                a_buf[x * rows : (x + 1) * rows, z * toks : (z + 1) * toks] = grad_ref[x, z]

    own_rows = pl.ds(pl.multiple_of(core[0] * piece, piece), piece)
    oth_rows = pl.ds(pl.multiple_of((1 - core[0]) * piece, piece), piece)
    for z in range(n_z):
        b_buf[own_rows, z * toks : (z + 1) * toks] = own_ref[0, z]
        b_buf[oth_rows, z * toks : (z + 1) * toks] = oth_ref[0, z]
    prod = lax.dot_general(
        a_buf[...], b_buf[...], (((1,), (1,)), ((), ())), preferred_element_type=F32
    )
    out_ref[...] = (prod * scale).astype(BF)


def wgrad_products(core, grad_x, act_own, act_oth, scale):
    n_x, n_z, rows, toks = grad_x.shape
    n_y, _, piece, _ = act_own.shape
    span = NC * piece
    block = pl.BlockSpec((1, n_z, piece, toks), lambda y, m: (y, 0, 0, 0))
    return pl.pallas_call(
        functools.partial(wgrad_kernel, scale=scale),
        grid_spec=pltpu.PrefetchScalarGridSpec(
            num_scalar_prefetch=1,
            grid=(n_y,),
            in_specs=[
                pl.BlockSpec((n_x, n_z, rows, toks), lambda y, m: (0, 0, 0, 0)),
                block,
                block,
            ],
            out_specs=pl.BlockSpec((n_x * rows, span), lambda y, m: (0, y)),
            scratch_shapes=[
                pltpu.VMEM((n_x * rows, n_z * toks), BF),
                pltpu.VMEM((span, n_z * toks), BF),
            ],
        ),
        out_shape=jax.ShapeDtypeStruct((n_x * rows, n_y * span), BF),
        compiler_params=pltpu.CompilerParams(vmem_limit_bytes=VMEM_BYTES),
        name="wgrad_products",
    )(core, grad_x, act_own, act_oth)


def slots_kernel(meta, prod_ref, out_ref, *, chunk, blk, per_x):
    for s in range(out_ref.shape[0]):
        hid, mod, full = meta[0, s], meta[1, s], meta[2, s]
        rows = pl.ds(pl.multiple_of(hid * chunk, chunk), chunk)
        cols = pl.ds(pl.multiple_of(lax.rem(mod, per_x) * blk, blk), blk)
        part = prod_ref[lax.div(mod, per_x), rows, cols]
        out_ref[s] = jnp.where(full > 0, part, jnp.zeros_like(part))


def pick_slots(meta, prods, chunk, blk):
    owners = meta.shape[1]
    return pl.pallas_call(
        functools.partial(slots_kernel, chunk=chunk, blk=blk, per_x=prods.shape[2] // blk),
        in_specs=[
            pl.BlockSpec(memory_space=pltpu.SMEM),
            pl.BlockSpec(memory_space=pltpu.VMEM),
        ],
        out_specs=pl.BlockSpec(memory_space=pltpu.VMEM),
        out_shape=jax.ShapeDtypeStruct((owners, chunk, blk), BF),
        compiler_params=pltpu.CompilerParams(vmem_limit_bytes=VMEM_BYTES),
        name="pick_slots",
    )(meta, prods)


def layout_tables(block_mask, block_owner, group, n_groups, owners):
    per_group = block_mask.shape[0] // n_groups
    model_blocks = block_mask.shape[1]
    size = per_group * model_blocks
    mask = lax.dynamic_slice_in_dim(block_mask, group * per_group, per_group, 0).reshape(size)
    owner = lax.dynamic_slice_in_dim(block_owner, group * per_group, per_group, 0).reshape(size)
    ids = jnp.arange(size, dtype=jnp.int32)
    before = jnp.sum(jnp.where(ids[:, None] < ids[None, :], mask[:, None], 0), axis=0)
    count = size // 4
    ranked = jnp.where(
        (before[None, :] == jnp.arange(count, dtype=jnp.int32)[:, None]) & (mask[None, :] == 1), 1, 0
    )
    id_of = jnp.sum(ranked * ids[None, :], axis=1)
    owner_of = jnp.sum(ranked * owner[None, :], axis=1)
    listed = jnp.stack([owner_of, id_of // model_blocks, id_of % model_blocks])
    held = jnp.where(
        (owner[None, :] == jnp.arange(owners, dtype=jnp.int32)[:, None]) & (mask[None, :] == 1), 1, 0
    )
    full = jnp.sum(held, axis=1)
    id_at = jnp.sum(held * ids[None, :], axis=1)
    slots = jnp.stack([id_at // model_blocks, id_at % model_blocks, full])
    return listed, slots


def share(x, groups):
    n = len(groups[0])
    wide = jnp.broadcast_to(x[None], (n, *x.shape))
    return lax.all_to_all(wide, "col", 0, 0, tiled=True, axis_index_groups=groups)


def per_device(activations, out_grad, weight_slots, block_mask, block_owner):
    blk = weight_slots.shape[2]
    owners, groups = lax.axis_size("row"), lax.axis_size("col")
    group = lax.axis_index("col")
    toks, piece = activations.shape
    hidden = out_grad.shape[1]
    hid_blocks = hidden // blk
    chunk = blk // owners
    listed, slots = layout_tables(block_mask, block_owner, group, groups, owners)

    w_all = lax.all_gather(weight_slots[0, 0], "row", axis=0)
    act_t = activations.T
    grad_t = out_grad.T

    act_z = lax.all_gather(act_t, "row", axis=0)
    grad_send = grad_t.reshape(hid_blocks, owners, chunk, toks).transpose(1, 0, 2, 3)
    grad_z = lax.all_to_all(
        grad_send.reshape(owners, hid_blocks * chunk, toks), "row", 0, 0, tiled=True
    )
    act_own = share(act_z, Y_GROUPS).reshape(NY, owners, piece, toks)
    act_oth = lax.ppermute(act_own, "col", CORE_SWAP)
    grad_x = share(grad_z, X_GROUPS).reshape(NX, owners, hid_blocks * chunk, toks)
    core = lax.rem(group, NC).reshape(1).astype(jnp.int32)
    scale = 1.0 / math.sqrt(toks * owners)
    prods = wgrad_products(core, grad_x, act_own, act_oth, scale)
    prods = lax.all_to_all(
        prods.reshape(NX, hid_blocks * chunk, -1),
        "col",
        0,
        0,
        tiled=True,
        axis_index_groups=X_GROUPS,
    )
    slot_parts = pick_slots(slots, prods, chunk, blk)
    weight_grad = lax.all_to_all(slot_parts, "row", 0, 0, tiled=True).reshape(1, 1, blk, blk)

    act_all = lax.all_to_all(
        jnp.broadcast_to(act_t[None], (groups, piece, toks)), "col", 0, 0, tiled=True
    ).reshape(groups * piece, toks)
    outputs, in_part = tokens_step(listed, act_all, out_grad, w_all)
    in_recv = lax.all_to_all(in_part.reshape(groups, piece, toks), "col", 0, 0, tiled=True)
    in_grad = jnp.sum(in_recv.astype(F32), axis=0).astype(BF).T
    return outputs, in_grad, weight_grad


def solution(mesh):
    placed = (P("row", "col"), P("row", "col"), P("col", "row", None, None), P(), P())
    return jax.shard_map(
        per_device,
        mesh=mesh,
        in_specs=placed,
        out_specs=(P("row", "col"), P("row", "col"), P("col", "row", None, None)),
        check_vma=False,
    )
```

```python
import functools
import math

import jax
import jax.numpy as jnp
from jax import lax
from jax.experimental import pallas as pl
from jax.experimental.pallas import tpu as pltpu
from jax.sharding import PartitionSpec as P

BF = jnp.bfloat16
F32 = jnp.float32
NX, NY, NC = 4, 4, 2
PARAMS = pltpu.CompilerParams(vmem_limit_bytes=48 * 1024 * 1024)


def col_of(x, y, c):
    return (x * NY + y) * NC + c


PLANE = [(x, y, c) for x in range(NX) for y in range(NY) for c in range(NC)]
XC_GROUPS = [[col_of(x, y, c) for x in range(NX) for c in range(NC)] for y in range(NY)]
Y_GROUPS = [[col_of(x, y, c) for y in range(NY)] for x in range(NX) for c in range(NC)]
CORE_SWAP = [(col_of(x, y, c), col_of(x, y, 1 - c)) for x, y, c in PLANE]
X_SHIFTS = {s: [(col_of(x, y, c), col_of((x + s) % NX, y, c)) for x, y, c in PLANE] for s in range(1, NX)}


def aligned(start, size, step):
    return pl.ds(pl.multiple_of(start, step), size)


def tokens_kernel(meta, place, own_ref, oth_ref, grad_ref, w_ref, out_ref, in_ref, act, out_acc, in_acc, *, blk):
    step = pl.program_id(0)

    @pl.when(step == 0)
    def _():
        out_acc[...] = jnp.zeros_like(out_acc)
        in_acc[...] = jnp.zeros_like(in_acc)
        piece = own_ref.shape[2]
        x, core = place[0], place[1]
        for s in range(NX):
            line = lax.rem(x - s + NX, NX) * NY
            for y in range(NY):
                act[aligned(((line + y) * NC + core) * piece, piece, 64), :] = own_ref[s, y]
                act[aligned(((line + y) * NC + 1 - core) * piece, piece, 64), :] = oth_ref[s, y]

    hid = aligned(meta[1, step] * blk, blk, blk)
    mod = aligned(meta[2, step] * blk, blk, blk)
    w = w_ref[0]
    out_acc[hid, :] += jnp.dot(w, act[mod, :], preferred_element_type=F32)
    in_acc[:, mod] += jnp.dot(grad_ref[:, hid], w, preferred_element_type=F32)

    @pl.when(step == pl.num_programs(0) - 1)
    def _():
        out_ref[...] = out_acc[...].T.astype(BF)
        in_ref[...] = in_acc[...].T.astype(BF)


def tokens_step(meta, place, act_own, act_oth, grad, w_all):
    blk = w_all.shape[1]
    piece, toks = act_own.shape[2:]
    feats = NX * NY * NC * piece
    hidden = grad.shape[1]
    lines = pl.BlockSpec((NX, NY, piece, toks), lambda k, m, p: (0, 0, 0, 0))
    whole = lambda k, m, p: (0, 0)
    return pl.pallas_call(
        functools.partial(tokens_kernel, blk=blk),
        grid_spec=pltpu.PrefetchScalarGridSpec(
            num_scalar_prefetch=2,
            grid=(meta.shape[1],),
            in_specs=[
                lines,
                lines,
                pl.BlockSpec((toks, hidden), whole),
                pl.BlockSpec((1, blk, blk), lambda k, m, p: (m[0, k], 0, 0)),
            ],
            out_specs=[
                pl.BlockSpec((toks, hidden), whole),
                pl.BlockSpec((feats, toks), whole),
            ],
            scratch_shapes=[
                pltpu.VMEM((feats, toks), BF),
                pltpu.VMEM((hidden, toks), F32),
                pltpu.VMEM((toks, feats), F32),
            ],
        ),
        out_shape=[
            jax.ShapeDtypeStruct((toks, hidden), BF),
            jax.ShapeDtypeStruct((feats, toks), BF),
        ],
        compiler_params=PARAMS,
        name="tokens_step",
    )(meta, place, act_own, act_oth, grad, w_all)


def wgrad_kernel(place, own_ref, oth_ref, act_ref, out_ref, a_buf, b_buf, *, scale):
    n_x, n_z, rows, toks = own_ref.shape
    n_y, _, piece, _ = act_ref.shape
    x, core = place[0], place[1]

    @pl.when(pl.program_id(0) == 0)
    def _():
        for s in range(n_x):
            line = lax.rem(x - s + n_x, n_x) * NC
            for z in range(n_z):
                a_buf[aligned((line + core) * rows, rows, rows), z * toks : (z + 1) * toks] = own_ref[s, z]
                a_buf[aligned((line + 1 - core) * rows, rows, rows), z * toks : (z + 1) * toks] = oth_ref[s, z]

    for y in range(n_y):
        for z in range(n_z):
            b_buf[y * piece : (y + 1) * piece, z * toks : (z + 1) * toks] = act_ref[y, z]
    prod = lax.dot_general(
        a_buf[...], b_buf[...], (((1,), (1,)), ((), ())), preferred_element_type=F32
    )
    out_ref[...] = (prod * scale).astype(BF)


def wgrad_products(place, grad_own, grad_oth, act_own, scale):
    n_x, n_z, rows, toks = grad_own.shape
    n_y, _, piece, _ = act_own.shape
    step_y = 2
    span = step_y * piece
    lines = pl.BlockSpec((n_x, n_z, rows, toks), lambda y, p: (0, 0, 0, 0))
    return pl.pallas_call(
        functools.partial(wgrad_kernel, scale=scale),
        grid_spec=pltpu.PrefetchScalarGridSpec(
            num_scalar_prefetch=1,
            grid=(n_y // step_y,),
            in_specs=[
                lines,
                lines,
                pl.BlockSpec((step_y, n_z, piece, toks), lambda y, p: (y, 0, 0, 0)),
            ],
            out_specs=pl.BlockSpec((n_x * NC * rows, span), lambda y, p: (0, y)),
            scratch_shapes=[
                pltpu.VMEM((n_x * NC * rows, n_z * toks), BF),
                pltpu.VMEM((span, n_z * toks), BF),
            ],
        ),
        out_shape=jax.ShapeDtypeStruct((n_x * NC * rows, n_y * piece), BF),
        compiler_params=PARAMS,
        name="wgrad_products",
    )(place, grad_own, grad_oth, act_own)


def slots_kernel(meta, prod_ref, out_ref, line_buf, *, chunk, blk):
    piece = prod_ref.shape[2] // NY
    for x in range(NX):
        for y in range(NY):
            for c in range(NC):
                at = (y * NC + c) * piece
                line_buf[x, :, at : at + piece] = prod_ref[x * NC + c, :, y * piece : (y + 1) * piece]
    per_x = line_buf.shape[2] // blk
    for s in range(out_ref.shape[0]):
        hid, mod, full = meta[0, s], meta[1, s], meta[2, s]
        rows = aligned(hid * chunk, chunk, chunk)
        cols = aligned(lax.rem(mod, per_x) * blk, blk, blk)
        part = line_buf[lax.div(mod, per_x), rows, cols]
        out_ref[s] = jnp.where(full > 0, part, jnp.zeros_like(part))


def pick_slots(meta, prods, chunk, blk):
    owners = meta.shape[1]
    _, rows, cols = prods.shape
    return pl.pallas_call(
        functools.partial(slots_kernel, chunk=chunk, blk=blk),
        in_specs=[
            pl.BlockSpec(memory_space=pltpu.SMEM),
            pl.BlockSpec(memory_space=pltpu.VMEM),
        ],
        out_specs=pl.BlockSpec(memory_space=pltpu.VMEM),
        out_shape=jax.ShapeDtypeStruct((owners, chunk, blk), BF),
        scratch_shapes=[pltpu.VMEM((NX, rows, NC * cols), BF)],
        compiler_params=PARAMS,
        name="pick_slots",
    )(meta, prods)


def sum_kernel(parts_ref, out_ref):
    out_ref[...] = jnp.sum(parts_ref[...].astype(F32), axis=0).astype(BF)


def sum_groups(parts):
    return pl.pallas_call(
        sum_kernel,
        in_specs=[pl.BlockSpec(memory_space=pltpu.VMEM)],
        out_specs=pl.BlockSpec(memory_space=pltpu.VMEM),
        out_shape=jax.ShapeDtypeStruct(parts.shape[1:], BF),
        compiler_params=PARAMS,
        name="sum_groups",
    )(parts)


def layout_tables(block_mask, block_owner, group, n_groups, owners):
    per_group = block_mask.shape[0] // n_groups
    model_blocks = block_mask.shape[1]
    size = per_group * model_blocks
    mask = lax.dynamic_slice_in_dim(block_mask, group * per_group, per_group, 0).reshape(size)
    owner = lax.dynamic_slice_in_dim(block_owner, group * per_group, per_group, 0).reshape(size)
    ids = jnp.arange(size, dtype=jnp.int32)
    before = jnp.sum(jnp.where(ids[:, None] < ids[None, :], mask[:, None], 0), axis=0)
    count = size // 4
    ranked = jnp.where(
        (before[None, :] == jnp.arange(count, dtype=jnp.int32)[:, None]) & (mask[None, :] == 1), 1, 0
    )
    id_of = jnp.sum(ranked * ids[None, :], axis=1)
    owner_of = jnp.sum(ranked * owner[None, :], axis=1)
    listed = jnp.stack([owner_of, id_of // model_blocks, id_of % model_blocks])
    held = jnp.where(
        (owner[None, :] == jnp.arange(owners, dtype=jnp.int32)[:, None]) & (mask[None, :] == 1), 1, 0
    )
    full = jnp.sum(held, axis=1)
    id_at = jnp.sum(held * ids[None, :], axis=1)
    slots = jnp.stack([id_at // model_blocks, id_at % model_blocks, full])
    return listed, slots


def share_x(x):
    own = jnp.stack([x] + [lax.ppermute(x, "col", X_SHIFTS[s]) for s in range(1, NX)])
    return own, lax.ppermute(own, "col", CORE_SWAP)


def per_device(activations, out_grad, weight_slots, block_mask, block_owner):
    blk = weight_slots.shape[2]
    owners, groups = lax.axis_size("row"), lax.axis_size("col")
    group = lax.axis_index("col")
    toks, piece = activations.shape
    hidden = out_grad.shape[1]
    hid_blocks = hidden // blk
    chunk = blk // owners
    listed, slots = layout_tables(block_mask, block_owner, group, groups, owners)
    place = jnp.stack([group // (NY * NC), group % NC]).astype(jnp.int32)

    w_all = lax.all_gather(weight_slots[0, 0], "row", axis=0)

    grad_send = out_grad.T.reshape(hid_blocks, owners, chunk, toks).transpose(1, 0, 2, 3)
    grad_z = lax.all_to_all(
        grad_send.reshape(owners, hid_blocks * chunk, toks), "row", 0, 0, tiled=True
    )
    act_z = lax.all_gather(activations.T, "row", axis=0)
    act_z, grad_z = lax.optimization_barrier((act_z, grad_z))
    act_y = lax.all_to_all(
        jnp.broadcast_to(act_z[None], (NY, *act_z.shape)),
        "col",
        0,
        0,
        tiled=True,
        axis_index_groups=Y_GROUPS,
    ).reshape(NY, owners, piece, toks)
    grad_own, grad_oth = share_x(grad_z)
    scale = 1.0 / math.sqrt(toks * owners)
    prods = wgrad_products(place, grad_own, grad_oth, act_y, scale)
    prods = lax.all_to_all(
        prods.reshape(NX * NC, hid_blocks * chunk, NY * piece),
        "col",
        0,
        0,
        tiled=True,
        axis_index_groups=XC_GROUPS,
    )
    slot_parts = pick_slots(slots, prods, chunk, blk)
    weight_grad = lax.all_to_all(slot_parts, "row", 0, 0, tiled=True).reshape(1, 1, blk, blk)

    act_here = lax.dynamic_index_in_dim(act_y, lax.axis_index("row"), 1, keepdims=False)
    act_own, act_oth = share_x(act_here)
    outputs, in_part = tokens_step(listed, place, act_own, act_oth, out_grad, w_all)
    in_recv = lax.all_to_all(in_part.reshape(groups, piece, toks), "col", 0, 0, tiled=True)
    return outputs, sum_groups(in_recv).T, weight_grad


def solution(mesh):
    placed = (P("row", "col"), P("row", "col"), P("col", "row", None, None), P(), P())
    return jax.shard_map(
        per_device,
        mesh=mesh,
        in_specs=placed,
        out_specs=(P("row", "col"), P("row", "col"), P("col", "row", None, None)),
        check_vma=False,
    )
```

```python
import functools
import math

import jax
import jax.numpy as jnp
from jax import lax
from jax.experimental import pallas as pl
from jax.experimental.pallas import tpu as pltpu
from jax.sharding import PartitionSpec as P

BF = jnp.bfloat16
F32 = jnp.float32
NX, NY, NC = 4, 4, 2
PARAMS = pltpu.CompilerParams(vmem_limit_bytes=48 * 1024 * 1024)


def col_of(x, y, c):
    return (x * NY + y) * NC + c


PLANE = [(x, y, c) for x in range(NX) for y in range(NY) for c in range(NC)]
XC_GROUPS = [[col_of(x, y, c) for x in range(NX) for c in range(NC)] for y in range(NY)]
Y_GROUPS = [[col_of(x, y, c) for y in range(NY)] for x in range(NX) for c in range(NC)]
CORE_SWAP = [(col_of(x, y, c), col_of(x, y, 1 - c)) for x, y, c in PLANE]
X_SHIFTS = {s: [(col_of(x, y, c), col_of((x + s) % NX, y, c)) for x, y, c in PLANE] for s in range(1, NX)}


def aligned(start, size, step):
    return pl.ds(pl.multiple_of(start, step), size)


def tokens_kernel(meta, place, own_ref, oth_ref, grad_ref, w_ref, out_ref, in_ref, act, out_acc, in_acc, *, blk):
    step = pl.program_id(0)

    @pl.when(step == 0)
    def _():
        out_acc[...] = jnp.zeros_like(out_acc)
        in_acc[...] = jnp.zeros_like(in_acc)
        piece = own_ref.shape[2]
        x, core = place[0], place[1]
        for s in range(NX):
            line = lax.rem(x - s + NX, NX) * NY
            for y in range(NY):
                act[aligned(((line + y) * NC + core) * piece, piece, 64), :] = own_ref[s, y]
                act[aligned(((line + y) * NC + 1 - core) * piece, piece, 64), :] = oth_ref[s, y]

    hid = aligned(meta[1, step] * blk, blk, blk)
    mod = aligned(meta[2, step] * blk, blk, blk)
    w = w_ref[0]
    out_acc[hid, :] += jnp.dot(w, act[mod, :], preferred_element_type=F32)
    in_acc[:, mod] += jnp.dot(grad_ref[:, hid], w, preferred_element_type=F32)

    @pl.when(step == pl.num_programs(0) - 1)
    def _():
        out_ref[...] = out_acc[...].T.astype(BF)
        in_ref[...] = in_acc[...].T.astype(BF)


def tokens_step(meta, place, act_own, act_oth, grad, w_all):
    blk = w_all.shape[1]
    piece, toks = act_own.shape[2:]
    feats = NX * NY * NC * piece
    hidden = grad.shape[1]
    lines = pl.BlockSpec((NX, NY, piece, toks), lambda k, m, p: (0, 0, 0, 0))
    whole = lambda k, m, p: (0, 0)
    return pl.pallas_call(
        functools.partial(tokens_kernel, blk=blk),
        grid_spec=pltpu.PrefetchScalarGridSpec(
            num_scalar_prefetch=2,
            grid=(meta.shape[1],),
            in_specs=[
                lines,
                lines,
                pl.BlockSpec((toks, hidden), whole),
                pl.BlockSpec((1, blk, blk), lambda k, m, p: (m[0, k], 0, 0)),
            ],
            out_specs=[
                pl.BlockSpec((toks, hidden), whole),
                pl.BlockSpec((feats, toks), whole),
            ],
            scratch_shapes=[
                pltpu.VMEM((feats, toks), BF),
                pltpu.VMEM((hidden, toks), F32),
                pltpu.VMEM((toks, feats), F32),
            ],
        ),
        out_shape=[
            jax.ShapeDtypeStruct((toks, hidden), BF),
            jax.ShapeDtypeStruct((feats, toks), BF),
        ],
        compiler_params=PARAMS,
        name="tokens_step",
    )(meta, place, act_own, act_oth, grad, w_all)


def wgrad_kernel(place, own_ref, oth_ref, act_ref, out_ref, a_buf, b_buf, *, scale):
    n_x, n_z, rows, toks = own_ref.shape
    n_y, _, piece, _ = act_ref.shape
    x, core = place[0], place[1]

    @pl.when(pl.program_id(0) == 0)
    def _():
        for s in range(n_x):
            line = lax.rem(x - s + n_x, n_x) * NC
            for z in range(n_z):
                a_buf[aligned((line + core) * rows, rows, rows), z * toks : (z + 1) * toks] = own_ref[s, z]
                a_buf[aligned((line + 1 - core) * rows, rows, rows), z * toks : (z + 1) * toks] = oth_ref[s, z]

    for y in range(n_y):
        for z in range(n_z):
            b_buf[y * piece : (y + 1) * piece, z * toks : (z + 1) * toks] = act_ref[y, z]
    prod = lax.dot_general(
        a_buf[...], b_buf[...], (((1,), (1,)), ((), ())), preferred_element_type=F32
    )
    out_ref[...] = (prod * scale).astype(BF)


def wgrad_products(place, grad_own, grad_oth, act_own, scale):
    n_x, n_z, rows, toks = grad_own.shape
    n_y, _, piece, _ = act_own.shape
    step_y = 2
    span = step_y * piece
    lines = pl.BlockSpec((n_x, n_z, rows, toks), lambda y, p: (0, 0, 0, 0))
    return pl.pallas_call(
        functools.partial(wgrad_kernel, scale=scale),
        grid_spec=pltpu.PrefetchScalarGridSpec(
            num_scalar_prefetch=1,
            grid=(n_y // step_y,),
            in_specs=[
                lines,
                lines,
                pl.BlockSpec((step_y, n_z, piece, toks), lambda y, p: (y, 0, 0, 0)),
            ],
            out_specs=pl.BlockSpec((n_x * NC * rows, span), lambda y, p: (0, y)),
            scratch_shapes=[
                pltpu.VMEM((n_x * NC * rows, n_z * toks), BF),
                pltpu.VMEM((span, n_z * toks), BF),
            ],
        ),
        out_shape=jax.ShapeDtypeStruct((n_x * NC * rows, n_y * piece), BF),
        compiler_params=PARAMS,
        name="wgrad_products",
    )(place, grad_own, grad_oth, act_own)


def slots_kernel(meta, at_z, prod_ref, *refs, chunk, blk):
    out_refs, line_buf = refs[:-1], refs[-1]
    owners = len(out_refs)
    piece = prod_ref.shape[2] // NY
    for x in range(NX):
        for y in range(NY):
            for c in range(NC):
                at = (y * NC + c) * piece
                line_buf[x, :, at : at + piece] = prod_ref[x * NC + c, :, y * piece : (y + 1) * piece]
    per_x = line_buf.shape[2] // blk
    for s in range(owners):
        owner = lax.rem(at_z[0] + s, owners)
        hid, mod, full = meta[0, owner], meta[1, owner], meta[2, owner]
        rows = aligned(hid * chunk, chunk, chunk)
        cols = aligned(lax.rem(mod, per_x) * blk, blk, blk)
        part = line_buf[lax.div(mod, per_x), rows, cols]
        out_refs[s][...] = jnp.where(full > 0, part, jnp.zeros_like(part))


def pick_slots(meta, at_z, prods, chunk, blk):
    owners = meta.shape[1]
    _, rows, cols = prods.shape
    return pl.pallas_call(
        functools.partial(slots_kernel, chunk=chunk, blk=blk),
        in_specs=[
            pl.BlockSpec(memory_space=pltpu.SMEM),
            pl.BlockSpec(memory_space=pltpu.SMEM),
            pl.BlockSpec(memory_space=pltpu.VMEM),
        ],
        out_specs=[pl.BlockSpec(memory_space=pltpu.VMEM)] * owners,
        out_shape=[jax.ShapeDtypeStruct((chunk, blk), BF)] * owners,
        scratch_shapes=[pltpu.VMEM((NX, rows, NC * cols), BF)],
        compiler_params=PARAMS,
        name="pick_slots",
    )(meta, at_z, prods)


def join_kernel(at_z, *refs):
    part_refs, out_ref = refs[:-1], refs[-1]
    owners = len(part_refs)
    chunk = part_refs[0].shape[0]
    for s in range(owners):
        source = lax.rem(at_z[0] - s + owners, owners)
        out_ref[aligned(source * chunk, chunk, chunk), :] = part_refs[s][...]


def join_rows(at_z, parts):
    chunk, blk = parts[0].shape
    return pl.pallas_call(
        join_kernel,
        in_specs=[pl.BlockSpec(memory_space=pltpu.SMEM)] + [pl.BlockSpec(memory_space=pltpu.VMEM)] * len(parts),
        out_specs=pl.BlockSpec(memory_space=pltpu.VMEM),
        out_shape=jax.ShapeDtypeStruct((chunk * len(parts), blk), BF),
        compiler_params=PARAMS,
        name="join_rows",
    )(at_z, *parts)


def sum_kernel(parts_ref, out_ref):
    out_ref[...] = jnp.sum(parts_ref[...].astype(F32), axis=0).astype(BF)


def sum_groups(parts):
    return pl.pallas_call(
        sum_kernel,
        in_specs=[pl.BlockSpec(memory_space=pltpu.VMEM)],
        out_specs=pl.BlockSpec(memory_space=pltpu.VMEM),
        out_shape=jax.ShapeDtypeStruct(parts.shape[1:], BF),
        compiler_params=PARAMS,
        name="sum_groups",
    )(parts)


def layout_tables(block_mask, block_owner, group, n_groups, owners):
    per_group = block_mask.shape[0] // n_groups
    model_blocks = block_mask.shape[1]
    size = per_group * model_blocks
    mask = lax.dynamic_slice_in_dim(block_mask, group * per_group, per_group, 0).reshape(size)
    owner = lax.dynamic_slice_in_dim(block_owner, group * per_group, per_group, 0).reshape(size)
    ids = jnp.arange(size, dtype=jnp.int32)
    before = jnp.sum(jnp.where(ids[:, None] < ids[None, :], mask[:, None], 0), axis=0)
    count = size // 4
    ranked = jnp.where(
        (before[None, :] == jnp.arange(count, dtype=jnp.int32)[:, None]) & (mask[None, :] == 1), 1, 0
    )
    id_of = jnp.sum(ranked * ids[None, :], axis=1)
    owner_of = jnp.sum(ranked * owner[None, :], axis=1)
    listed = jnp.stack([owner_of, id_of // model_blocks, id_of % model_blocks])
    held = jnp.where(
        (owner[None, :] == jnp.arange(owners, dtype=jnp.int32)[:, None]) & (mask[None, :] == 1), 1, 0
    )
    full = jnp.sum(held, axis=1)
    id_at = jnp.sum(held * ids[None, :], axis=1)
    slots = jnp.stack([id_at // model_blocks, id_at % model_blocks, full])
    return listed, slots


def share_x(x):
    own = jnp.stack([x] + [lax.ppermute(x, "col", X_SHIFTS[s]) for s in range(1, NX)])
    return own, lax.ppermute(own, "col", CORE_SWAP)


def per_device(activations, out_grad, weight_slots, block_mask, block_owner):
    blk = weight_slots.shape[2]
    owners, groups = lax.axis_size("row"), lax.axis_size("col")
    group = lax.axis_index("col")
    toks, piece = activations.shape
    hidden = out_grad.shape[1]
    hid_blocks = hidden // blk
    chunk = blk // owners
    listed, slots = layout_tables(block_mask, block_owner, group, groups, owners)
    place = jnp.stack([group // (NY * NC), group % NC]).astype(jnp.int32)

    w_all = lax.all_gather(weight_slots[0, 0], "row", axis=0)

    grad_send = out_grad.T.reshape(hid_blocks, owners, chunk, toks).transpose(1, 0, 2, 3)
    grad_z = lax.all_to_all(
        grad_send.reshape(owners, hid_blocks * chunk, toks), "row", 0, 0, tiled=True
    )
    act_z = lax.all_gather(activations.T, "row", axis=0)
    act_z, grad_z = lax.optimization_barrier((act_z, grad_z))
    act_y = lax.all_to_all(
        jnp.broadcast_to(act_z[None], (NY, *act_z.shape)),
        "col",
        0,
        0,
        tiled=True,
        axis_index_groups=Y_GROUPS,
    ).reshape(NY, owners, piece, toks)
    grad_own, grad_oth = share_x(grad_z)
    scale = 1.0 / math.sqrt(toks * owners)
    prods = wgrad_products(place, grad_own, grad_oth, act_y, scale)
    prods = lax.all_to_all(
        prods.reshape(NX * NC, hid_blocks * chunk, NY * piece),
        "col",
        0,
        0,
        tiled=True,
        axis_index_groups=XC_GROUPS,
    )
    at_z = lax.axis_index("row").reshape(1).astype(jnp.int32)
    slot_parts = pick_slots(slots, at_z, prods, chunk, blk)
    slot_parts = [slot_parts[0]] + [
        lax.ppermute(slot_parts[s], "row", [(z, (z + s) % owners) for z in range(owners)])
        for s in range(1, owners)
    ]
    weight_grad = join_rows(at_z, slot_parts)[None, None]

    act_here = lax.dynamic_index_in_dim(act_y, lax.axis_index("row"), 1, keepdims=False)
    act_own, act_oth = share_x(act_here)
    outputs, in_part = tokens_step(listed, place, act_own, act_oth, out_grad, w_all)
    in_recv = lax.all_to_all(in_part.reshape(groups, piece, toks), "col", 0, 0, tiled=True)
    return outputs, sum_groups(in_recv).T, weight_grad


def solution(mesh):
    placed = (P("row", "col"), P("row", "col"), P("col", "row", None, None), P(), P())
    return jax.shard_map(
        per_device,
        mesh=mesh,
        in_specs=placed,
        out_specs=(P("row", "col"), P("row", "col"), P("col", "row", None, None)),
        check_vma=False,
    )
```

```python
import functools
import math

import jax
import jax.numpy as jnp
from jax import lax
from jax.experimental import pallas as pl
from jax.experimental.pallas import tpu as pltpu
from jax.sharding import PartitionSpec as P

BF = jnp.bfloat16
F32 = jnp.float32
NX, NY, NC = 4, 4, 2
PARAMS = pltpu.CompilerParams(vmem_limit_bytes=48 * 1024 * 1024)


def col_of(x, y, c):
    return (x * NY + y) * NC + c


PLANE = [(x, y, c) for x in range(NX) for y in range(NY) for c in range(NC)]
XC_GROUPS = [[col_of(x, y, c) for x in range(NX) for c in range(NC)] for y in range(NY)]
Y_GROUPS = [[col_of(x, y, c) for y in range(NY)] for x in range(NX) for c in range(NC)]
CORE_SWAP = [(col_of(x, y, c), col_of(x, y, 1 - c)) for x, y, c in PLANE]
X_SHIFTS = {s: [(col_of(x, y, c), col_of((x + s) % NX, y, c)) for x, y, c in PLANE] for s in range(1, NX)}
Y_SHIFTS = {s: [(col_of(x, y, c), col_of(x, (y + s) % NY, c)) for x, y, c in PLANE] for s in range(1, NY)}


def aligned(start, size, step):
    return pl.ds(pl.multiple_of(start, step), size)


def tokens_kernel(meta, place, own_ref, oth_ref, grad_ref, w_ref, out_ref, *refs, blk):
    in_refs, (act, out_acc, in_acc, in_rows) = refs[:NY], refs[NY:]
    step = pl.program_id(0)
    piece = own_ref.shape[2]
    x, y, core = place[0], place[1], place[2]

    @pl.when(step == 0)
    def _():
        out_acc[...] = jnp.zeros_like(out_acc)
        in_acc[...] = jnp.zeros_like(in_acc)
        for s in range(NX):
            line = lax.rem(x - s + NX, NX) * NY
            for j in range(NY):
                act[aligned(((line + j) * NC + core) * piece, piece, 64), :] = own_ref[s, j]
                act[aligned(((line + j) * NC + 1 - core) * piece, piece, 64), :] = oth_ref[s, j]

    hid = aligned(meta[1, step] * blk, blk, blk)
    mod = aligned(meta[2, step] * blk, blk, blk)
    w = w_ref[0]
    out_acc[hid, :] += jnp.dot(w, act[mod, :], preferred_element_type=F32)
    in_acc[:, mod] += jnp.dot(grad_ref[:, hid], w, preferred_element_type=F32)

    @pl.when(step == pl.num_programs(0) - 1)
    def _():
        out_ref[...] = out_acc[...].T.astype(BF)
        in_rows[...] = in_acc[...].T.astype(BF)
        for s in range(NY):
            for t in range(NX):
                chip = (lax.rem(x + t, NX) * NY + lax.rem(y + s, NY)) * NC
                in_refs[s][t, 0] = in_rows[aligned((chip + core) * piece, piece, 64), :]
                in_refs[s][t, 1] = in_rows[aligned((chip + 1 - core) * piece, piece, 64), :]


def tokens_step(meta, place, act_own, act_oth, grad, w_all):
    blk = w_all.shape[1]
    piece, toks = act_own.shape[2:]
    feats = NX * NY * NC * piece
    hidden = grad.shape[1]
    lines = pl.BlockSpec((NX, NY, piece, toks), lambda k, m, p: (0, 0, 0, 0))
    whole = lambda k, m, p: (0, 0)
    return pl.pallas_call(
        functools.partial(tokens_kernel, blk=blk),
        grid_spec=pltpu.PrefetchScalarGridSpec(
            num_scalar_prefetch=2,
            grid=(meta.shape[1],),
            in_specs=[
                lines,
                lines,
                pl.BlockSpec((toks, hidden), whole),
                pl.BlockSpec((1, blk, blk), lambda k, m, p: (m[0, k], 0, 0)),
            ],
            out_specs=[pl.BlockSpec((toks, hidden), whole)]
            + [pl.BlockSpec((NX, NC, piece, toks), lambda k, m, p: (0, 0, 0, 0))] * NY,
            scratch_shapes=[
                pltpu.VMEM((feats, toks), BF),
                pltpu.VMEM((hidden, toks), F32),
                pltpu.VMEM((toks, feats), F32),
                pltpu.VMEM((feats, toks), BF),
            ],
        ),
        out_shape=[jax.ShapeDtypeStruct((toks, hidden), BF)]
        + [jax.ShapeDtypeStruct((NX, NC, piece, toks), BF)] * NY,
        compiler_params=PARAMS,
        name="tokens_step",
    )(meta, place, act_own, act_oth, grad, w_all)


def wgrad_kernel(place, own_ref, oth_ref, act_ref, out_ref, a_buf, b_buf, *, scale):
    n_x, n_z, rows, toks = own_ref.shape
    n_y, _, piece, _ = act_ref.shape
    x, core = place[0], place[2]

    @pl.when(pl.program_id(0) == 0)
    def _():
        for s in range(n_x):
            line = lax.rem(x - s + n_x, n_x) * NC
            for z in range(n_z):
                a_buf[aligned((line + core) * rows, rows, rows), z * toks : (z + 1) * toks] = own_ref[s, z]
                a_buf[aligned((line + 1 - core) * rows, rows, rows), z * toks : (z + 1) * toks] = oth_ref[s, z]

    for y in range(n_y):
        for z in range(n_z):
            b_buf[y * piece : (y + 1) * piece, z * toks : (z + 1) * toks] = act_ref[y, z]
    prod = lax.dot_general(
        a_buf[...], b_buf[...], (((1,), (1,)), ((), ())), preferred_element_type=F32
    )
    out_ref[...] = (prod * scale).astype(BF)


def wgrad_products(place, grad_own, grad_oth, act_own, scale):
    n_x, n_z, rows, toks = grad_own.shape
    n_y, _, piece, _ = act_own.shape
    step_y = 2
    span = step_y * piece
    lines = pl.BlockSpec((n_x, n_z, rows, toks), lambda y, p: (0, 0, 0, 0))
    return pl.pallas_call(
        functools.partial(wgrad_kernel, scale=scale),
        grid_spec=pltpu.PrefetchScalarGridSpec(
            num_scalar_prefetch=1,
            grid=(n_y // step_y,),
            in_specs=[
                lines,
                lines,
                pl.BlockSpec((step_y, n_z, piece, toks), lambda y, p: (y, 0, 0, 0)),
            ],
            out_specs=pl.BlockSpec((n_x * NC * rows, span), lambda y, p: (0, y)),
            scratch_shapes=[
                pltpu.VMEM((n_x * NC * rows, n_z * toks), BF),
                pltpu.VMEM((span, n_z * toks), BF),
            ],
        ),
        out_shape=jax.ShapeDtypeStruct((n_x * NC * rows, n_y * piece), BF),
        compiler_params=PARAMS,
        name="wgrad_products",
    )(place, grad_own, grad_oth, act_own)


def slots_kernel(meta, prod_ref, out_ref, line_buf, *, chunk, blk):
    piece = prod_ref.shape[2] // NY
    for x in range(NX):
        for y in range(NY):
            for c in range(NC):
                at = (y * NC + c) * piece
                line_buf[x, :, at : at + piece] = prod_ref[x * NC + c, :, y * piece : (y + 1) * piece]
    per_x = line_buf.shape[2] // blk
    for s in range(out_ref.shape[0]):
        hid, mod, full = meta[0, s], meta[1, s], meta[2, s]
        rows = aligned(hid * chunk, chunk, chunk)
        cols = aligned(lax.rem(mod, per_x) * blk, blk, blk)
        part = line_buf[lax.div(mod, per_x), rows, cols]
        out_ref[s] = jnp.where(full > 0, part, jnp.zeros_like(part))


def pick_slots(meta, prods, chunk, blk):
    owners = meta.shape[1]
    _, rows, cols = prods.shape
    return pl.pallas_call(
        functools.partial(slots_kernel, chunk=chunk, blk=blk),
        in_specs=[
            pl.BlockSpec(memory_space=pltpu.SMEM),
            pl.BlockSpec(memory_space=pltpu.VMEM),
        ],
        out_specs=pl.BlockSpec(memory_space=pltpu.VMEM),
        out_shape=jax.ShapeDtypeStruct((owners, chunk, blk), BF),
        scratch_shapes=[pltpu.VMEM((NX, rows, NC * cols), BF)],
        compiler_params=PARAMS,
        name="pick_slots",
    )(meta, prods)


def sum_y_kernel(*refs):
    parts, out_refs = refs[:NY], refs[NY:]
    for t in range(NX):
        out_refs[t][...] = sum(part[t].astype(F32) for part in parts)


def sum_x_kernel(*refs):
    parts, (own_ref, oth_ref) = refs[:NX], refs[NX:]
    own_ref[...] = sum(part[0] for part in parts)
    oth_ref[...] = sum(part[1] for part in parts)


def sum_core_kernel(own_ref, oth_ref, out_ref):
    out_ref[...] = (own_ref[...] + oth_ref[...]).astype(BF)


def small_call(kernel, name, outs, *args):
    return pl.pallas_call(
        kernel,
        in_specs=[pl.BlockSpec(memory_space=pltpu.VMEM)] * len(args),
        out_specs=[pl.BlockSpec(memory_space=pltpu.VMEM)] * len(outs),
        out_shape=outs,
        compiler_params=PARAMS,
        name=name,
    )(*args)


def sum_groups(in_parts):
    _, _, piece, toks = in_parts[0].shape
    got = [in_parts[0]] + [lax.ppermute(in_parts[s], "col", Y_SHIFTS[s]) for s in range(1, NY)]
    pair = jax.ShapeDtypeStruct((NC, piece, toks), F32)
    one = jax.ShapeDtypeStruct((piece, toks), F32)
    by_x = small_call(sum_y_kernel, "sum_y", [pair] * NX, *got)
    got = [by_x[0]] + [lax.ppermute(by_x[t], "col", X_SHIFTS[t]) for t in range(1, NX)]
    own, oth = small_call(sum_x_kernel, "sum_x", [one] * NC, *got)
    last = jax.ShapeDtypeStruct((piece, toks), BF)
    return small_call(sum_core_kernel, "sum_core", [last], own, lax.ppermute(oth, "col", CORE_SWAP))[0]


def layout_tables(block_mask, block_owner, group, n_groups, owners):
    per_group = block_mask.shape[0] // n_groups
    model_blocks = block_mask.shape[1]
    size = per_group * model_blocks
    mask = lax.dynamic_slice_in_dim(block_mask, group * per_group, per_group, 0).reshape(size)
    owner = lax.dynamic_slice_in_dim(block_owner, group * per_group, per_group, 0).reshape(size)
    ids = jnp.arange(size, dtype=jnp.int32)
    before = jnp.sum(jnp.where(ids[:, None] < ids[None, :], mask[:, None], 0), axis=0)
    count = size // 4
    ranked = jnp.where(
        (before[None, :] == jnp.arange(count, dtype=jnp.int32)[:, None]) & (mask[None, :] == 1), 1, 0
    )
    id_of = jnp.sum(ranked * ids[None, :], axis=1)
    owner_of = jnp.sum(ranked * owner[None, :], axis=1)
    listed = jnp.stack([owner_of, id_of // model_blocks, id_of % model_blocks])
    held = jnp.where(
        (owner[None, :] == jnp.arange(owners, dtype=jnp.int32)[:, None]) & (mask[None, :] == 1), 1, 0
    )
    full = jnp.sum(held, axis=1)
    id_at = jnp.sum(held * ids[None, :], axis=1)
    slots = jnp.stack([id_at // model_blocks, id_at % model_blocks, full])
    return listed, slots


def share_x(x):
    own = jnp.stack([x] + [lax.ppermute(x, "col", X_SHIFTS[s]) for s in range(1, NX)])
    return own, lax.ppermute(own, "col", CORE_SWAP)


def per_device(activations, out_grad, weight_slots, block_mask, block_owner):
    blk = weight_slots.shape[2]
    owners, groups = lax.axis_size("row"), lax.axis_size("col")
    group = lax.axis_index("col")
    toks, piece = activations.shape
    hidden = out_grad.shape[1]
    hid_blocks = hidden // blk
    chunk = blk // owners
    listed, slots = layout_tables(block_mask, block_owner, group, groups, owners)
    place = jnp.stack([group // (NY * NC), group // NC % NY, group % NC]).astype(jnp.int32)

    w_all = lax.all_gather(weight_slots[0, 0], "row", axis=0)

    grad_send = out_grad.T.reshape(hid_blocks, owners, chunk, toks).transpose(1, 0, 2, 3)
    grad_z = lax.all_to_all(
        grad_send.reshape(owners, hid_blocks * chunk, toks), "row", 0, 0, tiled=True
    )
    act_z = lax.all_gather(activations.T, "row", axis=0)
    act_z, grad_z = lax.optimization_barrier((act_z, grad_z))
    act_y = lax.all_to_all(
        jnp.broadcast_to(act_z[None], (NY, *act_z.shape)),
        "col",
        0,
        0,
        tiled=True,
        axis_index_groups=Y_GROUPS,
    ).reshape(NY, owners, piece, toks)
    grad_own, grad_oth = share_x(grad_z)
    scale = 1.0 / math.sqrt(toks * owners)
    prods = wgrad_products(place, grad_own, grad_oth, act_y, scale)
    prods, w_all = lax.optimization_barrier((prods, w_all))
    prods = lax.all_to_all(
        prods.reshape(NX * NC, hid_blocks * chunk, NY * piece),
        "col",
        0,
        0,
        tiled=True,
        axis_index_groups=XC_GROUPS,
    )
    slot_parts = pick_slots(slots, prods, chunk, blk)

    act_here = lax.dynamic_index_in_dim(act_y, lax.axis_index("row"), 1, keepdims=False)
    act_own, act_oth = share_x(act_here)
    outputs, *in_parts = tokens_step(listed, place, act_own, act_oth, out_grad, w_all)
    slot_parts, in_parts = lax.optimization_barrier((slot_parts, in_parts))
    weight_grad = lax.all_to_all(slot_parts, "row", 0, 0, tiled=True).reshape(1, 1, blk, blk)
    return outputs, sum_groups(in_parts).T, weight_grad


def solution(mesh):
    placed = (P("row", "col"), P("row", "col"), P("col", "row", None, None), P(), P())
    return jax.shard_map(
        per_device,
        mesh=mesh,
        in_specs=placed,
        out_specs=(P("row", "col"), P("row", "col"), P("col", "row", None, None)),
        check_vma=False,
    )
```

```python
import functools
import math

import jax
import jax.numpy as jnp
from jax import lax
from jax.experimental import pallas as pl
from jax.experimental.pallas import tpu as pltpu
from jax.sharding import PartitionSpec as P

BF = jnp.bfloat16
F32 = jnp.float32
NX, NY, NC = 4, 4, 2
PAD = 64
PARAMS = pltpu.CompilerParams(vmem_limit_bytes=48 * 1024 * 1024)


def col_of(x, y, c):
    return (x * NY + y) * NC + c


PLANE = [(x, y, c) for x in range(NX) for y in range(NY) for c in range(NC)]
XC_GROUPS = [[col_of(x, y, c) for x in range(NX) for c in range(NC)] for y in range(NY)]
Y_GROUPS = [[col_of(x, y, c) for y in range(NY)] for x in range(NX) for c in range(NC)]
CORE_SWAP = [(col_of(x, y, c), col_of(x, y, 1 - c)) for x, y, c in PLANE]
X_SHIFTS = {s: [(col_of(x, y, c), col_of((x + s) % NX, y, c)) for x, y, c in PLANE] for s in range(1, NX)}
Y_SHIFTS = {s: [(col_of(x, y, c), col_of(x, (y + s) % NY, c)) for x, y, c in PLANE] for s in range(1, NY)}


def aligned(start, size, step):
    return pl.ds(pl.multiple_of(start, step), size)


def tokens_kernel(meta, place, own_ref, oth_ref, grad_ref, w_ref, out_ref, *refs, blk):
    (in_own, in_oth), (act, out_acc, in_acc, in_rows) = refs[:NC], refs[NC:]
    step = pl.program_id(0)
    piece = own_ref.shape[2]
    x, y, core = place[0], place[1], place[2]

    @pl.when(step == 0)
    def _():
        out_acc[...] = jnp.zeros_like(out_acc)
        in_acc[...] = jnp.zeros_like(in_acc)
        for t in range(NX):
            for s in range(NY):
                chip = (lax.rem(x - t + NX, NX) * NY + lax.rem(y - s + NY, NY)) * NC
                act[aligned((chip + core) * piece, piece, 64), :] = own_ref[t, s]
                act[aligned((chip + 1 - core) * piece, piece, 64), :] = oth_ref[t, s]

    hid = aligned(meta[1, step] * blk, blk, blk)
    mod = aligned(meta[2, step] * blk, blk, blk)
    w = w_ref[:, 0].reshape(blk, blk)
    out_acc[hid, :] += jnp.dot(w, act[mod, :], preferred_element_type=F32)
    in_acc[:, mod] += jnp.dot(grad_ref[:, hid], w, preferred_element_type=F32)

    @pl.when(step == pl.num_programs(0) - 1)
    def _():
        out_ref[...] = out_acc[...].T.astype(BF)
        in_rows[...] = in_acc[...].T.astype(BF)
        for s in range(NY):
            for t in range(NX):
                chip = (lax.rem(x + t, NX) * NY + lax.rem(y + s, NY)) * NC
                in_own[s, t] = in_rows[aligned((chip + core) * piece, piece, 64), :]
                in_oth[s, t] = in_rows[aligned((chip + 1 - core) * piece, piece, 64), :]


def tokens_step(meta, place, act_own, act_oth, grad, w_all):
    parts, _, rows, blk = w_all.shape
    piece, toks = act_own.shape[2:]
    feats = NX * NY * NC * piece
    hidden = grad.shape[1]
    lines = pl.BlockSpec((NX, NY, piece, toks), lambda k, m, p: (0, 0, 0, 0))
    whole = lambda k, m, p: (0, 0)
    return pl.pallas_call(
        functools.partial(tokens_kernel, blk=blk),
        grid_spec=pltpu.PrefetchScalarGridSpec(
            num_scalar_prefetch=2,
            grid=(meta.shape[1],),
            in_specs=[
                lines,
                lines,
                pl.BlockSpec((toks, hidden), whole),
                pl.BlockSpec((parts, 1, rows, blk), lambda k, m, p: (0, k, 0, 0)),
            ],
            out_specs=[pl.BlockSpec((toks, hidden), whole)]
            + [pl.BlockSpec((NY, NX, piece, toks), lambda k, m, p: (0, 0, 0, 0))] * NC,
            scratch_shapes=[
                pltpu.VMEM((feats, toks), BF),
                pltpu.VMEM((hidden, toks), F32),
                pltpu.VMEM((toks, feats), F32),
                pltpu.VMEM((feats, toks), BF),
            ],
        ),
        out_shape=[jax.ShapeDtypeStruct((toks, hidden), BF)]
        + [jax.ShapeDtypeStruct((NY, NX, piece, toks), BF)] * NC,
        compiler_params=PARAMS,
        name="tokens_step",
    )(meta, place, act_own, act_oth, grad, w_all)


def keep_kernel(meta, parts_ref, out_ref):
    for k in range(out_ref.shape[0]):
        out_ref[k] = parts_ref[meta[0, k]]


def keep_filled(meta, parts):
    return pl.pallas_call(
        keep_kernel,
        in_specs=[
            pl.BlockSpec(memory_space=pltpu.SMEM),
            pl.BlockSpec(memory_space=pltpu.VMEM),
        ],
        out_specs=pl.BlockSpec(memory_space=pltpu.VMEM),
        out_shape=jax.ShapeDtypeStruct((meta.shape[1], *parts.shape[1:]), BF),
        compiler_params=PARAMS,
        name="keep_filled",
    )(meta, parts)


def wgrad_kernel(place, own_ref, oth_ref, here, before, far_lo, far_hi, after, out_ref, a_buf, b_buf, *, scale):
    _, n_z, rows, toks = own_ref.shape
    piece = b_buf.shape[0] // NY
    x, y, core = place[0], place[1], place[2]
    step = pl.program_id(0)
    half = n_z // 2

    @pl.when(step == 0)
    def _():
        for s, parts in enumerate(((here,), (before,), (far_lo, far_hi), (after,))):
            at = aligned(lax.rem(y - s + NY, NY) * piece, piece, 64)
            for z in range(n_z):
                src = parts[0][z] if len(parts) == 1 else parts[z // half][z % half]
                b_buf[at, z * toks : (z + 1) * toks] = src[:piece]

    for z in range(n_z):
        a_buf[:rows, z * toks : (z + 1) * toks] = own_ref[0, z]
        a_buf[rows:, z * toks : (z + 1) * toks] = oth_ref[0, z]
    prod = lax.dot_general(
        a_buf[...], b_buf[...], (((1,), (1,)), ((), ())), preferred_element_type=F32
    )
    prod = (prod * scale).astype(BF)
    line = lax.rem(x - step + NX, NX) * NC
    out_ref[line + core] = prod[:rows]
    out_ref[line + 1 - core] = prod[rows:]


def wgrad_products(place, grad_own, grad_oth, act_y, piece, scale):
    n_x, n_z, rows, toks = grad_own.shape
    line = pl.BlockSpec((1, n_z, rows, toks), lambda s, p: (s, 0, 0, 0))
    return pl.pallas_call(
        functools.partial(wgrad_kernel, scale=scale),
        grid_spec=pltpu.PrefetchScalarGridSpec(
            num_scalar_prefetch=1,
            grid=(n_x,),
            in_specs=[line, line] + [pl.BlockSpec(a.shape, lambda s, p: (0, 0, 0)) for a in act_y],
            out_specs=pl.BlockSpec((n_x * NC, rows, NY * piece), lambda s, p: (0, 0, 0)),
            scratch_shapes=[
                pltpu.VMEM((NC * rows, n_z * toks), BF),
                pltpu.VMEM((NY * piece, n_z * toks), BF),
            ],
        ),
        out_shape=jax.ShapeDtypeStruct((n_x * NC, rows, NY * piece), BF),
        compiler_params=PARAMS,
        name="wgrad_products",
    )(place, grad_own, grad_oth, *act_y)


def slots_kernel(meta, prod_ref, out_ref, line_buf, *, chunk, blk):
    piece = prod_ref.shape[2] // NY
    for x in range(NX):
        for y in range(NY):
            for c in range(NC):
                at = (y * NC + c) * piece
                line_buf[x, :, at : at + piece] = prod_ref[x * NC + c, :, y * piece : (y + 1) * piece]
    per_x = line_buf.shape[2] // blk
    for s in range(out_ref.shape[0]):
        hid, mod, full = meta[0, s], meta[1, s], meta[2, s]
        rows = aligned(hid * chunk, chunk, chunk)
        cols = aligned(lax.rem(mod, per_x) * blk, blk, blk)
        part = line_buf[lax.div(mod, per_x), rows, cols]
        out_ref[s] = jnp.where(full > 0, part, jnp.zeros_like(part))


def pick_slots(meta, prods, chunk, blk):
    owners = meta.shape[1]
    _, rows, cols = prods.shape
    return pl.pallas_call(
        functools.partial(slots_kernel, chunk=chunk, blk=blk),
        in_specs=[
            pl.BlockSpec(memory_space=pltpu.SMEM),
            pl.BlockSpec(memory_space=pltpu.VMEM),
        ],
        out_specs=pl.BlockSpec(memory_space=pltpu.VMEM),
        out_shape=jax.ShapeDtypeStruct((owners, chunk, blk), BF),
        scratch_shapes=[pltpu.VMEM((NX, rows, NC * cols), BF)],
        compiler_params=PARAMS,
        name="pick_slots",
    )(meta, prods)


def sum_core_kernel(own_ref, oth_ref, *out_refs):
    for s in range(NY):
        out_refs[s][...] = (own_ref[s].astype(F32) + oth_ref[s].astype(F32)).astype(out_refs[s].dtype)


def sum_y_kernel(*refs):
    parts, out_refs = refs[:NY], refs[NY:]
    for t in range(NX):
        out_refs[t][...] = sum(part[t].astype(F32) for part in parts)


def sum_x_kernel(*refs):
    parts, out_ref = refs[:NX], refs[NX]
    out_ref[...] = sum(part[...] for part in parts).astype(BF)


def small_call(kernel, name, outs, *args):
    return pl.pallas_call(
        kernel,
        in_specs=[pl.BlockSpec(memory_space=pltpu.VMEM)] * len(args),
        out_specs=[pl.BlockSpec(memory_space=pltpu.VMEM)] * len(outs),
        out_shape=outs,
        compiler_params=PARAMS,
        name=name,
    )(*args)


def sum_groups(in_own, in_oth):
    _, _, piece, toks = in_own.shape
    got = lax.ppermute(in_oth, "col", CORE_SWAP)
    line = lambda dtype: jax.ShapeDtypeStruct((NX, piece, toks), dtype)
    by_y = small_call(sum_core_kernel, "sum_core", [line(F32)] + [line(BF)] * (NY - 1), in_own, got)
    got = [by_y[0]] + [lax.ppermute(by_y[s], "col", Y_SHIFTS[s]) for s in range(1, NY)]
    by_x = small_call(sum_y_kernel, "sum_y", [jax.ShapeDtypeStruct((piece, toks), F32)] * NX, *got)
    got = [by_x[0]] + [lax.ppermute(by_x[t], "col", X_SHIFTS[t]) for t in range(1, NX)]
    return small_call(sum_x_kernel, "sum_x", [jax.ShapeDtypeStruct((piece, toks), BF)], *got)[0]


def layout_tables(block_mask, block_owner, group, n_groups, owners):
    per_group = block_mask.shape[0] // n_groups
    model_blocks = block_mask.shape[1]
    size = per_group * model_blocks
    mask = lax.dynamic_slice_in_dim(block_mask, group * per_group, per_group, 0).reshape(size)
    owner = lax.dynamic_slice_in_dim(block_owner, group * per_group, per_group, 0).reshape(size)
    ids = jnp.arange(size, dtype=jnp.int32)
    before = jnp.sum(jnp.where(ids[:, None] < ids[None, :], mask[:, None], 0), axis=0)
    count = size // 4
    ranked = jnp.where(
        (before[None, :] == jnp.arange(count, dtype=jnp.int32)[:, None]) & (mask[None, :] == 1), 1, 0
    )
    id_of = jnp.sum(ranked * ids[None, :], axis=1)
    owner_of = jnp.sum(ranked * owner[None, :], axis=1)
    listed = jnp.stack([owner_of, id_of // model_blocks, id_of % model_blocks])
    held = jnp.where(
        (owner[None, :] == jnp.arange(owners, dtype=jnp.int32)[:, None]) & (mask[None, :] == 1), 1, 0
    )
    full = jnp.sum(held, axis=1)
    id_at = jnp.sum(held * ids[None, :], axis=1)
    slots = jnp.stack([id_at // model_blocks, id_at % model_blocks, full])
    return listed, slots


def line_x(x):
    return jnp.stack([x] + [lax.ppermute(x, "col", X_SHIFTS[t]) for t in range(1, NX)])


def share_y(x):
    half = x.shape[0] // 2
    before = lax.ppermute(x, "col", Y_SHIFTS[1])
    after = lax.ppermute(x, "col", Y_SHIFTS[NY - 1])
    far_lo = lax.ppermute(before[:half], "col", Y_SHIFTS[1])
    far_hi = lax.ppermute(after[half:], "col", Y_SHIFTS[NY - 1])
    return x, before, far_lo, far_hi, after


def per_device(activations, out_grad, weight_slots, block_mask, block_owner):
    blk = weight_slots.shape[2]
    owners, groups = lax.axis_size("row"), lax.axis_size("col")
    group, at_z = lax.axis_index("col"), lax.axis_index("row")
    toks, piece = activations.shape
    hidden = out_grad.shape[1]
    hid_blocks = hidden // blk
    chunk = blk // owners
    listed, slots = layout_tables(block_mask, block_owner, group, groups, owners)
    place = jnp.stack([group // (NY * NC), group // NC % NY, group % NC]).astype(jnp.int32)

    w_parts = lax.all_to_all(weight_slots[0, 0].reshape(owners, chunk, blk), "row", 0, 0, tiled=True)
    act_t = activations.T
    act_z = lax.all_gather(jnp.pad(act_t, ((0, PAD), (0, 0))), "row", axis=0)
    line_y = [act_t] + [lax.ppermute(act_t, "col", Y_SHIFTS[s]) for s in range(1, NY)]
    act_own = line_x(jnp.stack(line_y))
    grad_send = out_grad.T.reshape(hid_blocks, owners, chunk, toks).transpose(1, 0, 2, 3)
    grad_send = grad_send.reshape(owners, hid_blocks * chunk, toks)
    grad_send, w_parts, act_own = lax.optimization_barrier((grad_send, w_parts, act_own))
    w_all = lax.all_gather(keep_filled(listed, w_parts), "row", axis=0)
    grad_z = lax.all_to_all(grad_send, "row", 0, 0, tiled=True)
    act_oth = lax.ppermute(act_own, "col", CORE_SWAP)
    act_y = share_y(act_z[:, :piece])
    grad_z, act_y, act_oth = lax.optimization_barrier((grad_z, act_y, act_oth))

    grad_own = line_x(grad_z)
    grad_oth = lax.ppermute(grad_own, "col", CORE_SWAP)
    scale = 1.0 / math.sqrt(toks * owners)
    prods = wgrad_products(place, grad_own, grad_oth, act_y, piece, scale)
    prods = lax.all_to_all(prods, "col", 0, 0, tiled=True, axis_index_groups=XC_GROUPS)
    slot_parts = pick_slots(slots, prods, chunk, blk)
    weight_grad = lax.all_to_all(slot_parts, "row", 0, 0, tiled=True).reshape(1, 1, blk, blk)

    outputs, in_own, in_oth = tokens_step(listed, place, act_own, act_oth, out_grad, w_all)
    return outputs, sum_groups(in_own, in_oth).T, weight_grad


def solution(mesh):
    placed = (P("row", "col"), P("row", "col"), P("col", "row", None, None), P(), P())
    return jax.shard_map(
        per_device,
        mesh=mesh,
        in_specs=placed,
        out_specs=(P("row", "col"), P("row", "col"), P("col", "row", None, None)),
        check_vma=False,
    )
```

```python
import functools
import math

import jax
import jax.numpy as jnp
from jax import lax
from jax.experimental import pallas as pl
from jax.experimental.pallas import tpu as pltpu
from jax.sharding import PartitionSpec as P

BF = jnp.bfloat16
F32 = jnp.float32
NX, NY, NC = 4, 4, 2
PARAMS = pltpu.CompilerParams(vmem_limit_bytes=48 * 1024 * 1024)


def col_of(x, y, c):
    return (x * NY + y) * NC + c


PLANE = [(x, y, c) for x in range(NX) for y in range(NY) for c in range(NC)]
XC_GROUPS = [[col_of(x, y, c) for x in range(NX) for c in range(NC)] for y in range(NY)]
Y_GROUPS = [[col_of(x, y, c) for y in range(NY)] for x in range(NX) for c in range(NC)]
CORE_SWAP = [(col_of(x, y, c), col_of(x, y, 1 - c)) for x, y, c in PLANE]
X_SHIFTS = {s: [(col_of(x, y, c), col_of((x + s) % NX, y, c)) for x, y, c in PLANE] for s in range(1, NX)}
Y_SHIFTS = {s: [(col_of(x, y, c), col_of(x, (y + s) % NY, c)) for x, y, c in PLANE] for s in range(1, NY)}


def aligned(start, size, step):
    return pl.ds(pl.multiple_of(start, step), size)


def tokens_kernel(meta, place, act_ref, grad_ref, w_ref, out_ref, *refs, blk):
    (in_own, in_oth), (out_acc, in_acc, in_rows) = refs[:NC], refs[NC:]
    step = pl.program_id(0)
    piece = in_own.shape[2]
    x, y, core = place[0], place[1], place[2]

    @pl.when(step == 0)
    def _():
        out_acc[...] = jnp.zeros_like(out_acc)
        in_acc[...] = jnp.zeros_like(in_acc)

    hid = aligned(meta[1, step] * blk, blk, blk)
    mod = aligned(meta[2, step] * blk, blk, blk)
    w = w_ref[:, 0].reshape(blk, blk)
    out_acc[hid, :] += jnp.dot(w, act_ref[mod, :], preferred_element_type=F32)
    in_acc[:, mod] += jnp.dot(grad_ref[:, hid], w, preferred_element_type=F32)

    @pl.when(step == pl.num_programs(0) - 1)
    def _():
        out_ref[...] = out_acc[...].T.astype(BF)
        in_rows[...] = in_acc[...].T.astype(BF)
        for s in range(NY):
            for t in range(NX):
                chip = (lax.rem(x + t, NX) * NY + lax.rem(y + s, NY)) * NC
                in_own[s, t] = in_rows[aligned((chip + core) * piece, piece, 64), :]
                in_oth[s, t] = in_rows[aligned((chip + 1 - core) * piece, piece, 64), :]


def tokens_step(meta, place, act, grad, w_all):
    parts, _, rows, blk = w_all.shape
    feats, toks = act.shape
    piece = feats // (NX * NY * NC)
    hidden = grad.shape[1]
    whole = lambda k, m, p: (0, 0)
    return pl.pallas_call(
        functools.partial(tokens_kernel, blk=blk),
        grid_spec=pltpu.PrefetchScalarGridSpec(
            num_scalar_prefetch=2,
            grid=(meta.shape[1],),
            in_specs=[
                pl.BlockSpec((feats, toks), whole),
                pl.BlockSpec((toks, hidden), whole),
                pl.BlockSpec((parts, 1, rows, blk), lambda k, m, p: (0, k, 0, 0)),
            ],
            out_specs=[pl.BlockSpec((toks, hidden), whole)]
            + [pl.BlockSpec((NY, NX, piece, toks), lambda k, m, p: (0, 0, 0, 0))] * NC,
            scratch_shapes=[
                pltpu.VMEM((hidden, toks), F32),
                pltpu.VMEM((toks, feats), F32),
                pltpu.VMEM((feats, toks), BF),
            ],
        ),
        out_shape=[jax.ShapeDtypeStruct((toks, hidden), BF)]
        + [jax.ShapeDtypeStruct((NY, NX, piece, toks), BF)] * NC,
        compiler_params=PARAMS,
        name="tokens_step",
    )(meta, place, act, grad, w_all)


def pack_kernel(grad_ref, w_ref, out_ref):
    owners, rows, toks = out_ref.shape
    blk = w_ref.shape[0]
    chunk = blk // owners
    hid_blocks = grad_ref.shape[1] // blk
    for f in range(hid_blocks):
        grad_t = grad_ref[:, f * blk : (f + 1) * blk].T
        for z in range(owners):
            out_ref[z, f * chunk : (f + 1) * chunk] = grad_t[z * chunk : (z + 1) * chunk]
    for q in range(blk // toks):
        at = (hid_blocks + q) * chunk
        for z in range(owners):
            out_ref[z, at : at + chunk] = w_ref[z * chunk : (z + 1) * chunk, q * toks : (q + 1) * toks]


def pack_rows(grad, w, owners):
    toks, hidden = grad.shape
    blk = w.shape[0]
    rows = (hidden + blk * blk // toks) // owners
    return small_call(pack_kernel, "pack_rows", [jax.ShapeDtypeStruct((owners, rows, toks), BF)], grad, w)[0]


def unpack_kernel(meta, parts_ref, grad_ref, w_ref):
    _, rows, toks = grad_ref.shape
    grad_ref[...] = parts_ref[:, :rows]
    kept, chunk, blk = w_ref.shape
    for k in range(kept):
        for q in range(blk // toks):
            at = rows + q * chunk
            w_ref[k, :, q * toks : (q + 1) * toks] = parts_ref[meta[0, k], at : at + chunk]


def unpack_rows(meta, parts, rows, chunk, blk):
    owners, _, toks = parts.shape
    return pl.pallas_call(
        unpack_kernel,
        in_specs=[
            pl.BlockSpec(memory_space=pltpu.SMEM),
            pl.BlockSpec(memory_space=pltpu.VMEM),
        ],
        out_specs=[pl.BlockSpec(memory_space=pltpu.VMEM)] * 2,
        out_shape=[
            jax.ShapeDtypeStruct((owners, rows, toks), BF),
            jax.ShapeDtypeStruct((meta.shape[1], chunk, blk), BF),
        ],
        compiler_params=PARAMS,
        name="unpack_rows",
    )(meta, parts)


def wgrad_kernel(place, own_ref, oth_ref, act_ref, out_ref, a_buf, b_buf, *, scale):
    _, n_z, rows, toks = own_ref.shape
    n_y, _, piece, _ = act_ref.shape
    x, core = place[0], place[2]
    step = pl.program_id(0)

    @pl.when(step == 0)
    def _():
        for y in range(n_y):
            for z in range(n_z):
                b_buf[y * piece : (y + 1) * piece, z * toks : (z + 1) * toks] = act_ref[y, z]

    for z in range(n_z):
        a_buf[:rows, z * toks : (z + 1) * toks] = own_ref[0, z]
        a_buf[rows:, z * toks : (z + 1) * toks] = oth_ref[0, z]
    prod = lax.dot_general(
        a_buf[...], b_buf[...], (((1,), (1,)), ((), ())), preferred_element_type=F32
    )
    prod = (prod * scale).astype(BF)
    line = lax.rem(x - step + NX, NX) * NC
    out_ref[line + core] = prod[:rows]
    out_ref[line + 1 - core] = prod[rows:]


def wgrad_products(place, grad_own, grad_oth, act_y, scale):
    n_x, n_z, rows, toks = grad_own.shape
    piece = act_y.shape[2]
    line = pl.BlockSpec((1, n_z, rows, toks), lambda s, p: (s, 0, 0, 0))
    return pl.pallas_call(
        functools.partial(wgrad_kernel, scale=scale),
        grid_spec=pltpu.PrefetchScalarGridSpec(
            num_scalar_prefetch=1,
            grid=(n_x,),
            in_specs=[line, line, pl.BlockSpec(act_y.shape, lambda s, p: (0, 0, 0, 0))],
            out_specs=pl.BlockSpec((n_x * NC, rows, NY * piece), lambda s, p: (0, 0, 0)),
            scratch_shapes=[
                pltpu.VMEM((NC * rows, n_z * toks), BF),
                pltpu.VMEM((NY * piece, n_z * toks), BF),
            ],
        ),
        out_shape=jax.ShapeDtypeStruct((n_x * NC, rows, NY * piece), BF),
        compiler_params=PARAMS,
        name="wgrad_products",
    )(place, grad_own, grad_oth, act_y)


def slots_kernel(meta, prod_ref, out_ref, line_buf, *, chunk, blk):
    piece = prod_ref.shape[2] // NY
    for x in range(NX):
        for y in range(NY):
            for c in range(NC):
                at = (y * NC + c) * piece
                line_buf[x, :, at : at + piece] = prod_ref[x * NC + c, :, y * piece : (y + 1) * piece]
    per_x = line_buf.shape[2] // blk
    for s in range(out_ref.shape[0]):
        hid, mod, full = meta[0, s], meta[1, s], meta[2, s]
        rows = aligned(hid * chunk, chunk, chunk)
        cols = aligned(lax.rem(mod, per_x) * blk, blk, blk)
        part = line_buf[lax.div(mod, per_x), rows, cols]
        out_ref[s] = jnp.where(full > 0, part, jnp.zeros_like(part))


def pick_slots(meta, prods, chunk, blk):
    owners = meta.shape[1]
    _, rows, cols = prods.shape
    return pl.pallas_call(
        functools.partial(slots_kernel, chunk=chunk, blk=blk),
        in_specs=[
            pl.BlockSpec(memory_space=pltpu.SMEM),
            pl.BlockSpec(memory_space=pltpu.VMEM),
        ],
        out_specs=pl.BlockSpec(memory_space=pltpu.VMEM),
        out_shape=jax.ShapeDtypeStruct((owners, chunk, blk), BF),
        scratch_shapes=[pltpu.VMEM((NX, rows, NC * cols), BF)],
        compiler_params=PARAMS,
        name="pick_slots",
    )(meta, prods)


def sum_core_kernel(own_ref, oth_ref, *out_refs):
    for s in range(NY):
        out_refs[s][...] = (own_ref[s].astype(F32) + oth_ref[s].astype(F32)).astype(out_refs[s].dtype)


def sum_y_kernel(*refs):
    parts, out_refs = refs[:NY], refs[NY:]
    for t in range(NX):
        out_refs[t][...] = sum(part[t].astype(F32) for part in parts)


def sum_x_kernel(*refs):
    parts, out_ref = refs[:NX], refs[NX]
    out_ref[...] = sum(part[...] for part in parts).astype(BF)


def small_call(kernel, name, outs, *args):
    return pl.pallas_call(
        kernel,
        in_specs=[pl.BlockSpec(memory_space=pltpu.VMEM)] * len(args),
        out_specs=[pl.BlockSpec(memory_space=pltpu.VMEM)] * len(outs),
        out_shape=outs,
        compiler_params=PARAMS,
        name=name,
    )(*args)


def sum_groups(in_own, in_oth):
    _, _, piece, toks = in_own.shape
    got = lax.ppermute(in_oth, "col", CORE_SWAP)
    line = lambda dtype: jax.ShapeDtypeStruct((NX, piece, toks), dtype)
    by_y = small_call(sum_core_kernel, "sum_core", [line(F32)] + [line(BF)] * (NY - 1), in_own, got)
    got = [by_y[0]] + [lax.ppermute(by_y[s], "col", Y_SHIFTS[s]) for s in range(1, NY)]
    by_x = small_call(sum_y_kernel, "sum_y", [jax.ShapeDtypeStruct((piece, toks), F32)] * NX, *got)
    got = [by_x[0]] + [lax.ppermute(by_x[t], "col", X_SHIFTS[t]) for t in range(1, NX)]
    return small_call(sum_x_kernel, "sum_x", [jax.ShapeDtypeStruct((piece, toks), BF)], *got)[0]


def layout_tables(block_mask, block_owner, group, n_groups, owners):
    per_group = block_mask.shape[0] // n_groups
    model_blocks = block_mask.shape[1]
    size = per_group * model_blocks
    mask = lax.dynamic_slice_in_dim(block_mask, group * per_group, per_group, 0).reshape(size)
    owner = lax.dynamic_slice_in_dim(block_owner, group * per_group, per_group, 0).reshape(size)
    ids = jnp.arange(size, dtype=jnp.int32)
    before = jnp.sum(jnp.where(ids[:, None] < ids[None, :], mask[:, None], 0), axis=0)
    count = size // 4
    ranked = jnp.where(
        (before[None, :] == jnp.arange(count, dtype=jnp.int32)[:, None]) & (mask[None, :] == 1), 1, 0
    )
    id_of = jnp.sum(ranked * ids[None, :], axis=1)
    owner_of = jnp.sum(ranked * owner[None, :], axis=1)
    listed = jnp.stack([owner_of, id_of // model_blocks, id_of % model_blocks])
    held = jnp.where(
        (owner[None, :] == jnp.arange(owners, dtype=jnp.int32)[:, None]) & (mask[None, :] == 1), 1, 0
    )
    full = jnp.sum(held, axis=1)
    id_at = jnp.sum(held * ids[None, :], axis=1)
    slots = jnp.stack([id_at // model_blocks, id_at % model_blocks, full])
    return listed, slots


def line_x(x):
    return jnp.stack([x] + [lax.ppermute(x, "col", X_SHIFTS[t]) for t in range(1, NX)])


def share_y(x):
    wide = jnp.broadcast_to(x[None], (NY, *x.shape))
    return lax.all_to_all(wide, "col", 0, 0, tiled=True, axis_index_groups=Y_GROUPS)


def per_device(activations, out_grad, weight_slots, block_mask, block_owner):
    blk = weight_slots.shape[2]
    owners, groups = lax.axis_size("row"), lax.axis_size("col")
    group = lax.axis_index("col")
    toks, piece = activations.shape
    hidden = out_grad.shape[1]
    chunk = blk // owners
    rows = hidden // owners
    listed, slots = layout_tables(block_mask, block_owner, group, groups, owners)
    place = jnp.stack([group // (NY * NC), group // NC % NY, group % NC]).astype(jnp.int32)

    act_t = activations.T
    act_all = lax.all_gather(act_t, "col", axis=0).reshape(groups * piece, toks)
    parts = pack_rows(out_grad, weight_slots[0, 0], owners)
    parts = lax.all_to_all(parts, "row", 0, 0, tiled=True)
    act_z = lax.all_gather(act_t, "row", axis=0)
    parts, act_z = lax.optimization_barrier((parts, act_z))
    grad_z, w_parts = unpack_rows(listed, parts, rows, chunk, blk)
    w_all = lax.all_gather(w_parts, "row", axis=0)

    act_y = share_y(act_z).reshape(NY, owners, piece, toks)
    grad_own = line_x(grad_z)
    grad_oth = lax.ppermute(grad_own, "col", CORE_SWAP)
    scale = 1.0 / math.sqrt(toks * owners)
    prods = wgrad_products(place, grad_own, grad_oth, act_y, scale)
    prods = lax.all_to_all(prods, "col", 0, 0, tiled=True, axis_index_groups=XC_GROUPS)
    slot_parts = pick_slots(slots, prods, chunk, blk)
    weight_grad = lax.all_to_all(slot_parts, "row", 0, 0, tiled=True).reshape(1, 1, blk, blk)

    outputs, in_own, in_oth = tokens_step(listed, place, act_all, out_grad, w_all)
    return outputs, sum_groups(in_own, in_oth).T, weight_grad


def solution(mesh):
    placed = (P("row", "col"), P("row", "col"), P("col", "row", None, None), P(), P())
    return jax.shard_map(
        per_device,
        mesh=mesh,
        in_specs=placed,
        out_specs=(P("row", "col"), P("row", "col"), P("col", "row", None, None)),
        check_vma=False,
    )
```

```python
import functools
import math

import jax
import jax.numpy as jnp
from jax import lax
from jax.experimental import pallas as pl
from jax.experimental.pallas import tpu as pltpu
from jax.sharding import PartitionSpec as P

BF = jnp.bfloat16
F32 = jnp.float32
NX, NY, NC = 4, 4, 2
PARAMS = pltpu.CompilerParams(vmem_limit_bytes=48 * 1024 * 1024)


def col_of(x, y, c):
    return (x * NY + y) * NC + c


PLANE = [(x, y, c) for x in range(NX) for y in range(NY) for c in range(NC)]
XC_GROUPS = [[col_of(x, y, c) for x in range(NX) for c in range(NC)] for y in range(NY)]
CORE_SWAP = [(col_of(x, y, c), col_of(x, y, 1 - c)) for x, y, c in PLANE]
X_SHIFTS = {s: [(col_of(x, y, c), col_of((x + s) % NX, y, c)) for x, y, c in PLANE] for s in range(1, NX)}
Y_SHIFTS = {s: [(col_of(x, y, c), col_of(x, (y + s) % NY, c)) for x, y, c in PLANE] for s in range(1, NY)}


def aligned(start, size, step):
    return pl.ds(pl.multiple_of(start, step), size)


def tokens_kernel(meta, place, act_ref, grad_ref, w_ref, out_ref, *refs, blk):
    (in_own, in_oth), (out_acc, in_acc, in_rows) = refs[:NC], refs[NC:]
    step = pl.program_id(0)
    piece = in_own.shape[2]
    x, y, core = place[0], place[1], place[2]

    @pl.when(step == 0)
    def _():
        out_acc[...] = jnp.zeros_like(out_acc)
        in_acc[...] = jnp.zeros_like(in_acc)

    hid = aligned(meta[1, step] * blk, blk, blk)
    mod = aligned(meta[2, step] * blk, blk, blk)
    w = w_ref[0]
    out_acc[hid, :] += jnp.dot(w, act_ref[mod, :], preferred_element_type=F32)
    in_acc[:, mod] += jnp.dot(grad_ref[:, hid], w, preferred_element_type=F32)

    @pl.when(step == pl.num_programs(0) - 1)
    def _():
        out_ref[...] = out_acc[...].T.astype(BF)
        in_rows[...] = in_acc[...].T.astype(BF)
        for s in range(NY):
            for t in range(NX):
                chip = (lax.rem(x + t, NX) * NY + lax.rem(y + s, NY)) * NC
                in_own[s, t] = in_rows[aligned((chip + core) * piece, piece, 64), :]
                in_oth[s, t] = in_rows[aligned((chip + 1 - core) * piece, piece, 64), :]


def tokens_step(meta, place, act, grad, w_all):
    blk = w_all.shape[1]
    feats, toks = act.shape
    piece = feats // (NX * NY * NC)
    hidden = grad.shape[1]
    whole = lambda k, m, p: (0, 0)
    return pl.pallas_call(
        functools.partial(tokens_kernel, blk=blk),
        grid_spec=pltpu.PrefetchScalarGridSpec(
            num_scalar_prefetch=2,
            grid=(meta.shape[1],),
            in_specs=[
                pl.BlockSpec((feats, toks), whole),
                pl.BlockSpec((toks, hidden), whole),
                pl.BlockSpec((1, blk, blk), lambda k, m, p: (m[0, k], 0, 0)),
            ],
            out_specs=[pl.BlockSpec((toks, hidden), whole)]
            + [pl.BlockSpec((NY, NX, piece, toks), lambda k, m, p: (0, 0, 0, 0))] * NC,
            scratch_shapes=[
                pltpu.VMEM((hidden, toks), F32),
                pltpu.VMEM((toks, feats), F32),
                pltpu.VMEM((feats, toks), BF),
            ],
        ),
        out_shape=[jax.ShapeDtypeStruct((toks, hidden), BF)]
        + [jax.ShapeDtypeStruct((NY, NX, piece, toks), BF)] * NC,
        compiler_params=PARAMS,
        name="tokens_step",
    )(meta, place, act, grad, w_all)


def wgrad_kernel(place, own_ref, oth_ref, here, before, far_lo, far_hi, after, out_ref, a_buf, b_buf, *, scale):
    _, n_z, rows, toks = own_ref.shape
    piece = b_buf.shape[0] // NY
    x, y, core = place[0], place[1], place[2]
    step = pl.program_id(0)
    half = n_z // 2

    @pl.when(step == 0)
    def _():
        for s, parts in enumerate(((here,), (before,), (far_lo, far_hi), (after,))):
            at = aligned(lax.rem(y - s + NY, NY) * piece, piece, 64)
            for z in range(n_z):
                src = parts[0][z] if len(parts) == 1 else parts[z // half][z % half]
                b_buf[at, z * toks : (z + 1) * toks] = src

    for z in range(n_z):
        a_buf[:rows, z * toks : (z + 1) * toks] = own_ref[0, z]
        a_buf[rows:, z * toks : (z + 1) * toks] = oth_ref[0, z]
    prod = lax.dot_general(
        a_buf[...], b_buf[...], (((1,), (1,)), ((), ())), preferred_element_type=F32
    )
    prod = (prod * scale).astype(BF)
    line = lax.rem(x - step + NX, NX) * NC
    out_ref[line + core] = prod[:rows]
    out_ref[line + 1 - core] = prod[rows:]


def wgrad_products(place, grad_own, grad_oth, act_y, piece, scale):
    n_x, n_z, rows, toks = grad_own.shape
    line = pl.BlockSpec((1, n_z, rows, toks), lambda s, p: (s, 0, 0, 0))
    return pl.pallas_call(
        functools.partial(wgrad_kernel, scale=scale),
        grid_spec=pltpu.PrefetchScalarGridSpec(
            num_scalar_prefetch=1,
            grid=(n_x,),
            in_specs=[line, line] + [pl.BlockSpec(a.shape, lambda s, p: (0, 0, 0)) for a in act_y],
            out_specs=pl.BlockSpec((n_x * NC, rows, NY * piece), lambda s, p: (0, 0, 0)),
            scratch_shapes=[
                pltpu.VMEM((NC * rows, n_z * toks), BF),
                pltpu.VMEM((NY * piece, n_z * toks), BF),
            ],
        ),
        out_shape=jax.ShapeDtypeStruct((n_x * NC, rows, NY * piece), BF),
        compiler_params=PARAMS,
        name="wgrad_products",
    )(place, grad_own, grad_oth, *act_y)


def slots_kernel(meta, prod_ref, out_ref, line_buf, *, chunk, blk):
    piece = prod_ref.shape[2] // NY
    for x in range(NX):
        for y in range(NY):
            for c in range(NC):
                at = (y * NC + c) * piece
                line_buf[x, :, at : at + piece] = prod_ref[x * NC + c, :, y * piece : (y + 1) * piece]
    per_x = line_buf.shape[2] // blk
    for s in range(out_ref.shape[0]):
        hid, mod, full = meta[0, s], meta[1, s], meta[2, s]
        rows = aligned(hid * chunk, chunk, chunk)
        cols = aligned(lax.rem(mod, per_x) * blk, blk, blk)
        part = line_buf[lax.div(mod, per_x), rows, cols]
        out_ref[s] = jnp.where(full > 0, part, jnp.zeros_like(part))


def pick_slots(meta, prods, chunk, blk):
    owners = meta.shape[1]
    _, rows, cols = prods.shape
    return pl.pallas_call(
        functools.partial(slots_kernel, chunk=chunk, blk=blk),
        in_specs=[
            pl.BlockSpec(memory_space=pltpu.SMEM),
            pl.BlockSpec(memory_space=pltpu.VMEM),
        ],
        out_specs=pl.BlockSpec(memory_space=pltpu.VMEM),
        out_shape=jax.ShapeDtypeStruct((owners, chunk, blk), BF),
        scratch_shapes=[pltpu.VMEM((NX, rows, NC * cols), BF)],
        compiler_params=PARAMS,
        name="pick_slots",
    )(meta, prods)


def sum_core_kernel(own_ref, oth_ref, *out_refs):
    for s in range(NY):
        out_refs[s][...] = (own_ref[s].astype(F32) + oth_ref[s].astype(F32)).astype(out_refs[s].dtype)


def sum_y_kernel(*refs):
    parts, out_refs = refs[:NY], refs[NY:]
    for t in range(NX):
        out_refs[t][...] = sum(part[t].astype(F32) for part in parts)


def sum_x_kernel(*refs):
    parts, out_ref = refs[:NX], refs[NX]
    out_ref[...] = sum(part[...] for part in parts).astype(BF)


def small_call(kernel, name, outs, *args):
    return pl.pallas_call(
        kernel,
        in_specs=[pl.BlockSpec(memory_space=pltpu.VMEM)] * len(args),
        out_specs=[pl.BlockSpec(memory_space=pltpu.VMEM)] * len(outs),
        out_shape=outs,
        compiler_params=PARAMS,
        name=name,
    )(*args)


def sum_pair(in_own, in_oth):
    line = lambda dtype: jax.ShapeDtypeStruct(in_own.shape[1:], dtype)
    got = lax.ppermute(in_oth, "col", CORE_SWAP)
    return small_call(sum_core_kernel, "sum_core", [line(F32)] + [line(BF)] * (NY - 1), in_own, got)


def sum_plane(by_y):
    _, piece, toks = by_y[0].shape
    got = [by_y[0]] + [lax.ppermute(by_y[s], "col", Y_SHIFTS[s]) for s in range(1, NY)]
    by_x = small_call(sum_y_kernel, "sum_y", [jax.ShapeDtypeStruct((piece, toks), F32)] * NX, *got)
    got = [by_x[0]] + [lax.ppermute(by_x[t], "col", X_SHIFTS[t]) for t in range(1, NX)]
    return small_call(sum_x_kernel, "sum_x", [jax.ShapeDtypeStruct((piece, toks), BF)], *got)[0]


def layout_tables(block_mask, block_owner, group, n_groups, owners):
    per_group = block_mask.shape[0] // n_groups
    model_blocks = block_mask.shape[1]
    size = per_group * model_blocks
    mask = lax.dynamic_slice_in_dim(block_mask, group * per_group, per_group, 0).reshape(size)
    owner = lax.dynamic_slice_in_dim(block_owner, group * per_group, per_group, 0).reshape(size)
    ids = jnp.arange(size, dtype=jnp.int32)
    before = jnp.sum(jnp.where(ids[:, None] < ids[None, :], mask[:, None], 0), axis=0)
    count = size // 4
    ranked = jnp.where(
        (before[None, :] == jnp.arange(count, dtype=jnp.int32)[:, None]) & (mask[None, :] == 1), 1, 0
    )
    id_of = jnp.sum(ranked * ids[None, :], axis=1)
    owner_of = jnp.sum(ranked * owner[None, :], axis=1)
    listed = jnp.stack([owner_of, id_of // model_blocks, id_of % model_blocks])
    held = jnp.where(
        (owner[None, :] == jnp.arange(owners, dtype=jnp.int32)[:, None]) & (mask[None, :] == 1), 1, 0
    )
    full = jnp.sum(held, axis=1)
    id_at = jnp.sum(held * ids[None, :], axis=1)
    slots = jnp.stack([id_at // model_blocks, id_at % model_blocks, full])
    return listed, slots


def line_x(x):
    return jnp.stack([x] + [lax.ppermute(x, "col", X_SHIFTS[t]) for t in range(1, NX)])


def share_y(x):
    half = x.shape[0] // 2
    before = lax.ppermute(x, "col", Y_SHIFTS[1])
    after = lax.ppermute(x, "col", Y_SHIFTS[NY - 1])
    far_lo = lax.ppermute(before[:half], "col", Y_SHIFTS[1])
    far_hi = lax.ppermute(after[half:], "col", Y_SHIFTS[NY - 1])
    return x, before, far_lo, far_hi, after


def per_device(activations, out_grad, weight_slots, block_mask, block_owner):
    blk = weight_slots.shape[2]
    owners, groups = lax.axis_size("row"), lax.axis_size("col")
    group = lax.axis_index("col")
    toks, piece = activations.shape
    hidden = out_grad.shape[1]
    chunk = blk // owners
    rows = hidden // owners
    listed, slots = layout_tables(block_mask, block_owner, group, groups, owners)
    place = jnp.stack([group // (NY * NC), group // NC % NY, group % NC]).astype(jnp.int32)

    w_all = lax.all_gather(weight_slots[0, 0], "row", axis=0)
    act_t = activations.T
    wide = jnp.broadcast_to(act_t[None], (groups, piece, toks))
    act_all = lax.all_to_all(wide, "col", 0, 0, tiled=True).reshape(groups * piece, toks)
    act_z = lax.all_gather(act_t, "row", axis=0)

    grad_send = out_grad.T.reshape(-1, owners, chunk, toks).transpose(1, 0, 2, 3)
    grad_send = grad_send.reshape(owners, rows, toks)
    grad_send, act_z, act_all = lax.optimization_barrier((grad_send, act_z, act_all))
    grad_z = lax.all_to_all(grad_send, "row", 0, 0, tiled=True)
    act_y = share_y(act_z)
    grad_z, act_y = lax.optimization_barrier((grad_z, act_y))

    grad_own = line_x(grad_z)
    grad_oth = lax.ppermute(grad_own, "col", CORE_SWAP)
    scale = 1.0 / math.sqrt(toks * owners)
    prods = wgrad_products(place, grad_own, grad_oth, act_y, piece, scale)
    prods = lax.all_to_all(prods, "col", 0, 0, tiled=True, axis_index_groups=XC_GROUPS)
    slot_parts = pick_slots(slots, prods, chunk, blk)

    outputs, in_own, in_oth = tokens_step(listed, place, act_all, out_grad, w_all)
    slot_parts, by_y = lax.optimization_barrier((slot_parts, sum_pair(in_own, in_oth)))
    weight_grad = lax.all_to_all(slot_parts, "row", 0, 0, tiled=True).reshape(1, 1, blk, blk)
    return outputs, sum_plane(by_y).T, weight_grad


def solution(mesh):
    placed = (P("row", "col"), P("row", "col"), P("col", "row", None, None), P(), P())
    return jax.shard_map(
        per_device,
        mesh=mesh,
        in_specs=placed,
        out_specs=(P("row", "col"), P("row", "col"), P("col", "row", None, None)),
        check_vma=False,
    )
```

```python
import functools
import math

import jax
import jax.numpy as jnp
from jax import lax
from jax.experimental import pallas as pl
from jax.experimental.pallas import tpu as pltpu
from jax.sharding import PartitionSpec as P

BF = jnp.bfloat16
F32 = jnp.float32
NX, NY, NC = 4, 4, 2
MIB = 1024 * 1024


def col_of(x, y, c):
    return (x * NY + y) * NC + c


PLANE = [(x, y, c) for x in range(NX) for y in range(NY) for c in range(NC)]
XC_GROUPS = [[col_of(x, y, c) for x in range(NX) for c in range(NC)] for y in range(NY)]
CORE_SWAP = [(col_of(x, y, c), col_of(x, y, 1 - c)) for x, y, c in PLANE]
X_SHIFTS = {s: [(col_of(x, y, c), col_of((x + s) % NX, y, c)) for x, y, c in PLANE] for s in range(1, NX)}
Y_SHIFTS = {s: [(col_of(x, y, c), col_of(x, (y + s) % NY, c)) for x, y, c in PLANE] for s in range(1, NY)}


def aligned(start, size, step):
    return pl.ds(pl.multiple_of(start, step), size)


def tokens_kernel(meta, place, act_ref, grad_ref, w_ref, out_ref, in_own, in_oth, w_buf, out_acc, in_acc, in_rows, sems):
    count, blk, _ = w_buf.shape
    piece = in_own.shape[2]
    x, y, core = place[0], place[1], place[2]
    copies = [pltpu.make_async_copy(w_ref.at[meta[0, k]], w_buf.at[k], sems.at[k]) for k in range(count)]
    for copy in copies:
        copy.start()
    out_acc[...] = jnp.zeros_like(out_acc)
    in_acc[...] = jnp.zeros_like(in_acc)
    for k in range(count):
        hid = aligned(meta[1, k] * blk, blk, blk)
        mod = aligned(meta[2, k] * blk, blk, blk)
        copies[k].wait()
        w = w_buf[k]
        out_acc[hid, :] += jnp.dot(w, act_ref[mod, :], preferred_element_type=F32)
        in_acc[:, mod] += jnp.dot(grad_ref[:, hid], w, preferred_element_type=F32)
    out_ref[...] = out_acc[...].T.astype(BF)
    in_rows[...] = in_acc[...].T.astype(BF)
    for s in range(NY):
        for t in range(NX):
            chip = (lax.rem(x + t, NX) * NY + lax.rem(y + s, NY)) * NC
            in_own[s, t] = in_rows[aligned((chip + core) * piece, piece, 64), :]
            in_oth[s, t] = in_rows[aligned((chip + 1 - core) * piece, piece, 64), :]


def tokens_step(meta, place, act, grad, w_all):
    count, blk = meta.shape[1], w_all.shape[1]
    feats, toks = act.shape
    hidden = grad.shape[1]
    parts = pltpu.HBM((NY, NX, feats // (NX * NY * NC), toks), BF)
    vmem = pl.BlockSpec(memory_space=pltpu.VMEM)
    smem = pl.BlockSpec(memory_space=pltpu.SMEM)
    return pl.pallas_call(
        tokens_kernel,
        in_specs=[smem, smem, vmem, vmem, pl.BlockSpec(memory_space=pltpu.HBM)],
        out_specs=[vmem] * 3,
        out_shape=[jax.ShapeDtypeStruct((toks, hidden), BF), parts, parts],
        scratch_shapes=[
            pltpu.VMEM((count, blk, blk), BF),
            pltpu.VMEM((hidden, toks), F32),
            pltpu.VMEM((toks, feats), F32),
            pltpu.VMEM((feats, toks), BF),
            pltpu.SemaphoreType.DMA((count,)),
        ],
        compiler_params=pltpu.CompilerParams(vmem_limit_bytes=28 * MIB),
        name="tokens_step",
    )(meta, place, act, grad, in_hbm(w_all))


def wgrad_kernel(place, *refs, scale):
    n_in = 7
    in_refs, out_ref, buffers, (a_buf, b_buf, sems) = refs[:n_in], refs[n_in], refs[n_in + 1 : -3], refs[-3:]
    copies = [pltpu.make_async_copy(in_refs[i], buffers[i], sems.at[i]) for i in range(n_in)]
    for copy in copies:
        copy.start()
    here, before, far_lo, far_hi, after, own, oth = buffers
    n_x, n_z, rows, toks = own.shape
    piece = here.shape[1]
    x, y, core = place[0], place[1], place[2]
    for i, (part, s, first) in enumerate(
        ((here, 0, 0), (before, 1, 0), (far_lo, 2, 0), (far_hi, 2, n_z // 2), (after, 3, 0))
    ):
        at = aligned(lax.rem(y - s + NY, NY) * piece, piece, 64)
        copies[i].wait()
        for z in range(part.shape[0]):
            b_buf[at, (first + z) * toks : (first + z + 1) * toks] = part[z]
    for c, part in enumerate((own, oth)):
        copies[n_in - 2 + c].wait()
        for t in range(n_x):
            at = (t * NC + c) * rows
            for z in range(n_z):
                a_buf[at : at + rows, z * toks : (z + 1) * toks] = part[t, z]
    prod = lax.dot_general(
        a_buf[...], b_buf[...], (((1,), (1,)), ((), ())), preferred_element_type=F32
    )
    prod = (prod * scale).astype(BF)
    for t in range(n_x):
        line = lax.rem(x - t + n_x, n_x) * NC
        out_ref[line + core] = prod[2 * t * rows : (2 * t + 1) * rows]
        out_ref[line + 1 - core] = prod[(2 * t + 1) * rows : (2 * t + 2) * rows]


def in_hbm(x):
    return pltpu.with_memory_space_constraint(x, pltpu.HBM)


def wgrad_products(place, grad_own, grad_oth, act_y, scale):
    n_x, n_z, rows, toks = grad_own.shape
    piece = act_y[0].shape[1]
    args = [in_hbm(a) for a in (*act_y, grad_own, grad_oth)]
    return pl.pallas_call(
        functools.partial(wgrad_kernel, scale=scale),
        in_specs=[pl.BlockSpec(memory_space=pltpu.SMEM)]
        + [pl.BlockSpec(memory_space=pltpu.HBM)] * len(args),
        out_specs=pl.BlockSpec(memory_space=pltpu.VMEM),
        out_shape=pltpu.HBM((n_x * NC, rows, NY * piece), BF),
        scratch_shapes=[pltpu.VMEM(a.shape, BF) for a in args]
        + [
            pltpu.VMEM((n_x * NC * rows, n_z * toks), BF),
            pltpu.VMEM((NY * piece, n_z * toks), BF),
            pltpu.SemaphoreType.DMA((len(args),)),
        ],
        compiler_params=pltpu.CompilerParams(vmem_limit_bytes=32 * MIB),
        name="wgrad_products",
    )(place, *args)


def slots_kernel(meta, prod_ref, out_ref, line_buf, *, chunk, blk):
    piece = prod_ref.shape[2] // NY
    for x in range(NX):
        for y in range(NY):
            for c in range(NC):
                at = (y * NC + c) * piece
                line_buf[x, :, at : at + piece] = prod_ref[x * NC + c, :, y * piece : (y + 1) * piece]
    per_x = line_buf.shape[2] // blk
    for s in range(out_ref.shape[0]):
        hid, mod, full = meta[0, s], meta[1, s], meta[2, s]
        rows = aligned(hid * chunk, chunk, chunk)
        cols = aligned(lax.rem(mod, per_x) * blk, blk, blk)
        part = line_buf[lax.div(mod, per_x), rows, cols]
        out_ref[s] = jnp.where(full > 0, part, jnp.zeros_like(part))


def pick_slots(meta, prods, chunk, blk):
    owners = meta.shape[1]
    _, rows, cols = prods.shape
    return pl.pallas_call(
        functools.partial(slots_kernel, chunk=chunk, blk=blk),
        in_specs=[
            pl.BlockSpec(memory_space=pltpu.SMEM),
            pl.BlockSpec(memory_space=pltpu.VMEM),
        ],
        out_specs=pl.BlockSpec(memory_space=pltpu.VMEM),
        out_shape=jax.ShapeDtypeStruct((owners, chunk, blk), BF),
        scratch_shapes=[pltpu.VMEM((NX, rows, NC * cols), BF)],
        compiler_params=pltpu.CompilerParams(vmem_limit_bytes=12 * MIB),
        name="pick_slots",
    )(meta, prods)


def sum_core_kernel(own_ref, oth_ref, *out_refs):
    for s in range(NY):
        out_refs[s][...] = (own_ref[s].astype(F32) + oth_ref[s].astype(F32)).astype(out_refs[s].dtype)


def sum_y_kernel(*refs):
    parts, out_refs = refs[:NY], refs[NY:]
    for t in range(NX):
        out_refs[t][...] = sum(part[t].astype(F32) for part in parts)


def sum_x_kernel(*refs):
    parts, out_ref = refs[:NX], refs[NX]
    out_ref[...] = sum(part[...] for part in parts).astype(BF)


def small_call(kernel, name, outs, *args):
    return pl.pallas_call(
        kernel,
        in_specs=[pl.BlockSpec(memory_space=pltpu.VMEM)] * len(args),
        out_specs=[pl.BlockSpec(memory_space=pltpu.VMEM)] * len(outs),
        out_shape=outs,
        compiler_params=pltpu.CompilerParams(vmem_limit_bytes=12 * MIB),
        name=name,
    )(*args)


def sum_pair(in_own, in_oth):
    line = lambda dtype: jax.ShapeDtypeStruct(in_own.shape[1:], dtype)
    got = lax.ppermute(in_oth, "col", CORE_SWAP)
    return small_call(sum_core_kernel, "sum_core", [line(F32)] + [line(BF)] * (NY - 1), in_own, got)


def sum_plane(by_y):
    _, piece, toks = by_y[0].shape
    got = [by_y[0]] + [lax.ppermute(by_y[s], "col", Y_SHIFTS[s]) for s in range(1, NY)]
    by_x = small_call(sum_y_kernel, "sum_y", [jax.ShapeDtypeStruct((piece, toks), F32)] * NX, *got)
    got = [by_x[0]] + [lax.ppermute(by_x[t], "col", X_SHIFTS[t]) for t in range(1, NX)]
    return small_call(sum_x_kernel, "sum_x", [jax.ShapeDtypeStruct((piece, toks), BF)], *got)[0]


def tables_kernel(at, mask_ref, owner_ref, listed_ref, slots_ref):
    model_blocks = mask_ref.shape[0]
    count, owners = listed_ref.shape[1], slots_ref.shape[1]
    for s in range(owners):
        slots_ref[0, s] = 0
        slots_ref[1, s] = 0
        slots_ref[2, s] = 0

    def look(i, k):
        hid, mod = lax.div(i, model_blocks), lax.rem(i, model_blocks)
        full = mask_ref[mod, at[0] + hid]
        owner = owner_ref[mod, at[0] + hid]

        @pl.when(full == 1)
        def _():
            listed_ref[0, k] = owner
            listed_ref[1, k] = hid
            listed_ref[2, k] = mod
            slots_ref[0, owner] = hid
            slots_ref[1, owner] = mod
            slots_ref[2, owner] = 1

        return k + full

    lax.fori_loop(0, count * 4, look, 0)


def layout_tables(block_mask, block_owner, group, n_groups, owners):
    hidden_blocks, model_blocks = block_mask.shape
    per_group = hidden_blocks // n_groups
    smem = pl.BlockSpec(memory_space=pltpu.SMEM)
    return pl.pallas_call(
        tables_kernel,
        in_specs=[smem] * 3,
        out_specs=[smem] * 2,
        out_shape=[
            jax.ShapeDtypeStruct((3, per_group * model_blocks // 4), jnp.int32),
            jax.ShapeDtypeStruct((3, owners), jnp.int32),
        ],
        name="layout_tables",
    )((group * per_group).reshape(1).astype(jnp.int32), block_mask.T, block_owner.T)


def line_x(x):
    return jnp.stack([x] + [lax.ppermute(x, "col", X_SHIFTS[t]) for t in range(1, NX)])


def share_y(x):
    half = x.shape[0] // 2
    before = lax.ppermute(x, "col", Y_SHIFTS[1])
    after = lax.ppermute(x, "col", Y_SHIFTS[NY - 1])
    far_lo = lax.ppermute(before[:half], "col", Y_SHIFTS[1])
    far_hi = lax.ppermute(after[half:], "col", Y_SHIFTS[NY - 1])
    return x, before, far_lo, far_hi, after


def per_device(activations, out_grad, weight_slots, block_mask, block_owner):
    blk = weight_slots.shape[2]
    owners, groups = lax.axis_size("row"), lax.axis_size("col")
    group = lax.axis_index("col")
    toks, piece = activations.shape
    hidden = out_grad.shape[1]
    chunk = blk // owners
    rows = hidden // owners
    listed, slots = layout_tables(block_mask, block_owner, group, groups, owners)
    place = jnp.stack([group // (NY * NC), group // NC % NY, group % NC]).astype(jnp.int32)

    w_all = lax.all_gather(weight_slots[0, 0], "row", axis=0)
    act_t = activations.T
    wide = jnp.broadcast_to(act_t[None], (groups, piece, toks))
    act_all = lax.all_to_all(wide, "col", 0, 0, tiled=True).reshape(groups * piece, toks)
    act_z = lax.all_gather(act_t, "row", axis=0)

    grad_send = out_grad.T.reshape(-1, owners, chunk, toks).transpose(1, 0, 2, 3)
    grad_send = grad_send.reshape(owners, rows, toks)
    grad_send, act_z, act_all = lax.optimization_barrier((grad_send, act_z, act_all))
    grad_z = lax.all_to_all(grad_send, "row", 0, 0, tiled=True)
    here, before, far_lo, far_hi, after = share_y(act_z)
    grad_z, far_lo, far_hi, listed, slots = lax.optimization_barrier((grad_z, far_lo, far_hi, listed, slots))
    act_y = (here, before, far_lo, far_hi, after)

    grad_own = line_x(grad_z)
    grad_oth = lax.ppermute(grad_own, "col", CORE_SWAP)
    scale = 1.0 / math.sqrt(toks * owners)
    prods = wgrad_products(place, grad_own, grad_oth, act_y, scale)
    prods = lax.all_to_all(prods, "col", 0, 0, tiled=True, axis_index_groups=XC_GROUPS)
    slot_parts = pick_slots(slots, prods, chunk, blk)

    outputs, in_own, in_oth = tokens_step(listed, place, act_all, out_grad, w_all)
    by_y = sum_pair(in_own, in_oth)
    slot_parts, by_y = lax.optimization_barrier((slot_parts, by_y))
    weight_grad = lax.all_to_all(slot_parts, "row", 0, 0, tiled=True).reshape(1, 1, blk, blk)
    return outputs, sum_plane(by_y).T, weight_grad


def solution(mesh):
    placed = (P("row", "col"), P("row", "col"), P("col", "row", None, None), P(), P())
    return jax.shard_map(
        per_device,
        mesh=mesh,
        in_specs=placed,
        out_specs=(P("row", "col"), P("row", "col"), P("col", "row", None, None)),
        check_vma=False,
    )
```

```python
import functools
import math

import jax
import jax.numpy as jnp
from jax import lax
from jax.experimental import pallas as pl
from jax.experimental.pallas import tpu as pltpu
from jax.sharding import PartitionSpec as P

BF = jnp.bfloat16
F32 = jnp.float32
NX, NY, NC = 4, 4, 2
MIB = 1024 * 1024


def col_of(x, y, c):
    return (x * NY + y) * NC + c


PLANE = [(x, y, c) for x in range(NX) for y in range(NY) for c in range(NC)]
X_GROUPS = [[col_of(x, y, c) for x in range(NX)] for y in range(NY) for c in range(NC)]
CORE_SWAP = [(col_of(x, y, c), col_of(x, y, 1 - c)) for x, y, c in PLANE]
X_SHIFTS = {s: [(col_of(x, y, c), col_of((x + s) % NX, y, c)) for x, y, c in PLANE] for s in range(1, NX)}
Y_SHIFTS = {s: [(col_of(x, y, c), col_of(x, (y + s) % NY, c)) for x, y, c in PLANE] for s in range(1, NY)}


def aligned(start, size, step):
    return pl.ds(pl.multiple_of(start, step), size)


def tokens_kernel(meta, place, act_ref, grad_ref, w_ref, out_ref, in_own, in_oth, w_buf, out_acc, in_acc, in_rows, sems):
    count, blk, _ = w_buf.shape
    piece = in_own.shape[2]
    x, y, core = place[0], place[1], place[2]
    copies = [pltpu.make_async_copy(w_ref.at[meta[0, k]], w_buf.at[k], sems.at[k]) for k in range(count)]
    for copy in copies:
        copy.start()
    out_acc[...] = jnp.zeros_like(out_acc)
    in_acc[...] = jnp.zeros_like(in_acc)
    for k in range(count):
        hid = aligned(meta[1, k] * blk, blk, blk)
        mod = aligned(meta[2, k] * blk, blk, blk)
        copies[k].wait()
        w = w_buf[k]
        out_acc[hid, :] += jnp.dot(w, act_ref[mod, :], preferred_element_type=F32)
        in_acc[:, mod] += jnp.dot(grad_ref[:, hid], w, preferred_element_type=F32)
    out_ref[...] = out_acc[...].T.astype(BF)
    in_rows[...] = in_acc[...].T.astype(BF)
    for s in range(NY):
        for t in range(NX):
            chip = (lax.rem(x + t, NX) * NY + lax.rem(y + s, NY)) * NC
            in_own[s, t] = in_rows[aligned((chip + core) * piece, piece, 64), :]
            in_oth[s, t] = in_rows[aligned((chip + 1 - core) * piece, piece, 64), :]


def tokens_step(meta, place, act, grad, w_all):
    count, blk = meta.shape[1], w_all.shape[1]
    feats, toks = act.shape
    hidden = grad.shape[1]
    parts = pltpu.HBM((NY, NX, feats // (NX * NY * NC), toks), BF)
    vmem = pl.BlockSpec(memory_space=pltpu.VMEM)
    smem = pl.BlockSpec(memory_space=pltpu.SMEM)
    return pl.pallas_call(
        tokens_kernel,
        in_specs=[smem, smem, vmem, vmem, pl.BlockSpec(memory_space=pltpu.HBM)],
        out_specs=[vmem] * 3,
        out_shape=[jax.ShapeDtypeStruct((toks, hidden), BF), parts, parts],
        scratch_shapes=[
            pltpu.VMEM((count, blk, blk), BF),
            pltpu.VMEM((hidden, toks), F32),
            pltpu.VMEM((toks, feats), F32),
            pltpu.VMEM((feats, toks), BF),
            pltpu.SemaphoreType.DMA((count,)),
        ],
        compiler_params=pltpu.CompilerParams(vmem_limit_bytes=28 * MIB),
        name="tokens_step",
    )(meta, place, act, grad, in_hbm(w_all))


def in_hbm(x):
    return pltpu.with_memory_space_constraint(x, pltpu.HBM)


def features_kernel(place, *refs):
    n_in = (len(refs) - 2) // 2
    in_refs, out_ref, buffers, sems = refs[:n_in], refs[n_in], refs[n_in + 1 : -1], refs[-1]
    copies = [pltpu.make_async_copy(in_refs[i], buffers[i], sems.at[i]) for i in range(n_in)]
    for copy in copies:
        copy.start()
    n_z, piece, toks = buffers[0].shape
    y, core = place[1], place[2]
    parts = ((0, 0), (1, 0), (2, 0), (2, n_z // 2), (3, 0))
    for i in range(n_in):
        s, first = parts[i % len(parts)]
        side = core if i < len(parts) else 1 - core
        at = aligned((lax.rem(y - s + NY, NY) * NC + side) * piece, piece, 64)
        copies[i].wait()
        for z in range(buffers[i].shape[0]):
            out_ref[at, (first + z) * toks : (first + z + 1) * toks] = buffers[i][z]


def line_features(place, own, oth):
    n_z, piece, toks = own[0].shape
    args = [in_hbm(a) for a in (*own, *oth)]
    return pl.pallas_call(
        features_kernel,
        in_specs=[pl.BlockSpec(memory_space=pltpu.SMEM)]
        + [pl.BlockSpec(memory_space=pltpu.HBM)] * len(args),
        out_specs=pl.BlockSpec(memory_space=pltpu.VMEM),
        out_shape=jax.ShapeDtypeStruct((NY * NC * piece, n_z * toks), BF),
        scratch_shapes=[pltpu.VMEM(a.shape, BF) for a in args] + [pltpu.SemaphoreType.DMA((len(args),))],
        compiler_params=pltpu.CompilerParams(vmem_limit_bytes=20 * MIB),
        name="line_features",
    )(place, *args)


def wgrad_kernel(place, *refs, scale):
    grad_refs, (feats_ref, out_ref, a_buf) = refs[:NX], refs[NX:]
    n_z, rows, toks = grad_refs[0].shape
    for t in range(NX):
        for z in range(n_z):
            a_buf[t * rows : (t + 1) * rows, z * toks : (z + 1) * toks] = grad_refs[t][z]
    prod = lax.dot_general(
        a_buf[...], feats_ref[...], (((1,), (1,)), ((), ())), preferred_element_type=F32
    )
    prod = (prod * scale).astype(BF)
    for t in range(NX):
        out_ref[lax.rem(place[0] - t + NX, NX)] = prod[t * rows : (t + 1) * rows]


def wgrad_products(place, grads, feats, scale):
    n_z, rows, toks = grads[0].shape
    vmem = pl.BlockSpec(memory_space=pltpu.VMEM)
    return pl.pallas_call(
        functools.partial(wgrad_kernel, scale=scale),
        in_specs=[pl.BlockSpec(memory_space=pltpu.SMEM)] + [vmem] * (NX + 1),
        out_specs=vmem,
        out_shape=pltpu.HBM((NX, rows, feats.shape[0]), BF),
        scratch_shapes=[pltpu.VMEM((NX * rows, n_z * toks), BF)],
        compiler_params=pltpu.CompilerParams(vmem_limit_bytes=20 * MIB),
        name="wgrad_products",
    )(place, *grads, feats)


def slots_kernel(meta, prod_ref, out_ref, *, chunk, blk):
    per_x = prod_ref.shape[2] // blk
    for s in range(out_ref.shape[0]):
        hid, mod, full = meta[0, s], meta[1, s], meta[2, s]
        rows = aligned(hid * chunk, chunk, chunk)
        cols = aligned(lax.rem(mod, per_x) * blk, blk, blk)
        part = prod_ref[lax.div(mod, per_x), rows, cols]
        out_ref[s] = jnp.where(full > 0, part, jnp.zeros_like(part))


def pick_slots(meta, prods, chunk, blk):
    owners = meta.shape[1]
    return pl.pallas_call(
        functools.partial(slots_kernel, chunk=chunk, blk=blk),
        in_specs=[
            pl.BlockSpec(memory_space=pltpu.SMEM),
            pl.BlockSpec(memory_space=pltpu.VMEM),
        ],
        out_specs=pl.BlockSpec(memory_space=pltpu.VMEM),
        out_shape=jax.ShapeDtypeStruct((owners, chunk, blk), BF),
        compiler_params=pltpu.CompilerParams(vmem_limit_bytes=12 * MIB),
        name="pick_slots",
    )(meta, prods)


def sum_core_kernel(own_ref, oth_ref, *out_refs):
    for s in range(NY):
        out_refs[s][...] = (own_ref[s].astype(F32) + oth_ref[s].astype(F32)).astype(out_refs[s].dtype)


def sum_y_kernel(*refs):
    parts, out_refs = refs[:NY], refs[NY:]
    for t in range(NX):
        out_refs[t][...] = sum(part[t].astype(F32) for part in parts)


def sum_x_kernel(*refs):
    parts, out_ref = refs[:NX], refs[NX]
    out_ref[...] = sum(part[...] for part in parts).astype(BF)


def small_call(kernel, name, outs, *args):
    return pl.pallas_call(
        kernel,
        in_specs=[pl.BlockSpec(memory_space=pltpu.VMEM)] * len(args),
        out_specs=[pl.BlockSpec(memory_space=pltpu.VMEM)] * len(outs),
        out_shape=outs,
        compiler_params=pltpu.CompilerParams(vmem_limit_bytes=12 * MIB),
        name=name,
    )(*args)


def sum_pair(in_own, in_oth):
    line = lambda dtype: jax.ShapeDtypeStruct(in_own.shape[1:], dtype)
    got = lax.ppermute(in_oth, "col", CORE_SWAP)
    return small_call(sum_core_kernel, "sum_core", [line(F32)] + [line(BF)] * (NY - 1), in_own, got)


def sum_plane(by_y):
    _, piece, toks = by_y[0].shape
    got = [by_y[0]] + [lax.ppermute(by_y[s], "col", Y_SHIFTS[s]) for s in range(1, NY)]
    by_x = small_call(sum_y_kernel, "sum_y", [jax.ShapeDtypeStruct((piece, toks), F32)] * NX, *got)
    got = [by_x[0]] + [lax.ppermute(by_x[t], "col", X_SHIFTS[t]) for t in range(1, NX)]
    return small_call(sum_x_kernel, "sum_x", [jax.ShapeDtypeStruct((piece, toks), BF)], *got)[0]


def tables_kernel(at, mask_ref, owner_ref, listed_ref, slots_ref):
    model_blocks = mask_ref.shape[0]
    count, owners = listed_ref.shape[1], slots_ref.shape[1]
    for s in range(owners):
        slots_ref[0, s] = 0
        slots_ref[1, s] = 0
        slots_ref[2, s] = 0

    def look(i, k):
        hid, mod = lax.div(i, model_blocks), lax.rem(i, model_blocks)
        full = mask_ref[mod, at[0] + hid]
        owner = owner_ref[mod, at[0] + hid]

        @pl.when(full == 1)
        def _():
            listed_ref[0, k] = owner
            listed_ref[1, k] = hid
            listed_ref[2, k] = mod
            slots_ref[0, owner] = hid
            slots_ref[1, owner] = mod
            slots_ref[2, owner] = 1

        return k + full

    lax.fori_loop(0, count * 4, look, 0)


def layout_tables(block_mask, block_owner, group, n_groups, owners):
    hidden_blocks, model_blocks = block_mask.shape
    per_group = hidden_blocks // n_groups
    smem = pl.BlockSpec(memory_space=pltpu.SMEM)
    return pl.pallas_call(
        tables_kernel,
        in_specs=[smem] * 3,
        out_specs=[smem] * 2,
        out_shape=[
            jax.ShapeDtypeStruct((3, per_group * model_blocks // 4), jnp.int32),
            jax.ShapeDtypeStruct((3, owners), jnp.int32),
        ],
        name="layout_tables",
    )((group * per_group).reshape(1).astype(jnp.int32), block_mask.T, block_owner.T)


def line_x(x):
    return [x] + [lax.ppermute(x, "col", X_SHIFTS[t]) for t in range(1, NX)]


def share_y(x):
    half = x.shape[0] // 2
    before = lax.ppermute(x, "col", Y_SHIFTS[1])
    after = lax.ppermute(x, "col", Y_SHIFTS[NY - 1])
    far_lo = lax.ppermute(before[:half], "col", Y_SHIFTS[1])
    far_hi = lax.ppermute(after[half:], "col", Y_SHIFTS[NY - 1])
    return x, before, far_lo, far_hi, after


def per_device(activations, out_grad, weight_slots, block_mask, block_owner):
    blk = weight_slots.shape[2]
    owners, groups = lax.axis_size("row"), lax.axis_size("col")
    group = lax.axis_index("col")
    toks, piece = activations.shape
    hidden = out_grad.shape[1]
    chunk = blk // owners
    rows = hidden // owners
    listed, slots = layout_tables(block_mask, block_owner, group, groups, owners)
    place = jnp.stack([group // (NY * NC), group // NC % NY, group % NC]).astype(jnp.int32)

    w_all = lax.all_gather(weight_slots[0, 0], "row", axis=0)
    act_t = activations.T
    wide = jnp.broadcast_to(act_t[None], (groups, piece, toks))
    act_all = lax.all_to_all(wide, "col", 0, 0, tiled=True).reshape(groups * piece, toks)
    act_z = lax.all_gather(act_t, "row", axis=0)

    grad_send = out_grad.T.reshape(-1, owners, chunk, toks).transpose(1, 0, 2, 3)
    grad_send = grad_send.reshape(owners, rows, toks)
    grad_send, act_z, act_all = lax.optimization_barrier((grad_send, act_z, act_all))
    grad_z = lax.all_to_all(grad_send, "row", 0, 0, tiled=True)
    here, before, far_lo, far_hi, after = share_y(act_z)
    grad_z, far_lo, far_hi, listed, slots = lax.optimization_barrier((grad_z, far_lo, far_hi, listed, slots))
    act_own = (here, before, far_lo, far_hi, after)
    act_oth = [lax.ppermute(a, "col", CORE_SWAP) for a in act_own]

    feats = line_features(place, act_own, act_oth)
    prods = wgrad_products(place, line_x(grad_z), feats, 1.0 / math.sqrt(toks * owners))
    prods = lax.all_to_all(prods, "col", 0, 0, tiled=True, axis_index_groups=X_GROUPS)
    slot_parts = pick_slots(slots, prods, chunk, blk)

    outputs, in_own, in_oth = tokens_step(listed, place, act_all, out_grad, w_all)
    by_y = sum_pair(in_own, in_oth)
    slot_parts, by_y = lax.optimization_barrier((slot_parts, by_y))
    weight_grad = lax.all_to_all(slot_parts, "row", 0, 0, tiled=True).reshape(1, 1, blk, blk)
    return outputs, sum_plane(by_y).T, weight_grad


def solution(mesh):
    placed = (P("row", "col"), P("row", "col"), P("col", "row", None, None), P(), P())
    return jax.shard_map(
        per_device,
        mesh=mesh,
        in_specs=placed,
        out_specs=(P("row", "col"), P("row", "col"), P("col", "row", None, None)),
        check_vma=False,
    )
```

```python
import functools
import math

import jax
import jax.numpy as jnp
from jax import lax
from jax.experimental import pallas as pl
from jax.experimental.pallas import tpu as pltpu
from jax.sharding import PartitionSpec as P

BF = jnp.bfloat16
F32 = jnp.float32
NX, NY, NC = 4, 4, 2
MIB = 1024 * 1024


def col_of(x, y, c):
    return (x * NY + y) * NC + c


PLANE = [(x, y, c) for x in range(NX) for y in range(NY) for c in range(NC)]
X_GROUPS = [[col_of(x, y, c) for x in range(NX)] for y in range(NY) for c in range(NC)]
CORE_SWAP = [(col_of(x, y, c), col_of(x, y, 1 - c)) for x, y, c in PLANE]
X_SHIFTS = {s: [(col_of(x, y, c), col_of((x + s) % NX, y, c)) for x, y, c in PLANE] for s in range(1, NX)}
Y_SHIFTS = {s: [(col_of(x, y, c), col_of(x, (y + s) % NY, c)) for x, y, c in PLANE] for s in range(1, NY)}


def aligned(start, size, step):
    return pl.ds(pl.multiple_of(start, step), size)


def tokens_kernel(meta, place, act_ref, grad_ref, w_ref, out_ref, in_own, in_oth, w_buf, out_acc, in_acc, in_rows, sems):
    count, blk, _ = w_buf.shape
    piece = in_own.shape[2]
    x, y, core = place[0], place[1], place[2]
    copies = [pltpu.make_async_copy(w_ref.at[meta[0, k]], w_buf.at[k], sems.at[k]) for k in range(count)]
    for copy in copies:
        copy.start()
    out_acc[...] = jnp.zeros_like(out_acc)
    in_acc[...] = jnp.zeros_like(in_acc)
    for k in range(count):
        hid = aligned(meta[1, k] * blk, blk, blk)
        mod = aligned(meta[2, k] * blk, blk, blk)
        copies[k].wait()
        w = w_buf[k]
        out_acc[hid, :] += jnp.dot(w, act_ref[mod, :], preferred_element_type=F32)
        in_acc[:, mod] += jnp.dot(grad_ref[:, hid], w, preferred_element_type=F32)
    out_ref[...] = out_acc[...].T.astype(BF)
    in_rows[...] = in_acc[...].T.astype(BF)
    for s in range(NY):
        for t in range(NX):
            chip = (lax.rem(x + t, NX) * NY + lax.rem(y + s, NY)) * NC
            in_own[s, t] = in_rows[aligned((chip + core) * piece, piece, 64), :]
            in_oth[s, t] = in_rows[aligned((chip + 1 - core) * piece, piece, 64), :]


def tokens_step(meta, place, act, grad, w_all):
    count, blk = meta.shape[1], w_all.shape[1]
    feats, toks = act.shape
    hidden = grad.shape[1]
    parts = pltpu.HBM((NY, NX, feats // (NX * NY * NC), toks), BF)
    vmem = pl.BlockSpec(memory_space=pltpu.VMEM)
    smem = pl.BlockSpec(memory_space=pltpu.SMEM)
    return pl.pallas_call(
        tokens_kernel,
        in_specs=[smem, smem, vmem, vmem, pl.BlockSpec(memory_space=pltpu.HBM)],
        out_specs=[vmem] * 3,
        out_shape=[jax.ShapeDtypeStruct((toks, hidden), BF), parts, parts],
        scratch_shapes=[
            pltpu.VMEM((count, blk, blk), BF),
            pltpu.VMEM((hidden, toks), F32),
            pltpu.VMEM((toks, feats), F32),
            pltpu.VMEM((feats, toks), BF),
            pltpu.SemaphoreType.DMA((count,)),
        ],
        compiler_params=pltpu.CompilerParams(vmem_limit_bytes=28 * MIB),
        name="tokens_step",
    )(meta, place, act, grad, in_hbm(w_all))


def in_hbm(x):
    return pltpu.with_memory_space_constraint(x, pltpu.HBM)


def features_kernel(place, *refs):
    n_in = (len(refs) - 2) // 2
    in_refs, out_ref, buffers, sems = refs[:n_in], refs[n_in], refs[n_in + 1 : -1], refs[-1]
    copies = [pltpu.make_async_copy(in_refs[i], buffers[i], sems.at[i]) for i in range(n_in)]
    for copy in copies:
        copy.start()
    n_z, piece, toks = buffers[0].shape
    y, core = place[1], place[2]
    parts = ((0, 0), (1, 0), (2, 0), (2, n_z // 2), (3, 0))
    for i in range(n_in):
        s, first = parts[i % len(parts)]
        side = core if i < len(parts) else 1 - core
        at = aligned((lax.rem(y - s + NY, NY) * NC + side) * piece, piece, 64)
        copies[i].wait()
        for z in range(buffers[i].shape[0]):
            out_ref[at, (first + z) * toks : (first + z + 1) * toks] = buffers[i][z]


def line_features(place, own, oth):
    n_z, piece, toks = own[0].shape
    args = [in_hbm(a) for a in (*own, *oth)]
    return pl.pallas_call(
        features_kernel,
        in_specs=[pl.BlockSpec(memory_space=pltpu.SMEM)]
        + [pl.BlockSpec(memory_space=pltpu.HBM)] * len(args),
        out_specs=pl.BlockSpec(memory_space=pltpu.VMEM),
        out_shape=pltpu.HBM((NY * NC * piece, n_z * toks), BF),
        scratch_shapes=[pltpu.VMEM(a.shape, BF) for a in args] + [pltpu.SemaphoreType.DMA((len(args),))],
        compiler_params=pltpu.CompilerParams(vmem_limit_bytes=20 * MIB),
        name="line_features",
    )(place, *args)


def wgrad_kernel(grad_ref, feats_ref, out_ref, a_buf, b_buf, sems, *, scale):
    n_x, n_z, rows, toks = grad_ref.shape
    span = feats_ref.shape[0] // NY
    parts = [pl.ds(y * span, span) for y in range(NY)]
    copies = [pltpu.make_async_copy(feats_ref.at[parts[y]], b_buf.at[parts[y]], sems.at[y]) for y in range(NY)]
    for copy in copies:
        copy.start()
    for x in range(n_x):
        for z in range(n_z):
            a_buf[x * rows : (x + 1) * rows, z * toks : (z + 1) * toks] = grad_ref[x, z]
    for y in range(NY):
        copies[y].wait()
        prod = lax.dot_general(
            a_buf[...], b_buf[parts[y]], (((1,), (1,)), ((), ())), preferred_element_type=F32
        )
        prod = (prod * scale).astype(BF)
        for x in range(n_x):
            out_ref[x, :, parts[y]] = prod[x * rows : (x + 1) * rows]


def wgrad_products(grads, feats, scale):
    n_x, n_z, rows, toks = grads.shape
    vmem = pl.BlockSpec(memory_space=pltpu.VMEM)
    return pl.pallas_call(
        functools.partial(wgrad_kernel, scale=scale),
        in_specs=[vmem, pl.BlockSpec(memory_space=pltpu.HBM)],
        out_specs=vmem,
        out_shape=pltpu.HBM((n_x, rows, feats.shape[0]), BF),
        scratch_shapes=[
            pltpu.VMEM((n_x * rows, n_z * toks), BF),
            pltpu.VMEM(feats.shape, BF),
            pltpu.SemaphoreType.DMA((NY,)),
        ],
        compiler_params=pltpu.CompilerParams(vmem_limit_bytes=20 * MIB),
        name="wgrad_products",
    )(grads, in_hbm(feats))


def slots_kernel(meta, prod_ref, out_ref, *, chunk, blk):
    per_x = prod_ref.shape[2] // blk
    for s in range(out_ref.shape[0]):
        hid, mod, full = meta[0, s], meta[1, s], meta[2, s]
        rows = aligned(hid * chunk, chunk, chunk)
        cols = aligned(lax.rem(mod, per_x) * blk, blk, blk)
        part = prod_ref[lax.div(mod, per_x), rows, cols]
        out_ref[s] = jnp.where(full > 0, part, jnp.zeros_like(part))


def pick_slots(meta, prods, chunk, blk):
    owners = meta.shape[1]
    return pl.pallas_call(
        functools.partial(slots_kernel, chunk=chunk, blk=blk),
        in_specs=[
            pl.BlockSpec(memory_space=pltpu.SMEM),
            pl.BlockSpec(memory_space=pltpu.VMEM),
        ],
        out_specs=pl.BlockSpec(memory_space=pltpu.VMEM),
        out_shape=jax.ShapeDtypeStruct((owners, chunk, blk), BF),
        compiler_params=pltpu.CompilerParams(vmem_limit_bytes=12 * MIB),
        name="pick_slots",
    )(meta, prods)


def sum_core_kernel(own_ref, oth_ref, *out_refs):
    for s in range(NY):
        out_refs[s][...] = (own_ref[s].astype(F32) + oth_ref[s].astype(F32)).astype(out_refs[s].dtype)


def sum_y_kernel(*refs):
    parts, out_refs = refs[:NY], refs[NY:]
    for t in range(NX):
        out_refs[t][...] = sum(part[t].astype(F32) for part in parts)


def sum_x_kernel(*refs):
    parts, out_ref = refs[:NX], refs[NX]
    out_ref[...] = sum(part[...] for part in parts).astype(BF)


def small_call(kernel, name, outs, *args):
    return pl.pallas_call(
        kernel,
        in_specs=[pl.BlockSpec(memory_space=pltpu.VMEM)] * len(args),
        out_specs=[pl.BlockSpec(memory_space=pltpu.VMEM)] * len(outs),
        out_shape=outs,
        compiler_params=pltpu.CompilerParams(vmem_limit_bytes=12 * MIB),
        name=name,
    )(*args)


def sum_pair(in_own, in_oth):
    line = lambda dtype: jax.ShapeDtypeStruct(in_own.shape[1:], dtype)
    got = lax.ppermute(in_oth, "col", CORE_SWAP)
    return small_call(sum_core_kernel, "sum_core", [line(F32)] + [line(BF)] * (NY - 1), in_own, got)


def sum_plane(by_y):
    _, piece, toks = by_y[0].shape
    got = [by_y[0]] + [lax.ppermute(by_y[s], "col", Y_SHIFTS[s]) for s in range(1, NY)]
    by_x = small_call(sum_y_kernel, "sum_y", [jax.ShapeDtypeStruct((piece, toks), F32)] * NX, *got)
    got = [by_x[0]] + [lax.ppermute(by_x[t], "col", X_SHIFTS[t]) for t in range(1, NX)]
    return small_call(sum_x_kernel, "sum_x", [jax.ShapeDtypeStruct((piece, toks), BF)], *got)[0]


def tables_kernel(at, mask_ref, owner_ref, listed_ref, slots_ref):
    model_blocks = mask_ref.shape[0]
    count, owners = listed_ref.shape[1], slots_ref.shape[1]
    for s in range(owners):
        slots_ref[0, s] = 0
        slots_ref[1, s] = 0
        slots_ref[2, s] = 0

    def look(i, k):
        hid, mod = lax.div(i, model_blocks), lax.rem(i, model_blocks)
        full = mask_ref[mod, at[0] + hid]
        owner = owner_ref[mod, at[0] + hid]

        @pl.when(full == 1)
        def _():
            listed_ref[0, k] = owner
            listed_ref[1, k] = hid
            listed_ref[2, k] = mod
            slots_ref[0, owner] = hid
            slots_ref[1, owner] = mod
            slots_ref[2, owner] = 1

        return k + full

    lax.fori_loop(0, count * 4, look, 0)


def layout_tables(block_mask, block_owner, group, n_groups, owners):
    hidden_blocks, model_blocks = block_mask.shape
    per_group = hidden_blocks // n_groups
    smem = pl.BlockSpec(memory_space=pltpu.SMEM)
    return pl.pallas_call(
        tables_kernel,
        in_specs=[smem] * 3,
        out_specs=[smem] * 2,
        out_shape=[
            jax.ShapeDtypeStruct((3, per_group * model_blocks // 4), jnp.int32),
            jax.ShapeDtypeStruct((3, owners), jnp.int32),
        ],
        name="layout_tables",
    )((group * per_group).reshape(1).astype(jnp.int32), block_mask.T, block_owner.T)


def spread_kernel(in_ref, out_ref, sems):
    copies = [pltpu.make_async_copy(in_ref, out_ref.at[i], sems.at[i]) for i in range(out_ref.shape[0])]
    for copy in copies:
        copy.start()
    for copy in copies:
        copy.wait()


def spread(x, n):
    return pl.pallas_call(
        spread_kernel,
        in_specs=[pl.BlockSpec(memory_space=pltpu.VMEM)],
        out_specs=pl.BlockSpec(memory_space=pltpu.HBM),
        out_shape=pltpu.HBM((n, *x.shape), x.dtype),
        scratch_shapes=[pltpu.SemaphoreType.DMA((n,))],
        compiler_params=pltpu.CompilerParams(vmem_limit_bytes=4 * MIB),
        name="spread",
    )(x)


def share_y(x):
    half = x.shape[0] // 2
    before = lax.ppermute(x, "col", Y_SHIFTS[1])
    after = lax.ppermute(x, "col", Y_SHIFTS[NY - 1])
    far_lo = lax.ppermute(before[:half], "col", Y_SHIFTS[1])
    far_hi = lax.ppermute(after[half:], "col", Y_SHIFTS[NY - 1])
    return x, before, far_lo, far_hi, after


def per_device(activations, out_grad, weight_slots, block_mask, block_owner):
    blk = weight_slots.shape[2]
    owners, groups = lax.axis_size("row"), lax.axis_size("col")
    group = lax.axis_index("col")
    toks, piece = activations.shape
    hidden = out_grad.shape[1]
    chunk = blk // owners
    rows = hidden // owners
    listed, slots = layout_tables(block_mask, block_owner, group, groups, owners)
    place = jnp.stack([group // (NY * NC), group // NC % NY, group % NC]).astype(jnp.int32)

    w_all = lax.all_gather(weight_slots[0, 0], "row", axis=0)
    act_t = activations.T
    act_all = lax.all_to_all(spread(act_t, groups), "col", 0, 0, tiled=True).reshape(groups * piece, toks)
    act_z = lax.all_gather(act_t, "row", axis=0)

    grad_send = out_grad.T.reshape(-1, owners, chunk, toks).transpose(1, 0, 2, 3)
    grad_send = grad_send.reshape(owners, rows, toks)
    grad_send, act_z, act_all = lax.optimization_barrier((grad_send, act_z, act_all))
    grad_z = lax.all_to_all(grad_send, "row", 0, 0, tiled=True)
    here, before, far_lo, far_hi, after = share_y(act_z)
    swap = lambda a: lax.ppermute(a, "col", CORE_SWAP)
    near_oth = swap(here), swap(before), swap(after)
    grad_z, far, near_oth, listed, slots = lax.optimization_barrier(
        (grad_z, (far_lo, far_hi), near_oth, listed, slots)
    )
    act_own = here, before, *far, after
    act_oth = near_oth[0], near_oth[1], swap(far[0]), swap(far[1]), near_oth[2]
    grad_x = lax.all_to_all(spread(grad_z, NX), "col", 0, 0, tiled=True, axis_index_groups=X_GROUPS)

    feats = line_features(place, act_own, act_oth)
    prods = wgrad_products(grad_x, feats, 1.0 / math.sqrt(toks * owners))
    prods = lax.all_to_all(prods, "col", 0, 0, tiled=True, axis_index_groups=X_GROUPS)
    slot_parts = pick_slots(slots, prods, chunk, blk)

    outputs, in_own, in_oth = tokens_step(listed, place, act_all, out_grad, w_all)
    by_y = sum_pair(in_own, in_oth)
    slot_parts, by_y = lax.optimization_barrier((slot_parts, by_y))
    weight_grad = lax.all_to_all(slot_parts, "row", 0, 0, tiled=True).reshape(1, 1, blk, blk)
    return outputs, sum_plane(by_y).T, weight_grad


def solution(mesh):
    placed = (P("row", "col"), P("row", "col"), P("col", "row", None, None), P(), P())
    return jax.shard_map(
        per_device,
        mesh=mesh,
        in_specs=placed,
        out_specs=(P("row", "col"), P("row", "col"), P("col", "row", None, None)),
        check_vma=False,
    )
```

```python
import functools
import math

import jax
import jax.numpy as jnp
from jax import lax
from jax.experimental import pallas as pl
from jax.experimental.pallas import tpu as pltpu
from jax.sharding import PartitionSpec as P

BF = jnp.bfloat16
F32 = jnp.float32
NX, NY, NC = 4, 4, 2
MIB = 1024 * 1024


def col_of(x, y, c):
    return (x * NY + y) * NC + c


PLANE = [(x, y, c) for x in range(NX) for y in range(NY) for c in range(NC)]
X_GROUPS = [[col_of(x, y, c) for x in range(NX)] for y in range(NY) for c in range(NC)]
CORE_SWAP = [(col_of(x, y, c), col_of(x, y, 1 - c)) for x, y, c in PLANE]
X_SHIFTS = {s: [(col_of(x, y, c), col_of((x + s) % NX, y, c)) for x, y, c in PLANE] for s in range(1, NX)}
Y_SHIFTS = {s: [(col_of(x, y, c), col_of(x, (y + s) % NY, c)) for x, y, c in PLANE] for s in range(1, NY)}


def aligned(start, size, step):
    return pl.ds(pl.multiple_of(start, step), size)


def tokens_kernel(meta, place, act_ref, grad_ref, w_ref, out_ref, in_own, in_oth, w_buf, out_acc, in_acc, in_rows, sems):
    count, blk, _ = w_buf.shape
    piece = in_own.shape[2]
    x, y, core = place[0], place[1], place[2]
    copies = [pltpu.make_async_copy(w_ref.at[meta[0, k]], w_buf.at[k], sems.at[k]) for k in range(count)]
    for copy in copies:
        copy.start()
    out_acc[...] = jnp.zeros_like(out_acc)
    in_acc[...] = jnp.zeros_like(in_acc)
    for k in range(count):
        hid = aligned(meta[1, k] * blk, blk, blk)
        mod = aligned(meta[2, k] * blk, blk, blk)
        copies[k].wait()
        w = w_buf[k]
        out_acc[hid, :] += jnp.dot(w, act_ref[mod, :], preferred_element_type=F32)
        in_acc[:, mod] += jnp.dot(grad_ref[:, hid], w, preferred_element_type=F32)
    out_ref[...] = out_acc[...].T.astype(BF)
    in_rows[...] = in_acc[...].T.astype(BF)
    for s in range(NY):
        for t in range(NX):
            chip = (lax.rem(x + t, NX) * NY + lax.rem(y + s, NY)) * NC
            in_own[s, t] = in_rows[aligned((chip + core) * piece, piece, 64), :]
            in_oth[s, t] = in_rows[aligned((chip + 1 - core) * piece, piece, 64), :]


def tokens_step(meta, place, act, grad, w_all):
    count, blk = meta.shape[1], w_all.shape[1]
    feats, toks = act.shape
    hidden = grad.shape[1]
    parts = pltpu.HBM((NY, NX, feats // (NX * NY * NC), toks), BF)
    vmem = pl.BlockSpec(memory_space=pltpu.VMEM)
    smem = pl.BlockSpec(memory_space=pltpu.SMEM)
    return pl.pallas_call(
        tokens_kernel,
        in_specs=[smem, smem, vmem, vmem, pl.BlockSpec(memory_space=pltpu.HBM)],
        out_specs=[vmem] * 3,
        out_shape=[jax.ShapeDtypeStruct((toks, hidden), BF), parts, parts],
        scratch_shapes=[
            pltpu.VMEM((count, blk, blk), BF),
            pltpu.VMEM((hidden, toks), F32),
            pltpu.VMEM((toks, feats), F32),
            pltpu.VMEM((feats, toks), BF),
            pltpu.SemaphoreType.DMA((count,)),
        ],
        compiler_params=pltpu.CompilerParams(vmem_limit_bytes=28 * MIB),
        name="tokens_step",
    )(meta, place, act, grad, in_hbm(w_all))


def in_hbm(x):
    return pltpu.with_memory_space_constraint(x, pltpu.HBM)


def features_kernel(place, *refs):
    n_in = (len(refs) - 2) // 2
    in_refs, out_ref, buffers, sems = refs[:n_in], refs[n_in], refs[n_in + 1 : -1], refs[-1]
    copies = [pltpu.make_async_copy(in_refs[i], buffers[i], sems.at[i]) for i in range(n_in)]
    for copy in copies:
        copy.start()
    n_z, piece, toks = buffers[0].shape
    y, core = place[1], place[2]
    parts = ((0, 0), (1, 0), (2, 0), (2, n_z // 2), (3, 0))
    for i in range(n_in):
        s, first = parts[i % len(parts)]
        side = core if i < len(parts) else 1 - core
        at = aligned((lax.rem(y - s + NY, NY) * NC + side) * piece, piece, 64)
        copies[i].wait()
        for z in range(buffers[i].shape[0]):
            out_ref[at, (first + z) * toks : (first + z + 1) * toks] = buffers[i][z]


def line_features(place, own, oth):
    n_z, piece, toks = own[0].shape
    args = [in_hbm(a) for a in (*own, *oth)]
    return pl.pallas_call(
        features_kernel,
        in_specs=[pl.BlockSpec(memory_space=pltpu.SMEM)]
        + [pl.BlockSpec(memory_space=pltpu.HBM)] * len(args),
        out_specs=pl.BlockSpec(memory_space=pltpu.VMEM),
        out_shape=pltpu.HBM((NY * NC * piece, n_z * toks), BF),
        scratch_shapes=[pltpu.VMEM(a.shape, BF) for a in args] + [pltpu.SemaphoreType.DMA((len(args),))],
        compiler_params=pltpu.CompilerParams(vmem_limit_bytes=20 * MIB),
        name="line_features",
    )(place, *args)


def wgrad_kernel(grad_ref, feats_ref, out_ref, a_buf, b_buf, sems, *, scale):
    n_x, n_z, rows, toks = grad_ref.shape
    steps = sems.shape[0]
    span = feats_ref.shape[0] // steps
    parts = [pl.ds(i * span, span) for i in range(steps)]
    copies = [pltpu.make_async_copy(feats_ref.at[parts[i]], b_buf.at[parts[i]], sems.at[i]) for i in range(steps)]
    for copy in copies:
        copy.start()
    for x in range(n_x):
        for z in range(n_z):
            a_buf[x * rows : (x + 1) * rows, z * toks : (z + 1) * toks] = grad_ref[x, z]
    for i in range(steps):
        copies[i].wait()
        prod = lax.dot_general(
            a_buf[...], b_buf[parts[i]], (((1,), (1,)), ((), ())), preferred_element_type=F32
        )
        prod = (prod * scale).astype(BF)
        for x in range(n_x):
            out_ref[x, :, parts[i]] = prod[x * rows : (x + 1) * rows]


def wgrad_products(grads, feats, scale):
    n_x, n_z, rows, toks = grads.shape
    vmem = pl.BlockSpec(memory_space=pltpu.VMEM)
    return pl.pallas_call(
        functools.partial(wgrad_kernel, scale=scale),
        in_specs=[vmem, pl.BlockSpec(memory_space=pltpu.HBM)],
        out_specs=vmem,
        out_shape=pltpu.HBM((n_x, rows, feats.shape[0]), BF),
        scratch_shapes=[
            pltpu.VMEM((n_x * rows, n_z * toks), BF),
            pltpu.VMEM(feats.shape, BF),
            pltpu.SemaphoreType.DMA((3,)),
        ],
        compiler_params=pltpu.CompilerParams(vmem_limit_bytes=20 * MIB),
        name="wgrad_products",
    )(grads, in_hbm(feats))


def slots_kernel(meta, prod_ref, out_ref, *, chunk, blk):
    per_x = prod_ref.shape[2] // blk
    for s in range(out_ref.shape[0]):
        hid, mod, full = meta[0, s], meta[1, s], meta[2, s]
        rows = aligned(hid * chunk, chunk, chunk)
        cols = aligned(lax.rem(mod, per_x) * blk, blk, blk)
        part = prod_ref[lax.div(mod, per_x), rows, cols]
        out_ref[s] = jnp.where(full > 0, part, jnp.zeros_like(part))


def pick_slots(meta, prods, chunk, blk):
    owners = meta.shape[1]
    return pl.pallas_call(
        functools.partial(slots_kernel, chunk=chunk, blk=blk),
        in_specs=[
            pl.BlockSpec(memory_space=pltpu.SMEM),
            pl.BlockSpec(memory_space=pltpu.VMEM),
        ],
        out_specs=pl.BlockSpec(memory_space=pltpu.VMEM),
        out_shape=jax.ShapeDtypeStruct((owners, chunk, blk), BF),
        compiler_params=pltpu.CompilerParams(vmem_limit_bytes=12 * MIB),
        name="pick_slots",
    )(meta, prods)


def sum_core_kernel(own_ref, oth_ref, *out_refs):
    for s in range(NY):
        out_refs[s][...] = (own_ref[s].astype(F32) + oth_ref[s].astype(F32)).astype(out_refs[s].dtype)


def sum_y_kernel(*refs):
    parts, out_refs = refs[:NY], refs[NY:]
    for t in range(NX):
        out_refs[t][...] = sum(part[t].astype(F32) for part in parts)


def sum_x_kernel(*refs):
    parts, out_ref = refs[:NX], refs[NX]
    out_ref[...] = sum(part[...] for part in parts).astype(BF)


def small_call(kernel, name, outs, *args):
    return pl.pallas_call(
        kernel,
        in_specs=[pl.BlockSpec(memory_space=pltpu.VMEM)] * len(args),
        out_specs=[pl.BlockSpec(memory_space=pltpu.VMEM)] * len(outs),
        out_shape=outs,
        compiler_params=pltpu.CompilerParams(vmem_limit_bytes=12 * MIB),
        name=name,
    )(*args)


def sum_pair(in_own, in_oth):
    line = lambda dtype: jax.ShapeDtypeStruct(in_own.shape[1:], dtype)
    got = lax.ppermute(in_oth, "col", CORE_SWAP)
    return small_call(sum_core_kernel, "sum_core", [line(F32)] + [line(BF)] * (NY - 1), in_own, got)


def sum_plane(by_y):
    _, piece, toks = by_y[0].shape
    got = [by_y[0]] + [lax.ppermute(by_y[s], "col", Y_SHIFTS[s]) for s in range(1, NY)]
    by_x = small_call(sum_y_kernel, "sum_y", [jax.ShapeDtypeStruct((piece, toks), F32)] * NX, *got)
    got = [by_x[0]] + [lax.ppermute(by_x[t], "col", X_SHIFTS[t]) for t in range(1, NX)]
    return small_call(sum_x_kernel, "sum_x", [jax.ShapeDtypeStruct((piece, toks), BF)], *got)[0]


def tables_kernel(at, mask_ref, owner_ref, listed_ref, slots_ref):
    model_blocks = mask_ref.shape[0]
    count, owners = listed_ref.shape[1], slots_ref.shape[1]
    for s in range(owners):
        slots_ref[0, s] = 0
        slots_ref[1, s] = 0
        slots_ref[2, s] = 0

    def look(i, k):
        hid, mod = lax.div(i, model_blocks), lax.rem(i, model_blocks)
        full = mask_ref[mod, at[0] + hid]
        owner = owner_ref[mod, at[0] + hid]

        @pl.when(full == 1)
        def _():
            listed_ref[0, k] = owner
            listed_ref[1, k] = hid
            listed_ref[2, k] = mod
            slots_ref[0, owner] = hid
            slots_ref[1, owner] = mod
            slots_ref[2, owner] = 1

        return k + full

    lax.fori_loop(0, count * 4, look, 0)


def layout_tables(block_mask, block_owner, group, n_groups, owners):
    hidden_blocks, model_blocks = block_mask.shape
    per_group = hidden_blocks // n_groups
    smem = pl.BlockSpec(memory_space=pltpu.SMEM)
    return pl.pallas_call(
        tables_kernel,
        in_specs=[smem] * 3,
        out_specs=[smem] * 2,
        out_shape=[
            jax.ShapeDtypeStruct((3, per_group * model_blocks // 4), jnp.int32),
            jax.ShapeDtypeStruct((3, owners), jnp.int32),
        ],
        name="layout_tables",
    )((group * per_group).reshape(1).astype(jnp.int32), block_mask.T, block_owner.T)


def spread_kernel(in_ref, out_ref, sems):
    copies = [pltpu.make_async_copy(in_ref, out_ref.at[i], sems.at[i]) for i in range(out_ref.shape[0])]
    for copy in copies:
        copy.start()
    for copy in copies:
        copy.wait()


def spread(x, n):
    return pl.pallas_call(
        spread_kernel,
        in_specs=[pl.BlockSpec(memory_space=pltpu.VMEM)],
        out_specs=pl.BlockSpec(memory_space=pltpu.HBM),
        out_shape=pltpu.HBM((n, *x.shape), x.dtype),
        scratch_shapes=[pltpu.SemaphoreType.DMA((n,))],
        compiler_params=pltpu.CompilerParams(vmem_limit_bytes=4 * MIB),
        name="spread",
    )(x)


def share_y(x):
    half = x.shape[0] // 2
    before = lax.ppermute(x, "col", Y_SHIFTS[1])
    after = lax.ppermute(x, "col", Y_SHIFTS[NY - 1])
    far_lo = lax.ppermute(before[:half], "col", Y_SHIFTS[1])
    far_hi = lax.ppermute(after[half:], "col", Y_SHIFTS[NY - 1])
    return x, before, far_lo, far_hi, after


def per_device(activations, out_grad, weight_slots, block_mask, block_owner):
    blk = weight_slots.shape[2]
    owners, groups = lax.axis_size("row"), lax.axis_size("col")
    group = lax.axis_index("col")
    toks, piece = activations.shape
    hidden = out_grad.shape[1]
    chunk = blk // owners
    rows = hidden // owners
    listed, slots = layout_tables(block_mask, block_owner, group, groups, owners)
    place = jnp.stack([group // (NY * NC), group // NC % NY, group % NC]).astype(jnp.int32)

    w_all = lax.all_gather(weight_slots[0, 0], "row", axis=0)
    act_t = activations.T
    act_all = lax.all_to_all(spread(act_t, groups), "col", 0, 0, tiled=True).reshape(groups * piece, toks)
    act_z = lax.all_gather(act_t, "row", axis=0)

    grad_send = out_grad.T.reshape(-1, owners, chunk, toks).transpose(1, 0, 2, 3)
    grad_send = grad_send.reshape(owners, rows, toks)
    grad_send, act_z, act_all = lax.optimization_barrier((grad_send, act_z, act_all))
    grad_z = lax.all_to_all(grad_send, "row", 0, 0, tiled=True)
    here, before, far_lo, far_hi, after = share_y(act_z)
    grad_z, far_lo, far_hi, listed, slots = lax.optimization_barrier((grad_z, far_lo, far_hi, listed, slots))
    act_own = here, before, far_lo, far_hi, after
    act_oth = [lax.ppermute(a, "col", CORE_SWAP) for a in act_own]
    grad_x = lax.all_to_all(spread(grad_z, NX), "col", 0, 0, tiled=True, axis_index_groups=X_GROUPS)

    feats = line_features(place, act_own, act_oth)
    prods = wgrad_products(grad_x, feats, 1.0 / math.sqrt(toks * owners))
    prods = lax.all_to_all(prods, "col", 0, 0, tiled=True, axis_index_groups=X_GROUPS)
    slot_parts = pick_slots(slots, prods, chunk, blk)

    outputs, in_own, in_oth = tokens_step(listed, place, act_all, out_grad, w_all)
    by_y = sum_pair(in_own, in_oth)
    slot_parts, by_y = lax.optimization_barrier((slot_parts, by_y))
    weight_grad = lax.all_to_all(slot_parts, "row", 0, 0, tiled=True).reshape(1, 1, blk, blk)
    return outputs, sum_plane(by_y).T, weight_grad


def solution(mesh):
    placed = (P("row", "col"), P("row", "col"), P("col", "row", None, None), P(), P())
    return jax.shard_map(
        per_device,
        mesh=mesh,
        in_specs=placed,
        out_specs=(P("row", "col"), P("row", "col"), P("col", "row", None, None)),
        check_vma=False,
    )
```

```python
import functools
import math

import jax
import jax.numpy as jnp
from jax import lax
from jax.experimental import pallas as pl
from jax.experimental.pallas import tpu as pltpu
from jax.sharding import PartitionSpec as P

BF = jnp.bfloat16
F32 = jnp.float32
NX, NY, NC = 4, 4, 2
MIB = 1024 * 1024


def col_of(x, y, c):
    return (x * NY + y) * NC + c


PLANE = [(x, y, c) for x in range(NX) for y in range(NY) for c in range(NC)]
X_GROUPS = [[col_of(x, y, c) for x in range(NX)] for y in range(NY) for c in range(NC)]
CORE_SWAP = [(col_of(x, y, c), col_of(x, y, 1 - c)) for x, y, c in PLANE]
X_SHIFTS = {s: [(col_of(x, y, c), col_of((x + s) % NX, y, c)) for x, y, c in PLANE] for s in range(1, NX)}
Y_SHIFTS = {s: [(col_of(x, y, c), col_of(x, (y + s) % NY, c)) for x, y, c in PLANE] for s in range(1, NY)}


def aligned(start, size, step):
    return pl.ds(pl.multiple_of(start, step), size)


def tokens_kernel(meta, place, act_ref, grad_ref, w_ref, out_ref, in_own, in_oth, w_buf, out_acc, in_acc, in_rows, sems):
    count, blk, _ = w_buf.shape
    piece = in_own.shape[2]
    x, y, core = place[0], place[1], place[2]
    copies = [pltpu.make_async_copy(w_ref.at[meta[0, k]], w_buf.at[k], sems.at[k]) for k in range(count)]
    for copy in copies:
        copy.start()
    out_acc[...] = jnp.zeros_like(out_acc)
    in_acc[...] = jnp.zeros_like(in_acc)
    for k in range(count):
        hid = aligned(meta[1, k] * blk, blk, blk)
        mod = aligned(meta[2, k] * blk, blk, blk)
        copies[k].wait()
        w = w_buf[k]
        out_acc[hid, :] += jnp.dot(w, act_ref[mod, :], preferred_element_type=F32)
        in_acc[:, mod] += jnp.dot(grad_ref[:, hid], w, preferred_element_type=F32)
    out_ref[...] = out_acc[...].T.astype(BF)
    in_rows[...] = in_acc[...].T.astype(BF)
    for s in range(NY):
        for t in range(NX):
            chip = (lax.rem(x + t, NX) * NY + lax.rem(y + s, NY)) * NC
            in_own[s, t] = in_rows[aligned((chip + core) * piece, piece, 64), :]
            in_oth[s, t] = in_rows[aligned((chip + 1 - core) * piece, piece, 64), :]


def tokens_step(meta, place, act, grad, w_all):
    count, blk = meta.shape[1], w_all.shape[1]
    feats, toks = act.shape
    hidden = grad.shape[1]
    parts = pltpu.HBM((NY, NX, feats // (NX * NY * NC), toks), BF)
    vmem = pl.BlockSpec(memory_space=pltpu.VMEM)
    smem = pl.BlockSpec(memory_space=pltpu.SMEM)
    return pl.pallas_call(
        tokens_kernel,
        in_specs=[smem, smem, vmem, vmem, pl.BlockSpec(memory_space=pltpu.HBM)],
        out_specs=[vmem] * 3,
        out_shape=[jax.ShapeDtypeStruct((toks, hidden), BF), parts, parts],
        scratch_shapes=[
            pltpu.VMEM((count, blk, blk), BF),
            pltpu.VMEM((hidden, toks), F32),
            pltpu.VMEM((toks, feats), F32),
            pltpu.VMEM((feats, toks), BF),
            pltpu.SemaphoreType.DMA((count,)),
        ],
        compiler_params=pltpu.CompilerParams(vmem_limit_bytes=28 * MIB),
        name="tokens_step",
    )(meta, place, act, grad, in_hbm(w_all))


def in_hbm(x):
    return pltpu.with_memory_space_constraint(x, pltpu.HBM)


def wgrad_kernel(place, grad_ref, *refs, scale):
    act_refs, (out_ref, a_buf, b_buf, sems) = refs[:-4], refs[-4:]
    n_x, n_z, rows, toks = grad_ref.shape
    piece = act_refs[0].shape[1]
    y, core = place[1], place[2]
    parts = ((0, 0), (1, 0), (2, 0), (2, n_z // 2), (3, 0))
    copies = [[] for _ in range(NY)]
    count = 0
    for i, (s, first) in enumerate(parts):
        for side, ref in ((core, act_refs[i]), (1 - core, act_refs[i + len(parts)])):
            at = aligned((s * NC + side) * piece, piece, 64)
            for z in range(ref.shape[0]):
                lanes = pl.ds((first + z) * toks, toks)
                copies[s].append(pltpu.make_async_copy(ref.at[z], b_buf.at[at, lanes], sems.at[count]))
                count += 1
    for line in copies:
        for copy in line:
            copy.start()
    for x in range(n_x):
        for z in range(n_z):
            a_buf[x * rows : (x + 1) * rows, z * toks : (z + 1) * toks] = grad_ref[x, z]
    span = NC * piece
    for s in range(0, NY, 2):
        for copy in copies[s] + copies[s + 1]:
            copy.wait()
        prod = lax.dot_general(
            a_buf[...], b_buf[s * span : (s + 2) * span], (((1,), (1,)), ((), ())), preferred_element_type=F32
        )
        prod = (prod * scale).astype(BF)
        for i in range(2):
            cols = aligned(lax.rem(y - s - i + NY, NY) * span, span, span)
            for x in range(n_x):
                out_ref[x, :, cols] = prod[x * rows : (x + 1) * rows, i * span : (i + 1) * span]


def wgrad_products(place, grads, own, oth, scale):
    n_x, n_z, rows, toks = grads.shape
    feats = NY * NC * own[0].shape[1]
    args = [in_hbm(a) for a in (*own, *oth)]
    vmem = pl.BlockSpec(memory_space=pltpu.VMEM)
    return pl.pallas_call(
        functools.partial(wgrad_kernel, scale=scale),
        in_specs=[pl.BlockSpec(memory_space=pltpu.SMEM), vmem]
        + [pl.BlockSpec(memory_space=pltpu.HBM)] * len(args),
        out_specs=vmem,
        out_shape=pltpu.HBM((n_x, rows, feats), BF),
        scratch_shapes=[
            pltpu.VMEM((n_x * rows, n_z * toks), BF),
            pltpu.VMEM((feats, n_z * toks), BF),
            pltpu.SemaphoreType.DMA((NY * NC * n_z,)),
        ],
        compiler_params=pltpu.CompilerParams(vmem_limit_bytes=20 * MIB),
        name="wgrad_products",
    )(place, grads, *args)


def slots_kernel(meta, prod_ref, out_ref, *, chunk, blk):
    per_x = prod_ref.shape[2] // blk
    for s in range(out_ref.shape[0]):
        hid, mod, full = meta[0, s], meta[1, s], meta[2, s]
        rows = aligned(hid * chunk, chunk, chunk)
        cols = aligned(lax.rem(mod, per_x) * blk, blk, blk)
        part = prod_ref[lax.div(mod, per_x), rows, cols]
        out_ref[s] = jnp.where(full > 0, part, jnp.zeros_like(part))


def pick_slots(meta, prods, chunk, blk):
    owners = meta.shape[1]
    return pl.pallas_call(
        functools.partial(slots_kernel, chunk=chunk, blk=blk),
        in_specs=[
            pl.BlockSpec(memory_space=pltpu.SMEM),
            pl.BlockSpec(memory_space=pltpu.VMEM),
        ],
        out_specs=pl.BlockSpec(memory_space=pltpu.VMEM),
        out_shape=jax.ShapeDtypeStruct((owners, chunk, blk), BF),
        compiler_params=pltpu.CompilerParams(vmem_limit_bytes=12 * MIB),
        name="pick_slots",
    )(meta, prods)


def sum_core_kernel(own_ref, oth_ref, *out_refs):
    for s in range(NY):
        out_refs[s][...] = (own_ref[s].astype(F32) + oth_ref[s].astype(F32)).astype(out_refs[s].dtype)


def sum_y_kernel(*refs):
    parts, out_refs = refs[:NY], refs[NY:]
    for t in range(NX):
        out_refs[t][...] = sum(part[t].astype(F32) for part in parts)


def sum_x_kernel(*refs):
    parts, out_ref = refs[:NX], refs[NX]
    out_ref[...] = sum(part[...] for part in parts).astype(BF)


def small_call(kernel, name, outs, *args):
    return pl.pallas_call(
        kernel,
        in_specs=[pl.BlockSpec(memory_space=pltpu.VMEM)] * len(args),
        out_specs=[pl.BlockSpec(memory_space=pltpu.VMEM)] * len(outs),
        out_shape=outs,
        compiler_params=pltpu.CompilerParams(vmem_limit_bytes=12 * MIB),
        name=name,
    )(*args)


def sum_pair(in_own, in_oth):
    line = lambda dtype: jax.ShapeDtypeStruct(in_own.shape[1:], dtype)
    got = lax.ppermute(in_oth, "col", CORE_SWAP)
    return small_call(sum_core_kernel, "sum_core", [line(F32)] + [line(BF)] * (NY - 1), in_own, got)


def sum_plane(by_y):
    _, piece, toks = by_y[0].shape
    got = [by_y[0]] + [lax.ppermute(by_y[s], "col", Y_SHIFTS[s]) for s in range(1, NY)]
    by_x = small_call(sum_y_kernel, "sum_y", [jax.ShapeDtypeStruct((piece, toks), F32)] * NX, *got)
    got = [by_x[0]] + [lax.ppermute(by_x[t], "col", X_SHIFTS[t]) for t in range(1, NX)]
    return small_call(sum_x_kernel, "sum_x", [jax.ShapeDtypeStruct((piece, toks), BF)], *got)[0]


def tables_kernel(at, mask_ref, owner_ref, listed_ref, slots_ref):
    model_blocks = mask_ref.shape[0]
    count, owners = listed_ref.shape[1], slots_ref.shape[1]
    for s in range(owners):
        slots_ref[0, s] = 0
        slots_ref[1, s] = 0
        slots_ref[2, s] = 0

    def look(i, k):
        hid, mod = lax.div(i, model_blocks), lax.rem(i, model_blocks)
        full = mask_ref[mod, at[0] + hid]
        owner = owner_ref[mod, at[0] + hid]

        @pl.when(full == 1)
        def _():
            listed_ref[0, k] = owner
            listed_ref[1, k] = hid
            listed_ref[2, k] = mod
            slots_ref[0, owner] = hid
            slots_ref[1, owner] = mod
            slots_ref[2, owner] = 1

        return k + full

    lax.fori_loop(0, count * 4, look, 0)


def layout_tables(block_mask, block_owner, group, n_groups, owners):
    hidden_blocks, model_blocks = block_mask.shape
    per_group = hidden_blocks // n_groups
    smem = pl.BlockSpec(memory_space=pltpu.SMEM)
    return pl.pallas_call(
        tables_kernel,
        in_specs=[smem] * 3,
        out_specs=[smem] * 2,
        out_shape=[
            jax.ShapeDtypeStruct((3, per_group * model_blocks // 4), jnp.int32),
            jax.ShapeDtypeStruct((3, owners), jnp.int32),
        ],
        name="layout_tables",
    )((group * per_group).reshape(1).astype(jnp.int32), block_mask.T, block_owner.T)


def spread_kernel(in_ref, out_ref, sems):
    copies = [pltpu.make_async_copy(in_ref, out_ref.at[i], sems.at[i]) for i in range(out_ref.shape[0])]
    for copy in copies:
        copy.start()
    for copy in copies:
        copy.wait()


def spread(x, n):
    return pl.pallas_call(
        spread_kernel,
        in_specs=[pl.BlockSpec(memory_space=pltpu.VMEM)],
        out_specs=pl.BlockSpec(memory_space=pltpu.HBM),
        out_shape=pltpu.HBM((n, *x.shape), x.dtype),
        scratch_shapes=[pltpu.SemaphoreType.DMA((n,))],
        compiler_params=pltpu.CompilerParams(vmem_limit_bytes=4 * MIB),
        name="spread",
    )(x)


def share_y(x):
    half = x.shape[0] // 2
    before = lax.ppermute(x, "col", Y_SHIFTS[1])
    after = lax.ppermute(x, "col", Y_SHIFTS[NY - 1])
    far_lo = lax.ppermute(before[:half], "col", Y_SHIFTS[1])
    far_hi = lax.ppermute(after[half:], "col", Y_SHIFTS[NY - 1])
    return x, before, far_lo, far_hi, after


def per_device(activations, out_grad, weight_slots, block_mask, block_owner):
    blk = weight_slots.shape[2]
    owners, groups = lax.axis_size("row"), lax.axis_size("col")
    group = lax.axis_index("col")
    toks, piece = activations.shape
    hidden = out_grad.shape[1]
    chunk = blk // owners
    rows = hidden // owners
    listed, slots = layout_tables(block_mask, block_owner, group, groups, owners)
    place = jnp.stack([group // (NY * NC), group // NC % NY, group % NC]).astype(jnp.int32)

    w_all = lax.all_gather(weight_slots[0, 0], "row", axis=0)
    act_t = activations.T
    act_all = lax.all_to_all(spread(act_t, groups), "col", 0, 0, tiled=True).reshape(groups * piece, toks)
    act_z = lax.all_gather(act_t, "row", axis=0)

    grad_send = out_grad.T.reshape(-1, owners, chunk, toks).transpose(1, 0, 2, 3)
    grad_send = grad_send.reshape(owners, rows, toks)
    grad_send, act_z, act_all = lax.optimization_barrier((grad_send, act_z, act_all))
    grad_z = lax.all_to_all(grad_send, "row", 0, 0, tiled=True)
    here, before, far_lo, far_hi, after = share_y(act_z)
    grad_z, far_lo, far_hi, listed, slots = lax.optimization_barrier((grad_z, far_lo, far_hi, listed, slots))
    act_own = here, before, far_lo, far_hi, after
    act_oth = [lax.ppermute(a, "col", CORE_SWAP) for a in act_own]
    grad_x = lax.all_to_all(spread(grad_z, NX), "col", 0, 0, tiled=True, axis_index_groups=X_GROUPS)

    prods = wgrad_products(place, grad_x, act_own, act_oth, 1.0 / math.sqrt(toks * owners))
    prods = lax.all_to_all(prods, "col", 0, 0, tiled=True, axis_index_groups=X_GROUPS)
    slot_parts = pick_slots(slots, prods, chunk, blk)

    outputs, in_own, in_oth = tokens_step(listed, place, act_all, out_grad, w_all)
    by_y = sum_pair(in_own, in_oth)
    slot_parts, by_y = lax.optimization_barrier((slot_parts, by_y))
    weight_grad = lax.all_to_all(slot_parts, "row", 0, 0, tiled=True).reshape(1, 1, blk, blk)
    return outputs, sum_plane(by_y).T, weight_grad


def solution(mesh):
    placed = (P("row", "col"), P("row", "col"), P("col", "row", None, None), P(), P())
    return jax.shard_map(
        per_device,
        mesh=mesh,
        in_specs=placed,
        out_specs=(P("row", "col"), P("row", "col"), P("col", "row", None, None)),
        check_vma=False,
    )
```

```python
import functools
import math

import jax
import jax.numpy as jnp
from jax import lax
from jax.experimental import pallas as pl
from jax.experimental.pallas import tpu as pltpu
from jax.sharding import PartitionSpec as P

BF = jnp.bfloat16
F32 = jnp.float32
NX, NY, NC = 4, 4, 2
MIB = 1024 * 1024


def col_of(x, y, c):
    return (x * NY + y) * NC + c


PLANE = [(x, y, c) for x in range(NX) for y in range(NY) for c in range(NC)]
X_GROUPS = [[col_of(x, y, c) for x in range(NX)] for y in range(NY) for c in range(NC)]
CORE_SWAP = [(col_of(x, y, c), col_of(x, y, 1 - c)) for x, y, c in PLANE]
X_SHIFTS = {s: [(col_of(x, y, c), col_of((x + s) % NX, y, c)) for x, y, c in PLANE] for s in range(1, NX)}
Y_SHIFTS = {s: [(col_of(x, y, c), col_of(x, (y + s) % NY, c)) for x, y, c in PLANE] for s in range(1, NY)}


def aligned(start, size, step):
    return pl.ds(pl.multiple_of(start, step), size)


def slot_copies(meta, w_ref, w_buf, sems):
    copies = [
        pltpu.make_async_copy(w_ref.at[meta[0, k]], w_buf.at[k], sems.at[k]) for k in range(w_buf.shape[0])
    ]
    for copy in copies:
        copy.start()
    return copies


def in_kernel(meta, place, grad_ref, w_ref, in_own, in_oth, w_buf, in_acc, in_rows, sems):
    count, blk, _ = w_buf.shape
    piece = in_own.shape[2]
    x, y, core = place[0], place[1], place[2]
    copies = slot_copies(meta, w_ref, w_buf, sems)
    in_acc[...] = jnp.zeros_like(in_acc)
    for k in range(count):
        hid = aligned(meta[1, k] * blk, blk, blk)
        mod = aligned(meta[2, k] * blk, blk, blk)
        copies[k].wait()
        in_acc[:, mod] += jnp.dot(grad_ref[:, hid], w_buf[k], preferred_element_type=F32)
    in_rows[...] = in_acc[...].T.astype(BF)
    for s in range(NY):
        for t in range(NX):
            chip = (lax.rem(x + t, NX) * NY + lax.rem(y + s, NY)) * NC
            in_own[s, t] = in_rows[aligned((chip + core) * piece, piece, 64), :]
            in_oth[s, t] = in_rows[aligned((chip + 1 - core) * piece, piece, 64), :]


def in_step(meta, place, grad, w_all, feats):
    count, blk = meta.shape[1], w_all.shape[1]
    toks = grad.shape[0]
    parts = pltpu.HBM((NY, NX, feats // (NX * NY * NC), toks), BF)
    vmem = pl.BlockSpec(memory_space=pltpu.VMEM)
    smem = pl.BlockSpec(memory_space=pltpu.SMEM)
    return pl.pallas_call(
        in_kernel,
        in_specs=[smem, smem, vmem, pl.BlockSpec(memory_space=pltpu.HBM)],
        out_specs=[vmem] * 2,
        out_shape=[parts, parts],
        scratch_shapes=[
            pltpu.VMEM((count, blk, blk), BF),
            pltpu.VMEM((toks, feats), F32),
            pltpu.VMEM((feats, toks), BF),
            pltpu.SemaphoreType.DMA((count,)),
        ],
        compiler_params=pltpu.CompilerParams(vmem_limit_bytes=24 * MIB),
        name="in_step",
    )(meta, place, grad, in_hbm(w_all))


def out_kernel(meta, act_ref, w_ref, out_ref, w_buf, out_acc, sems):
    count, blk, _ = w_buf.shape
    copies = slot_copies(meta, w_ref, w_buf, sems)
    out_acc[...] = jnp.zeros_like(out_acc)
    for k in range(count):
        hid = aligned(meta[1, k] * blk, blk, blk)
        mod = aligned(meta[2, k] * blk, blk, blk)
        copies[k].wait()
        out_acc[hid, :] += jnp.dot(w_buf[k], act_ref[mod, :], preferred_element_type=F32)
    out_ref[...] = out_acc[...].T.astype(BF)


def out_step(meta, act, w_all, hidden):
    count, blk = meta.shape[1], w_all.shape[1]
    toks = act.shape[1]
    vmem = pl.BlockSpec(memory_space=pltpu.VMEM)
    return pl.pallas_call(
        out_kernel,
        in_specs=[pl.BlockSpec(memory_space=pltpu.SMEM), vmem, pl.BlockSpec(memory_space=pltpu.HBM)],
        out_specs=vmem,
        out_shape=jax.ShapeDtypeStruct((toks, hidden), BF),
        scratch_shapes=[
            pltpu.VMEM((count, blk, blk), BF),
            pltpu.VMEM((hidden, toks), F32),
            pltpu.SemaphoreType.DMA((count,)),
        ],
        compiler_params=pltpu.CompilerParams(vmem_limit_bytes=16 * MIB),
        name="out_step",
    )(meta, act, in_hbm(w_all))


def in_hbm(x):
    return pltpu.with_memory_space_constraint(x, pltpu.HBM)


def wgrad_kernel(place, grad_ref, *refs, scale):
    act_refs, (out_ref, a_buf, b_buf, sems) = refs[:-4], refs[-4:]
    n_x, n_z, rows, toks = grad_ref.shape
    piece = act_refs[0].shape[1]
    y, core = place[1], place[2]
    parts = ((0, 0), (1, 0), (2, 0), (2, n_z // 2), (3, 0))
    copies = [[] for _ in range(NY)]
    count = 0
    for i, (s, first) in enumerate(parts):
        for side, ref in ((core, act_refs[i]), (1 - core, act_refs[i + len(parts)])):
            at = aligned((s * NC + side) * piece, piece, 64)
            for z in range(ref.shape[0]):
                lanes = pl.ds((first + z) * toks, toks)
                copies[s].append(pltpu.make_async_copy(ref.at[z], b_buf.at[at, lanes], sems.at[count]))
                count += 1
    for line in copies:
        for copy in line:
            copy.start()
    for x in range(n_x):
        for z in range(n_z):
            a_buf[x * rows : (x + 1) * rows, z * toks : (z + 1) * toks] = grad_ref[x, z]
    span = NC * piece
    for s in range(0, NY, 2):
        for copy in copies[s] + copies[s + 1]:
            copy.wait()
        prod = lax.dot_general(
            a_buf[...], b_buf[s * span : (s + 2) * span], (((1,), (1,)), ((), ())), preferred_element_type=F32
        )
        prod = (prod * scale).astype(BF)
        for i in range(2):
            cols = aligned(lax.rem(y - s - i + NY, NY) * span, span, span)
            for x in range(n_x):
                out_ref[x, :, cols] = prod[x * rows : (x + 1) * rows, i * span : (i + 1) * span]


def wgrad_products(place, grads, own, oth, scale):
    n_x, n_z, rows, toks = grads.shape
    feats = NY * NC * own[0].shape[1]
    args = [in_hbm(a) for a in (*own, *oth)]
    vmem = pl.BlockSpec(memory_space=pltpu.VMEM)
    return pl.pallas_call(
        functools.partial(wgrad_kernel, scale=scale),
        in_specs=[pl.BlockSpec(memory_space=pltpu.SMEM), vmem]
        + [pl.BlockSpec(memory_space=pltpu.HBM)] * len(args),
        out_specs=vmem,
        out_shape=pltpu.HBM((n_x, rows, feats), BF),
        scratch_shapes=[
            pltpu.VMEM((n_x * rows, n_z * toks), BF),
            pltpu.VMEM((feats, n_z * toks), BF),
            pltpu.SemaphoreType.DMA((NY * NC * n_z,)),
        ],
        compiler_params=pltpu.CompilerParams(vmem_limit_bytes=20 * MIB),
        name="wgrad_products",
    )(place, grads, *args)


def slots_kernel(meta, prod_ref, out_ref, *, chunk, blk):
    per_x = prod_ref.shape[2] // blk
    for s in range(out_ref.shape[0]):
        hid, mod, full = meta[0, s], meta[1, s], meta[2, s]
        rows = aligned(hid * chunk, chunk, chunk)
        cols = aligned(lax.rem(mod, per_x) * blk, blk, blk)
        part = prod_ref[lax.div(mod, per_x), rows, cols]
        out_ref[s] = jnp.where(full > 0, part, jnp.zeros_like(part))


def pick_slots(meta, prods, chunk, blk):
    owners = meta.shape[1]
    return pl.pallas_call(
        functools.partial(slots_kernel, chunk=chunk, blk=blk),
        in_specs=[
            pl.BlockSpec(memory_space=pltpu.SMEM),
            pl.BlockSpec(memory_space=pltpu.VMEM),
        ],
        out_specs=pl.BlockSpec(memory_space=pltpu.VMEM),
        out_shape=jax.ShapeDtypeStruct((owners, chunk, blk), BF),
        compiler_params=pltpu.CompilerParams(vmem_limit_bytes=12 * MIB),
        name="pick_slots",
    )(meta, prods)


def sum_core_kernel(own_ref, oth_ref, *out_refs):
    for s in range(NY):
        out_refs[s][...] = (own_ref[s].astype(F32) + oth_ref[s].astype(F32)).astype(out_refs[s].dtype)


def sum_y_kernel(*refs):
    parts, out_refs = refs[:NY], refs[NY:]
    for t in range(NX):
        out_refs[t][...] = sum(part[t].astype(F32) for part in parts)


def sum_x_kernel(*refs):
    parts, out_ref = refs[:NX], refs[NX]
    out_ref[...] = sum(part[...] for part in parts).astype(BF)


def small_call(kernel, name, outs, *args):
    return pl.pallas_call(
        kernel,
        in_specs=[pl.BlockSpec(memory_space=pltpu.VMEM)] * len(args),
        out_specs=[pl.BlockSpec(memory_space=pltpu.VMEM)] * len(outs),
        out_shape=outs,
        compiler_params=pltpu.CompilerParams(vmem_limit_bytes=12 * MIB),
        name=name,
    )(*args)


def sum_pair(in_own, in_oth):
    line = lambda dtype: jax.ShapeDtypeStruct(in_own.shape[1:], dtype)
    got = lax.ppermute(in_oth, "col", CORE_SWAP)
    return small_call(sum_core_kernel, "sum_core", [line(F32)] + [line(BF)] * (NY - 1), in_own, got)


def sum_line(by_y):
    _, piece, toks = by_y[0].shape
    got = [by_y[0]] + [lax.ppermute(by_y[s], "col", Y_SHIFTS[s]) for s in range(1, NY)]
    return small_call(sum_y_kernel, "sum_y", [jax.ShapeDtypeStruct((piece, toks), F32)] * NX, *got)


def sum_plane(by_x):
    got = [by_x[0]] + [lax.ppermute(by_x[t], "col", X_SHIFTS[t]) for t in range(1, NX)]
    return small_call(sum_x_kernel, "sum_x", [jax.ShapeDtypeStruct(by_x[0].shape, BF)], *got)[0]


def tables_kernel(at, mask_ref, owner_ref, listed_ref, slots_ref):
    model_blocks = mask_ref.shape[0]
    count, owners = listed_ref.shape[1], slots_ref.shape[1]
    for s in range(owners):
        slots_ref[0, s] = 0
        slots_ref[1, s] = 0
        slots_ref[2, s] = 0

    def look(i, k):
        hid, mod = lax.div(i, model_blocks), lax.rem(i, model_blocks)
        full = mask_ref[mod, at[0] + hid]
        owner = owner_ref[mod, at[0] + hid]

        @pl.when(full == 1)
        def _():
            listed_ref[0, k] = owner
            listed_ref[1, k] = hid
            listed_ref[2, k] = mod
            slots_ref[0, owner] = hid
            slots_ref[1, owner] = mod
            slots_ref[2, owner] = 1

        return k + full

    lax.fori_loop(0, count * 4, look, 0)


def layout_tables(block_mask, block_owner, group, n_groups, owners):
    hidden_blocks, model_blocks = block_mask.shape
    per_group = hidden_blocks // n_groups
    smem = pl.BlockSpec(memory_space=pltpu.SMEM)
    return pl.pallas_call(
        tables_kernel,
        in_specs=[smem] * 3,
        out_specs=[smem] * 2,
        out_shape=[
            jax.ShapeDtypeStruct((3, per_group * model_blocks // 4), jnp.int32),
            jax.ShapeDtypeStruct((3, owners), jnp.int32),
        ],
        name="layout_tables",
    )((group * per_group).reshape(1).astype(jnp.int32), block_mask.T, block_owner.T)


def spread_kernel(in_ref, out_ref, sems):
    copies = [pltpu.make_async_copy(in_ref, out_ref.at[i], sems.at[i]) for i in range(out_ref.shape[0])]
    for copy in copies:
        copy.start()
    for copy in copies:
        copy.wait()


def spread(x, n):
    return pl.pallas_call(
        spread_kernel,
        in_specs=[pl.BlockSpec(memory_space=pltpu.VMEM)],
        out_specs=pl.BlockSpec(memory_space=pltpu.HBM),
        out_shape=pltpu.HBM((n, *x.shape), x.dtype),
        scratch_shapes=[pltpu.SemaphoreType.DMA((n,))],
        compiler_params=pltpu.CompilerParams(vmem_limit_bytes=4 * MIB),
        name="spread",
    )(x)


def share_y(x):
    half = x.shape[0] // 2
    before = lax.ppermute(x, "col", Y_SHIFTS[1])
    after = lax.ppermute(x, "col", Y_SHIFTS[NY - 1])
    far_lo = lax.ppermute(before[:half], "col", Y_SHIFTS[1])
    far_hi = lax.ppermute(after[half:], "col", Y_SHIFTS[NY - 1])
    return x, before, far_lo, far_hi, after


def per_device(activations, out_grad, weight_slots, block_mask, block_owner):
    blk = weight_slots.shape[2]
    owners, groups = lax.axis_size("row"), lax.axis_size("col")
    group = lax.axis_index("col")
    toks, piece = activations.shape
    hidden = out_grad.shape[1]
    chunk = blk // owners
    rows = hidden // owners
    listed, slots = layout_tables(block_mask, block_owner, group, groups, owners)
    place = jnp.stack([group // (NY * NC), group // NC % NY, group % NC]).astype(jnp.int32)

    w_all = lax.all_gather(weight_slots[0, 0], "row", axis=0)
    act_t = activations.T
    act_all = lax.all_to_all(spread(act_t, groups), "col", 0, 0, tiled=True).reshape(groups * piece, toks)
    act_z = lax.all_gather(act_t, "row", axis=0)

    grad_send = out_grad.T.reshape(-1, owners, chunk, toks).transpose(1, 0, 2, 3)
    grad_send = grad_send.reshape(owners, rows, toks)
    grad_send, act_z, act_all = lax.optimization_barrier((grad_send, act_z, act_all))
    grad_z = lax.all_to_all(grad_send, "row", 0, 0, tiled=True)
    here, before, far_lo, far_hi, after = share_y(act_z)
    grad_z, far_lo, far_hi, listed, slots = lax.optimization_barrier((grad_z, far_lo, far_hi, listed, slots))
    act_own = here, before, far_lo, far_hi, after
    act_oth = [lax.ppermute(a, "col", CORE_SWAP) for a in act_own]
    grad_x = lax.all_to_all(spread(grad_z, NX), "col", 0, 0, tiled=True, axis_index_groups=X_GROUPS)

    prods = wgrad_products(place, grad_x, act_own, act_oth, 1.0 / math.sqrt(toks * owners))
    prods = lax.all_to_all(prods, "col", 0, 0, tiled=True, axis_index_groups=X_GROUPS)
    slot_parts = pick_slots(slots, prods, chunk, blk)

    in_own, in_oth = in_step(listed, place, out_grad, w_all, groups * piece)
    by_y = sum_pair(in_own, in_oth)
    slot_parts, by_y, act_all = lax.optimization_barrier((slot_parts, by_y, act_all))
    weight_grad = lax.all_to_all(slot_parts, "row", 0, 0, tiled=True).reshape(1, 1, blk, blk)
    by_x, outputs = lax.optimization_barrier((sum_line(by_y), out_step(listed, act_all, w_all, hidden)))
    return outputs, sum_plane(by_x).T, weight_grad


def solution(mesh):
    placed = (P("row", "col"), P("row", "col"), P("col", "row", None, None), P(), P())
    return jax.shard_map(
        per_device,
        mesh=mesh,
        in_specs=placed,
        out_specs=(P("row", "col"), P("row", "col"), P("col", "row", None, None)),
        check_vma=False,
    )
```

```python
import functools
import math

import jax
import jax.numpy as jnp
from jax import lax
from jax.experimental import pallas as pl
from jax.experimental.pallas import tpu as pltpu
from jax.sharding import PartitionSpec as P

BF = jnp.bfloat16
F32 = jnp.float32
NX, NY, NC = 4, 4, 2
MIB = 1024 * 1024


def col_of(x, y, c):
    return (x * NY + y) * NC + c


PLANE = [(x, y, c) for x in range(NX) for y in range(NY) for c in range(NC)]
X_GROUPS = [[col_of(x, y, c) for x in range(NX)] for y in range(NY) for c in range(NC)]
CORE_SWAP = [(col_of(x, y, c), col_of(x, y, 1 - c)) for x, y, c in PLANE]
X_SHIFTS = {s: [(col_of(x, y, c), col_of((x + s) % NX, y, c)) for x, y, c in PLANE] for s in range(1, NX)}
Y_SHIFTS = {s: [(col_of(x, y, c), col_of(x, (y + s) % NY, c)) for x, y, c in PLANE] for s in range(1, NY)}


def aligned(start, size, step):
    return pl.ds(pl.multiple_of(start, step), size)


def slot_copies(meta, w_ref, w_buf, sems):
    copies = [
        pltpu.make_async_copy(w_ref.at[meta[0, k]], w_buf.at[k], sems.at[k]) for k in range(w_buf.shape[0])
    ]
    for copy in copies:
        copy.start()
    return copies


def in_kernel(meta, place, grad_ref, w_ref, in_own, in_oth, w_buf, in_acc, in_rows, sems):
    count, blk, _ = w_buf.shape
    piece = in_own.shape[2]
    x, y, core = place[0], place[1], place[2]
    copies = slot_copies(meta, w_ref, w_buf, sems)
    in_acc[...] = jnp.zeros_like(in_acc)
    for k in range(count):
        hid = aligned(meta[1, k] * blk, blk, blk)
        mod = aligned(meta[2, k] * blk, blk, blk)
        copies[k].wait()
        in_acc[:, mod] += jnp.dot(grad_ref[:, hid], w_buf[k], preferred_element_type=F32)
    in_rows[...] = in_acc[...].T.astype(BF)
    for s in range(NY):
        for t in range(NX):
            chip = (lax.rem(x + t, NX) * NY + lax.rem(y + s, NY)) * NC
            in_own[s, t] = in_rows[aligned((chip + core) * piece, piece, 64), :]
            in_oth[s, t] = in_rows[aligned((chip + 1 - core) * piece, piece, 64), :]


def in_step(meta, place, grad, w_all, feats):
    count, blk = meta.shape[1], w_all.shape[1]
    toks = grad.shape[0]
    parts = pltpu.HBM((NY, NX, feats // (NX * NY * NC), toks), BF)
    vmem = pl.BlockSpec(memory_space=pltpu.VMEM)
    smem = pl.BlockSpec(memory_space=pltpu.SMEM)
    return pl.pallas_call(
        in_kernel,
        in_specs=[smem, smem, vmem, pl.BlockSpec(memory_space=pltpu.HBM)],
        out_specs=[vmem] * 2,
        out_shape=[parts, parts],
        scratch_shapes=[
            pltpu.VMEM((count, blk, blk), BF),
            pltpu.VMEM((toks, feats), F32),
            pltpu.VMEM((feats, toks), BF),
            pltpu.SemaphoreType.DMA((count,)),
        ],
        compiler_params=pltpu.CompilerParams(vmem_limit_bytes=24 * MIB),
        name="in_step",
    )(meta, place, grad, in_hbm(w_all))


def out_kernel(meta, act_ref, w_ref, out_ref, w_buf, out_acc, sems):
    count, blk, _ = w_buf.shape
    copies = slot_copies(meta, w_ref, w_buf, sems)
    out_acc[...] = jnp.zeros_like(out_acc)
    for k in range(count):
        hid = aligned(meta[1, k] * blk, blk, blk)
        mod = aligned(meta[2, k] * blk, blk, blk)
        copies[k].wait()
        out_acc[hid, :] += jnp.dot(w_buf[k], act_ref[mod, :], preferred_element_type=F32)
    out_ref[...] = out_acc[...].T.astype(BF)


def out_step(meta, act, w_all, hidden):
    count, blk = meta.shape[1], w_all.shape[1]
    toks = act.shape[1]
    vmem = pl.BlockSpec(memory_space=pltpu.VMEM)
    return pl.pallas_call(
        out_kernel,
        in_specs=[pl.BlockSpec(memory_space=pltpu.SMEM), vmem, pl.BlockSpec(memory_space=pltpu.HBM)],
        out_specs=vmem,
        out_shape=jax.ShapeDtypeStruct((toks, hidden), BF),
        scratch_shapes=[
            pltpu.VMEM((count, blk, blk), BF),
            pltpu.VMEM((hidden, toks), F32),
            pltpu.SemaphoreType.DMA((count,)),
        ],
        compiler_params=pltpu.CompilerParams(vmem_limit_bytes=16 * MIB),
        name="out_step",
    )(meta, act, in_hbm(w_all))


def in_hbm(x):
    return pltpu.with_memory_space_constraint(x, pltpu.HBM)


def wgrad_kernel(place, grad_ref, *refs, scale):
    n_in = (len(refs) - 4) // 2
    act_refs, out_ref, buffers, (a_buf, b_buf, sems) = refs[:n_in], refs[n_in], refs[n_in + 1 : -3], refs[-3:]
    n_x, n_z, rows, toks = grad_ref.shape
    piece = act_refs[0].shape[1]
    span = NC * piece
    y, core = place[1], place[2]
    near = ((0, 0, 0), (1, 1, 0)), ((2, 2, 0), (3, 2, n_z // 2), (4, 3, 0))
    half = n_in // 2
    copies = [pltpu.make_async_copy(act_refs[i], buffers[i], sems.at[i]) for i in range(n_in)]
    for parts in near:
        for i, _, _ in parts:
            copies[i].start()
            copies[i + half].start()
    for x in range(n_x):
        for z in range(n_z):
            a_buf[x * rows : (x + 1) * rows, z * toks : (z + 1) * toks] = grad_ref[x, z]
    for pair, parts in enumerate(near):
        for i, s, first in parts:
            for side, j in ((core, i), (1 - core, i + half)):
                copies[j].wait()
                at = aligned((s * NC + side) * piece, piece, 64)
                for z in range(buffers[j].shape[0]):
                    b_buf[at, (first + z) * toks : (first + z + 1) * toks] = buffers[j][z]
        prod = lax.dot_general(
            a_buf[...],
            b_buf[2 * pair * span : 2 * (pair + 1) * span],
            (((1,), (1,)), ((), ())),
            preferred_element_type=F32,
        )
        prod = (prod * scale).astype(BF)
        for i in range(2):
            cols = aligned(lax.rem(y - 2 * pair - i + NY, NY) * span, span, span)
            for x in range(n_x):
                out_ref[x, :, cols] = prod[x * rows : (x + 1) * rows, i * span : (i + 1) * span]


def wgrad_products(place, grads, own, oth, scale):
    n_x, n_z, rows, toks = grads.shape
    feats = NY * NC * own[0].shape[1]
    args = [in_hbm(a) for a in (*own, *oth)]
    vmem = pl.BlockSpec(memory_space=pltpu.VMEM)
    return pl.pallas_call(
        functools.partial(wgrad_kernel, scale=scale),
        in_specs=[pl.BlockSpec(memory_space=pltpu.SMEM), vmem]
        + [pl.BlockSpec(memory_space=pltpu.HBM)] * len(args),
        out_specs=vmem,
        out_shape=pltpu.HBM((n_x, rows, feats), BF),
        scratch_shapes=[pltpu.VMEM(a.shape, BF) for a in args]
        + [
            pltpu.VMEM((n_x * rows, n_z * toks), BF),
            pltpu.VMEM((feats, n_z * toks), BF),
            pltpu.SemaphoreType.DMA((len(args),)),
        ],
        compiler_params=pltpu.CompilerParams(vmem_limit_bytes=28 * MIB),
        name="wgrad_products",
    )(place, grads, *args)


def slots_kernel(meta, prod_ref, out_ref, *, chunk, blk):
    per_x = prod_ref.shape[2] // blk
    for s in range(out_ref.shape[0]):
        hid, mod, full = meta[0, s], meta[1, s], meta[2, s]
        rows = aligned(hid * chunk, chunk, chunk)
        cols = aligned(lax.rem(mod, per_x) * blk, blk, blk)
        part = prod_ref[lax.div(mod, per_x), rows, cols]
        out_ref[s] = jnp.where(full > 0, part, jnp.zeros_like(part))


def pick_slots(meta, prods, chunk, blk):
    owners = meta.shape[1]
    return pl.pallas_call(
        functools.partial(slots_kernel, chunk=chunk, blk=blk),
        in_specs=[
            pl.BlockSpec(memory_space=pltpu.SMEM),
            pl.BlockSpec(memory_space=pltpu.VMEM),
        ],
        out_specs=pl.BlockSpec(memory_space=pltpu.VMEM),
        out_shape=jax.ShapeDtypeStruct((owners, chunk, blk), BF),
        compiler_params=pltpu.CompilerParams(vmem_limit_bytes=12 * MIB),
        name="pick_slots",
    )(meta, prods)


def sum_core_kernel(own_ref, oth_ref, *out_refs):
    for s in range(NY):
        out_refs[s][...] = (own_ref[s].astype(F32) + oth_ref[s].astype(F32)).astype(out_refs[s].dtype)


def sum_y_kernel(*refs):
    parts, out_refs = refs[:NY], refs[NY:]
    for t in range(NX):
        out_refs[t][...] = sum(part[t].astype(F32) for part in parts)


def sum_x_kernel(*refs):
    parts, out_ref = refs[:NX], refs[NX]
    out_ref[...] = sum(part[...] for part in parts).astype(BF)


def small_call(kernel, name, outs, *args):
    return pl.pallas_call(
        kernel,
        in_specs=[pl.BlockSpec(memory_space=pltpu.VMEM)] * len(args),
        out_specs=[pl.BlockSpec(memory_space=pltpu.VMEM)] * len(outs),
        out_shape=outs,
        compiler_params=pltpu.CompilerParams(vmem_limit_bytes=12 * MIB),
        name=name,
    )(*args)


def sum_pair(in_own, in_oth):
    line = lambda dtype: jax.ShapeDtypeStruct(in_own.shape[1:], dtype)
    got = lax.ppermute(in_oth, "col", CORE_SWAP)
    return small_call(sum_core_kernel, "sum_core", [line(F32)] + [line(BF)] * (NY - 1), in_own, got)


def sum_line(by_y):
    _, piece, toks = by_y[0].shape
    got = [by_y[0]] + [lax.ppermute(by_y[s], "col", Y_SHIFTS[s]) for s in range(1, NY)]
    return small_call(sum_y_kernel, "sum_y", [jax.ShapeDtypeStruct((piece, toks), F32)] * NX, *got)


def sum_plane(by_x):
    got = [by_x[0]] + [lax.ppermute(by_x[t], "col", X_SHIFTS[t]) for t in range(1, NX)]
    return small_call(sum_x_kernel, "sum_x", [jax.ShapeDtypeStruct(by_x[0].shape, BF)], *got)[0]


def tables_kernel(at, mask_ref, owner_ref, listed_ref, slots_ref):
    model_blocks = mask_ref.shape[0]
    count, owners = listed_ref.shape[1], slots_ref.shape[1]
    for s in range(owners):
        slots_ref[0, s] = 0
        slots_ref[1, s] = 0
        slots_ref[2, s] = 0

    def look(i, k):
        hid, mod = lax.div(i, model_blocks), lax.rem(i, model_blocks)
        full = mask_ref[mod, at[0] + hid]
        owner = owner_ref[mod, at[0] + hid]

        @pl.when(full == 1)
        def _():
            listed_ref[0, k] = owner
            listed_ref[1, k] = hid
            listed_ref[2, k] = mod
            slots_ref[0, owner] = hid
            slots_ref[1, owner] = mod
            slots_ref[2, owner] = 1

        return k + full

    lax.fori_loop(0, count * 4, look, 0)


def layout_tables(block_mask, block_owner, group, n_groups, owners):
    hidden_blocks, model_blocks = block_mask.shape
    per_group = hidden_blocks // n_groups
    smem = pl.BlockSpec(memory_space=pltpu.SMEM)
    return pl.pallas_call(
        tables_kernel,
        in_specs=[smem] * 3,
        out_specs=[smem] * 2,
        out_shape=[
            jax.ShapeDtypeStruct((3, per_group * model_blocks // 4), jnp.int32),
            jax.ShapeDtypeStruct((3, owners), jnp.int32),
        ],
        name="layout_tables",
    )((group * per_group).reshape(1).astype(jnp.int32), block_mask.T, block_owner.T)


def spread_kernel(in_ref, out_ref, sems):
    copies = [pltpu.make_async_copy(in_ref, out_ref.at[i], sems.at[i]) for i in range(out_ref.shape[0])]
    for copy in copies:
        copy.start()
    for copy in copies:
        copy.wait()


def spread(x, n):
    return pl.pallas_call(
        spread_kernel,
        in_specs=[pl.BlockSpec(memory_space=pltpu.VMEM)],
        out_specs=pl.BlockSpec(memory_space=pltpu.HBM),
        out_shape=pltpu.HBM((n, *x.shape), x.dtype),
        scratch_shapes=[pltpu.SemaphoreType.DMA((n,))],
        compiler_params=pltpu.CompilerParams(vmem_limit_bytes=4 * MIB),
        name="spread",
    )(x)


def share_y(x):
    half = x.shape[0] // 2
    before = lax.ppermute(x, "col", Y_SHIFTS[1])
    after = lax.ppermute(x, "col", Y_SHIFTS[NY - 1])
    far_lo = lax.ppermute(before[:half], "col", Y_SHIFTS[1])
    far_hi = lax.ppermute(after[half:], "col", Y_SHIFTS[NY - 1])
    return x, before, far_lo, far_hi, after


def per_device(activations, out_grad, weight_slots, block_mask, block_owner):
    blk = weight_slots.shape[2]
    owners, groups = lax.axis_size("row"), lax.axis_size("col")
    group = lax.axis_index("col")
    toks, piece = activations.shape
    hidden = out_grad.shape[1]
    chunk = blk // owners
    rows = hidden // owners
    listed, slots = layout_tables(block_mask, block_owner, group, groups, owners)
    place = jnp.stack([group // (NY * NC), group // NC % NY, group % NC]).astype(jnp.int32)

    w_all = lax.all_gather(weight_slots[0, 0], "row", axis=0)
    act_t = activations.T
    act_all = lax.all_to_all(spread(act_t, groups), "col", 0, 0, tiled=True).reshape(groups * piece, toks)
    act_z = lax.all_gather(act_t, "row", axis=0)

    grad_send = out_grad.T.reshape(-1, owners, chunk, toks).transpose(1, 0, 2, 3)
    grad_send = grad_send.reshape(owners, rows, toks)
    grad_send, act_z, act_all = lax.optimization_barrier((grad_send, act_z, act_all))
    grad_z = lax.all_to_all(grad_send, "row", 0, 0, tiled=True)
    here, before, far_lo, far_hi, after = share_y(act_z)
    grad_z, far_lo, far_hi, listed, slots = lax.optimization_barrier((grad_z, far_lo, far_hi, listed, slots))
    act_own = here, before, far_lo, far_hi, after
    act_oth = [lax.ppermute(a, "col", CORE_SWAP) for a in act_own]
    grad_x = lax.all_to_all(spread(grad_z, NX), "col", 0, 0, tiled=True, axis_index_groups=X_GROUPS)

    prods = wgrad_products(place, grad_x, act_own, act_oth, 1.0 / math.sqrt(toks * owners))
    prods = lax.all_to_all(prods, "col", 0, 0, tiled=True, axis_index_groups=X_GROUPS)
    slot_parts = pick_slots(slots, prods, chunk, blk)

    in_own, in_oth = in_step(listed, place, out_grad, w_all, groups * piece)
    by_y = sum_pair(in_own, in_oth)
    slot_parts, by_y, act_all = lax.optimization_barrier((slot_parts, by_y, act_all))
    weight_grad = lax.all_to_all(slot_parts, "row", 0, 0, tiled=True).reshape(1, 1, blk, blk)
    by_x, outputs = lax.optimization_barrier((sum_line(by_y), out_step(listed, act_all, w_all, hidden)))
    return outputs, sum_plane(by_x).T, weight_grad


def solution(mesh):
    placed = (P("row", "col"), P("row", "col"), P("col", "row", None, None), P(), P())
    return jax.shard_map(
        per_device,
        mesh=mesh,
        in_specs=placed,
        out_specs=(P("row", "col"), P("row", "col"), P("col", "row", None, None)),
        check_vma=False,
    )
```

```python
import functools
import math

import jax
import jax.numpy as jnp
from jax import lax
from jax.experimental import pallas as pl
from jax.experimental.pallas import tpu as pltpu
from jax.sharding import PartitionSpec as P

BF = jnp.bfloat16
F32 = jnp.float32
NX, NY, NC = 4, 4, 2
MIB = 1024 * 1024


def col_of(x, y, c):
    return (x * NY + y) * NC + c


PLANE = [(x, y, c) for x in range(NX) for y in range(NY) for c in range(NC)]
X_GROUPS = [[col_of(x, y, c) for x in range(NX)] for y in range(NY) for c in range(NC)]
CORE_SWAP = [(col_of(x, y, c), col_of(x, y, 1 - c)) for x, y, c in PLANE]
X_SHIFTS = {s: [(col_of(x, y, c), col_of((x + s) % NX, y, c)) for x, y, c in PLANE] for s in range(1, NX)}
Y_SHIFTS = {s: [(col_of(x, y, c), col_of(x, (y + s) % NY, c)) for x, y, c in PLANE] for s in range(1, NY)}


def aligned(start, size, step):
    return pl.ds(pl.multiple_of(start, step), size)


def slot_copies(meta, w_ref, w_buf, sems):
    copies = [
        pltpu.make_async_copy(w_ref.at[meta[0, k]], w_buf.at[k], sems.at[k]) for k in range(w_buf.shape[0])
    ]
    for copy in copies:
        copy.start()
    return copies


def in_kernel(meta, place, grad_ref, w_ref, in_own, in_oth, w_buf, in_acc, in_rows, sems):
    count, blk, _ = w_buf.shape
    piece = in_own.shape[2]
    x, y, core = place[0], place[1], place[2]
    copies = slot_copies(meta, w_ref, w_buf, sems)
    in_acc[...] = jnp.zeros_like(in_acc)
    for k in range(count):
        hid = aligned(meta[1, k] * blk, blk, blk)
        mod = aligned(meta[2, k] * blk, blk, blk)
        copies[k].wait()
        in_acc[:, mod] += jnp.dot(grad_ref[:, hid], w_buf[k], preferred_element_type=F32)
    in_rows[...] = in_acc[...].T.astype(BF)
    for s in range(NY):
        for t in range(NX):
            chip = (lax.rem(x + t, NX) * NY + lax.rem(y + s, NY)) * NC
            in_own[s, t] = in_rows[aligned((chip + core) * piece, piece, 64), :]
            in_oth[s, t] = in_rows[aligned((chip + 1 - core) * piece, piece, 64), :]


def in_step(meta, place, grad, w_all, feats):
    count, blk = meta.shape[1], w_all.shape[1]
    toks = grad.shape[0]
    parts = pltpu.HBM((NY, NX, feats // (NX * NY * NC), toks), BF)
    vmem = pl.BlockSpec(memory_space=pltpu.VMEM)
    smem = pl.BlockSpec(memory_space=pltpu.SMEM)
    return pl.pallas_call(
        in_kernel,
        in_specs=[smem, smem, vmem, pl.BlockSpec(memory_space=pltpu.HBM)],
        out_specs=[vmem] * 2,
        out_shape=[parts, parts],
        scratch_shapes=[
            pltpu.VMEM((count, blk, blk), BF),
            pltpu.VMEM((toks, feats), F32),
            pltpu.VMEM((feats, toks), BF),
            pltpu.SemaphoreType.DMA((count,)),
        ],
        compiler_params=pltpu.CompilerParams(vmem_limit_bytes=24 * MIB),
        name="in_step",
    )(meta, place, grad, in_hbm(w_all))


def out_kernel(meta, act_ref, w_ref, out_ref, w_buf, out_acc, sems):
    count, blk, _ = w_buf.shape
    copies = slot_copies(meta, w_ref, w_buf, sems)
    out_acc[...] = jnp.zeros_like(out_acc)
    for k in range(count):
        hid = aligned(meta[1, k] * blk, blk, blk)
        mod = aligned(meta[2, k] * blk, blk, blk)
        copies[k].wait()
        out_acc[hid, :] += jnp.dot(w_buf[k], act_ref[mod, :], preferred_element_type=F32)
    out_ref[...] = out_acc[...].T.astype(BF)


def out_step(meta, act, w_all, hidden):
    count, blk = meta.shape[1], w_all.shape[1]
    toks = act.shape[1]
    vmem = pl.BlockSpec(memory_space=pltpu.VMEM)
    return pl.pallas_call(
        out_kernel,
        in_specs=[pl.BlockSpec(memory_space=pltpu.SMEM), vmem, pl.BlockSpec(memory_space=pltpu.HBM)],
        out_specs=vmem,
        out_shape=jax.ShapeDtypeStruct((toks, hidden), BF),
        scratch_shapes=[
            pltpu.VMEM((count, blk, blk), BF),
            pltpu.VMEM((hidden, toks), F32),
            pltpu.SemaphoreType.DMA((count,)),
        ],
        compiler_params=pltpu.CompilerParams(vmem_limit_bytes=16 * MIB),
        name="out_step",
    )(meta, act, in_hbm(w_all))


def in_hbm(x):
    return pltpu.with_memory_space_constraint(x, pltpu.HBM)


def wgrad_kernel(place, grad_ref, *refs, scale):
    act_refs, (out_ref, a_buf, b_buf, sems) = refs[:-4], refs[-4:]
    n_x, n_z, rows, toks = grad_ref.shape
    piece = act_refs[0].shape[1]
    y, core = place[1], place[2]
    parts = ((0, 0), (1, 0), (2, 0), (2, n_z // 2), (3, 0))
    copies = [[] for _ in range(NY)]
    count = 0
    for i, (s, first) in enumerate(parts):
        for side, ref in ((core, act_refs[i]), (1 - core, act_refs[i + len(parts)])):
            at = aligned((s * NC + side) * piece, piece, 64)
            for z in range(ref.shape[0]):
                lanes = pl.ds((first + z) * toks, toks)
                copies[s].append(pltpu.make_async_copy(ref.at[z], b_buf.at[at, lanes], sems.at[count]))
                count += 1
    for line in copies:
        for copy in line:
            copy.start()
    for x in range(n_x):
        for z in range(n_z):
            a_buf[x * rows : (x + 1) * rows, z * toks : (z + 1) * toks] = grad_ref[x, z]
    span = NC * piece
    for line in copies:
        for copy in line:
            copy.wait()
    prod = lax.dot_general(
        a_buf[...], b_buf[...], (((1,), (1,)), ((), ())), preferred_element_type=F32
    )
    prod = (prod * scale).astype(BF)
    for s in range(NY):
        cols = aligned(lax.rem(y - s + NY, NY) * span, span, span)
        for x in range(n_x):
            out_ref[x, :, cols] = prod[x * rows : (x + 1) * rows, s * span : (s + 1) * span]


def wgrad_products(place, grads, own, oth, scale):
    n_x, n_z, rows, toks = grads.shape
    feats = NY * NC * own[0].shape[1]
    args = [in_hbm(a) for a in (*own, *oth)]
    vmem = pl.BlockSpec(memory_space=pltpu.VMEM)
    return pl.pallas_call(
        functools.partial(wgrad_kernel, scale=scale),
        in_specs=[pl.BlockSpec(memory_space=pltpu.SMEM), vmem]
        + [pl.BlockSpec(memory_space=pltpu.HBM)] * len(args),
        out_specs=vmem,
        out_shape=pltpu.HBM((n_x, rows, feats), BF),
        scratch_shapes=[
            pltpu.VMEM((n_x * rows, n_z * toks), BF),
            pltpu.VMEM((feats, n_z * toks), BF),
            pltpu.SemaphoreType.DMA((NY * NC * n_z,)),
        ],
        compiler_params=pltpu.CompilerParams(vmem_limit_bytes=20 * MIB),
        name="wgrad_products",
    )(place, grads, *args)


def slots_kernel(meta, prod_ref, out_ref, *, chunk, blk):
    per_x = prod_ref.shape[2] // blk
    for s in range(out_ref.shape[0]):
        hid, mod, full = meta[0, s], meta[1, s], meta[2, s]
        rows = aligned(hid * chunk, chunk, chunk)
        cols = aligned(lax.rem(mod, per_x) * blk, blk, blk)
        part = prod_ref[lax.div(mod, per_x), rows, cols]
        out_ref[s] = jnp.where(full > 0, part, jnp.zeros_like(part))


def pick_slots(meta, prods, chunk, blk):
    owners = meta.shape[1]
    return pl.pallas_call(
        functools.partial(slots_kernel, chunk=chunk, blk=blk),
        in_specs=[
            pl.BlockSpec(memory_space=pltpu.SMEM),
            pl.BlockSpec(memory_space=pltpu.VMEM),
        ],
        out_specs=pl.BlockSpec(memory_space=pltpu.VMEM),
        out_shape=jax.ShapeDtypeStruct((owners, chunk, blk), BF),
        compiler_params=pltpu.CompilerParams(vmem_limit_bytes=12 * MIB),
        name="pick_slots",
    )(meta, prods)


def sum_core_kernel(own_ref, oth_ref, *out_refs):
    for s in range(NY):
        out_refs[s][...] = (own_ref[s].astype(F32) + oth_ref[s].astype(F32)).astype(out_refs[s].dtype)


def sum_y_kernel(*refs):
    parts, out_refs = refs[:NY], refs[NY:]
    for t in range(NX):
        out_refs[t][...] = sum(part[t].astype(F32) for part in parts)


def sum_x_kernel(*refs):
    parts, out_ref = refs[:NX], refs[NX]
    out_ref[...] = sum(part[...] for part in parts).astype(BF)


def small_call(kernel, name, outs, *args):
    return pl.pallas_call(
        kernel,
        in_specs=[pl.BlockSpec(memory_space=pltpu.VMEM)] * len(args),
        out_specs=[pl.BlockSpec(memory_space=pltpu.VMEM)] * len(outs),
        out_shape=outs,
        compiler_params=pltpu.CompilerParams(vmem_limit_bytes=12 * MIB),
        name=name,
    )(*args)


def sum_pair(in_own, in_oth):
    line = lambda dtype: jax.ShapeDtypeStruct(in_own.shape[1:], dtype)
    got = lax.ppermute(in_oth, "col", CORE_SWAP)
    return small_call(sum_core_kernel, "sum_core", [line(F32)] + [line(BF)] * (NY - 1), in_own, got)


def sum_line(by_y):
    _, piece, toks = by_y[0].shape
    got = [by_y[0]] + [lax.ppermute(by_y[s], "col", Y_SHIFTS[s]) for s in range(1, NY)]
    return small_call(sum_y_kernel, "sum_y", [jax.ShapeDtypeStruct((piece, toks), F32)] * NX, *got)


def sum_plane(by_x):
    got = [by_x[0]] + [lax.ppermute(by_x[t], "col", X_SHIFTS[t]) for t in range(1, NX)]
    return small_call(sum_x_kernel, "sum_x", [jax.ShapeDtypeStruct(by_x[0].shape, BF)], *got)[0]


def tables_kernel(at, mask_ref, owner_ref, listed_ref, slots_ref):
    model_blocks = mask_ref.shape[0]
    count, owners = listed_ref.shape[1], slots_ref.shape[1]
    for s in range(owners):
        slots_ref[0, s] = 0
        slots_ref[1, s] = 0
        slots_ref[2, s] = 0

    def look(i, k):
        hid, mod = lax.div(i, model_blocks), lax.rem(i, model_blocks)
        full = mask_ref[mod, at[0] + hid]
        owner = owner_ref[mod, at[0] + hid]

        @pl.when(full == 1)
        def _():
            listed_ref[0, k] = owner
            listed_ref[1, k] = hid
            listed_ref[2, k] = mod
            slots_ref[0, owner] = hid
            slots_ref[1, owner] = mod
            slots_ref[2, owner] = 1

        return k + full

    lax.fori_loop(0, count * 4, look, 0)


def layout_tables(block_mask, block_owner, group, n_groups, owners):
    hidden_blocks, model_blocks = block_mask.shape
    per_group = hidden_blocks // n_groups
    smem = pl.BlockSpec(memory_space=pltpu.SMEM)
    return pl.pallas_call(
        tables_kernel,
        in_specs=[smem] * 3,
        out_specs=[smem] * 2,
        out_shape=[
            jax.ShapeDtypeStruct((3, per_group * model_blocks // 4), jnp.int32),
            jax.ShapeDtypeStruct((3, owners), jnp.int32),
        ],
        name="layout_tables",
    )((group * per_group).reshape(1).astype(jnp.int32), block_mask.T, block_owner.T)


def spread_kernel(in_ref, out_ref, sems):
    copies = [pltpu.make_async_copy(in_ref, out_ref.at[i], sems.at[i]) for i in range(out_ref.shape[0])]
    for copy in copies:
        copy.start()
    for copy in copies:
        copy.wait()


def spread(x, n):
    return pl.pallas_call(
        spread_kernel,
        in_specs=[pl.BlockSpec(memory_space=pltpu.VMEM)],
        out_specs=pl.BlockSpec(memory_space=pltpu.HBM),
        out_shape=pltpu.HBM((n, *x.shape), x.dtype),
        scratch_shapes=[pltpu.SemaphoreType.DMA((n,))],
        compiler_params=pltpu.CompilerParams(vmem_limit_bytes=4 * MIB),
        name="spread",
    )(x)


def share_y(x):
    half = x.shape[0] // 2
    before = lax.ppermute(x, "col", Y_SHIFTS[1])
    after = lax.ppermute(x, "col", Y_SHIFTS[NY - 1])
    far_lo = lax.ppermute(before[:half], "col", Y_SHIFTS[1])
    far_hi = lax.ppermute(after[half:], "col", Y_SHIFTS[NY - 1])
    return x, before, far_lo, far_hi, after


def per_device(activations, out_grad, weight_slots, block_mask, block_owner):
    blk = weight_slots.shape[2]
    owners, groups = lax.axis_size("row"), lax.axis_size("col")
    group = lax.axis_index("col")
    toks, piece = activations.shape
    hidden = out_grad.shape[1]
    chunk = blk // owners
    rows = hidden // owners
    listed, slots = layout_tables(block_mask, block_owner, group, groups, owners)
    place = jnp.stack([group // (NY * NC), group // NC % NY, group % NC]).astype(jnp.int32)

    w_all = lax.all_gather(weight_slots[0, 0], "row", axis=0)
    act_t = activations.T
    act_all = lax.all_to_all(spread(act_t, groups), "col", 0, 0, tiled=True).reshape(groups * piece, toks)
    act_z = lax.all_gather(act_t, "row", axis=0)

    grad_send = out_grad.T.reshape(-1, owners, chunk, toks).transpose(1, 0, 2, 3)
    grad_send = grad_send.reshape(owners, rows, toks)
    grad_send, act_z, act_all = lax.optimization_barrier((grad_send, act_z, act_all))
    grad_z = lax.all_to_all(grad_send, "row", 0, 0, tiled=True)
    here, before, far_lo, far_hi, after = share_y(act_z)
    grad_z, far_lo, far_hi, listed, slots = lax.optimization_barrier((grad_z, far_lo, far_hi, listed, slots))
    act_own = here, before, far_lo, far_hi, after
    act_oth = [lax.ppermute(a, "col", CORE_SWAP) for a in act_own]
    grad_x = lax.all_to_all(spread(grad_z, NX), "col", 0, 0, tiled=True, axis_index_groups=X_GROUPS)

    prods = wgrad_products(place, grad_x, act_own, act_oth, 1.0 / math.sqrt(toks * owners))
    prods = lax.all_to_all(prods, "col", 0, 0, tiled=True, axis_index_groups=X_GROUPS)
    slot_parts = pick_slots(slots, prods, chunk, blk)

    in_own, in_oth = in_step(listed, place, out_grad, w_all, groups * piece)
    by_y = sum_pair(in_own, in_oth)
    slot_parts, by_y, act_all = lax.optimization_barrier((slot_parts, by_y, act_all))
    weight_grad = lax.all_to_all(slot_parts, "row", 0, 0, tiled=True).reshape(1, 1, blk, blk)
    by_x, outputs = lax.optimization_barrier((sum_line(by_y), out_step(listed, act_all, w_all, hidden)))
    return outputs, sum_plane(by_x).T, weight_grad


def solution(mesh):
    placed = (P("row", "col"), P("row", "col"), P("col", "row", None, None), P(), P())
    return jax.shard_map(
        per_device,
        mesh=mesh,
        in_specs=placed,
        out_specs=(P("row", "col"), P("row", "col"), P("col", "row", None, None)),
        check_vma=False,
    )
```

```python
import functools
import math

import jax
import jax.numpy as jnp
from jax import lax
from jax.experimental import pallas as pl
from jax.experimental.pallas import tpu as pltpu
from jax.sharding import PartitionSpec as P

BF = jnp.bfloat16
F32 = jnp.float32
NX, NY, NC = 4, 4, 2
MIB = 1024 * 1024


def col_of(x, y, c):
    return (x * NY + y) * NC + c


PLANE = [(x, y, c) for x in range(NX) for y in range(NY) for c in range(NC)]
X_GROUPS = [[col_of(x, y, c) for x in range(NX)] for y in range(NY) for c in range(NC)]
CORE_SWAP = [(col_of(x, y, c), col_of(x, y, 1 - c)) for x, y, c in PLANE]
X_SHIFTS = {s: [(col_of(x, y, c), col_of((x + s) % NX, y, c)) for x, y, c in PLANE] for s in range(1, NX)}
Y_SHIFTS = {s: [(col_of(x, y, c), col_of(x, (y + s) % NY, c)) for x, y, c in PLANE] for s in range(1, NY)}


def aligned(start, size, step):
    return pl.ds(pl.multiple_of(start, step), size)


def tokens_kernel(meta, place, act_ref, grad_ref, w_ref, out_ref, in_own, in_oth, w_buf, out_acc, in_acc, in_rows, sems):
    count, blk, _ = w_buf.shape
    piece = in_own.shape[2]
    x, y, core = place[0], place[1], place[2]
    copies = [pltpu.make_async_copy(w_ref.at[meta[0, k]], w_buf.at[k], sems.at[k]) for k in range(count)]
    for copy in copies:
        copy.start()
    out_acc[...] = jnp.zeros_like(out_acc)
    in_acc[...] = jnp.zeros_like(in_acc)
    for k in range(count):
        hid = aligned(meta[1, k] * blk, blk, blk)
        mod = aligned(meta[2, k] * blk, blk, blk)
        copies[k].wait()
        w = w_buf[k]
        out_acc[hid, :] += jnp.dot(w, act_ref[mod, :], preferred_element_type=F32)
        in_acc[:, mod] += jnp.dot(grad_ref[:, hid], w, preferred_element_type=F32)
    out_ref[...] = out_acc[...].T.astype(BF)
    in_rows[...] = in_acc[...].T.astype(BF)
    for s in range(NY):
        for t in range(NX):
            chip = (lax.rem(x + t, NX) * NY + lax.rem(y + s, NY)) * NC
            in_own[s, t] = in_rows[aligned((chip + core) * piece, piece, 64), :]
            in_oth[s, t] = in_rows[aligned((chip + 1 - core) * piece, piece, 64), :]


def tokens_step(meta, place, act, grad, w_all):
    count, blk = meta.shape[1], w_all.shape[1]
    feats, toks = act.shape
    hidden = grad.shape[1]
    parts = pltpu.HBM((NY, NX, feats // (NX * NY * NC), toks), BF)
    vmem = pl.BlockSpec(memory_space=pltpu.VMEM)
    smem = pl.BlockSpec(memory_space=pltpu.SMEM)
    return pl.pallas_call(
        tokens_kernel,
        in_specs=[smem, smem, vmem, vmem, pl.BlockSpec(memory_space=pltpu.HBM)],
        out_specs=[vmem] * 3,
        out_shape=[jax.ShapeDtypeStruct((toks, hidden), BF), parts, parts],
        scratch_shapes=[
            pltpu.VMEM((count, blk, blk), BF),
            pltpu.VMEM((hidden, toks), F32),
            pltpu.VMEM((toks, feats), F32),
            pltpu.VMEM((feats, toks), BF),
            pltpu.SemaphoreType.DMA((count,)),
        ],
        compiler_params=pltpu.CompilerParams(vmem_limit_bytes=28 * MIB),
        name="tokens_step",
    )(meta, place, act, grad, in_hbm(w_all))


def in_hbm(x):
    return pltpu.with_memory_space_constraint(x, pltpu.HBM)


def wgrad_kernel(place, grad_ref, *refs, scale):
    act_refs, (out_ref, a_buf, b_buf, sems) = refs[:-4], refs[-4:]
    n_x, n_z, rows, toks = grad_ref.shape
    piece = act_refs[0].shape[1]
    y, core = place[1], place[2]
    parts = ((0, 0), (1, 0), (2, 0), (2, n_z // 2), (3, 0))
    copies = [[] for _ in range(NY)]
    count = 0
    for i, (s, first) in enumerate(parts):
        for side, ref in ((core, act_refs[i]), (1 - core, act_refs[i + len(parts)])):
            at = aligned((s * NC + side) * piece, piece, 64)
            for z in range(ref.shape[0]):
                lanes = pl.ds((first + z) * toks, toks)
                copies[s].append(pltpu.make_async_copy(ref.at[z], b_buf.at[at, lanes], sems.at[count]))
                count += 1
    for line in copies:
        for copy in line:
            copy.start()
    for x in range(n_x):
        for z in range(n_z):
            a_buf[x * rows : (x + 1) * rows, z * toks : (z + 1) * toks] = grad_ref[x, z]
    span = NC * piece
    for line in copies:
        for copy in line:
            copy.wait()
    prod = lax.dot_general(
        a_buf[...], b_buf[...], (((1,), (1,)), ((), ())), preferred_element_type=F32
    )
    prod = (prod * scale).astype(BF)
    for s in range(NY):
        cols = aligned(lax.rem(y - s + NY, NY) * span, span, span)
        for x in range(n_x):
            out_ref[x, :, cols] = prod[x * rows : (x + 1) * rows, s * span : (s + 1) * span]


def wgrad_products(place, grads, own, oth, scale):
    n_x, n_z, rows, toks = grads.shape
    feats = NY * NC * own[0].shape[1]
    args = [in_hbm(a) for a in (*own, *oth)]
    vmem = pl.BlockSpec(memory_space=pltpu.VMEM)
    return pl.pallas_call(
        functools.partial(wgrad_kernel, scale=scale),
        in_specs=[pl.BlockSpec(memory_space=pltpu.SMEM), vmem]
        + [pl.BlockSpec(memory_space=pltpu.HBM)] * len(args),
        out_specs=vmem,
        out_shape=pltpu.HBM((n_x, rows, feats), BF),
        scratch_shapes=[
            pltpu.VMEM((n_x * rows, n_z * toks), BF),
            pltpu.VMEM((feats, n_z * toks), BF),
            pltpu.SemaphoreType.DMA((NY * NC * n_z,)),
        ],
        compiler_params=pltpu.CompilerParams(vmem_limit_bytes=20 * MIB),
        name="wgrad_products",
    )(place, grads, *args)


def slots_kernel(meta, prod_ref, out_ref, *, chunk, blk):
    per_x = prod_ref.shape[2] // blk
    for s in range(out_ref.shape[0]):
        hid, mod, full = meta[0, s], meta[1, s], meta[2, s]
        rows = aligned(hid * chunk, chunk, chunk)
        cols = aligned(lax.rem(mod, per_x) * blk, blk, blk)
        part = prod_ref[lax.div(mod, per_x), rows, cols]
        out_ref[s] = jnp.where(full > 0, part, jnp.zeros_like(part))


def pick_slots(meta, prods, chunk, blk):
    owners = meta.shape[1]
    return pl.pallas_call(
        functools.partial(slots_kernel, chunk=chunk, blk=blk),
        in_specs=[
            pl.BlockSpec(memory_space=pltpu.SMEM),
            pl.BlockSpec(memory_space=pltpu.VMEM),
        ],
        out_specs=pl.BlockSpec(memory_space=pltpu.VMEM),
        out_shape=jax.ShapeDtypeStruct((owners, chunk, blk), BF),
        compiler_params=pltpu.CompilerParams(vmem_limit_bytes=12 * MIB),
        name="pick_slots",
    )(meta, prods)


def sum_core_kernel(own_ref, oth_ref, *out_refs):
    for s in range(NY):
        out_refs[s][...] = (own_ref[s].astype(F32) + oth_ref[s].astype(F32)).astype(out_refs[s].dtype)


def sum_y_kernel(*refs):
    parts, out_refs = refs[:NY], refs[NY:]
    for t in range(NX):
        out_refs[t][...] = sum(part[t].astype(F32) for part in parts)


def sum_x_kernel(*refs):
    parts, out_ref = refs[:NX], refs[NX]
    out_ref[...] = sum(part[...] for part in parts).astype(BF)


def small_call(kernel, name, outs, *args):
    return pl.pallas_call(
        kernel,
        in_specs=[pl.BlockSpec(memory_space=pltpu.VMEM)] * len(args),
        out_specs=[pl.BlockSpec(memory_space=pltpu.VMEM)] * len(outs),
        out_shape=outs,
        compiler_params=pltpu.CompilerParams(vmem_limit_bytes=12 * MIB),
        name=name,
    )(*args)


def sum_pair(in_own, in_oth):
    line = lambda dtype: jax.ShapeDtypeStruct(in_own.shape[1:], dtype)
    got = lax.ppermute(in_oth, "col", CORE_SWAP)
    return small_call(sum_core_kernel, "sum_core", [line(F32)] + [line(BF)] * (NY - 1), in_own, got)


def sum_plane(by_y):
    _, piece, toks = by_y[0].shape
    got = [by_y[0]] + [lax.ppermute(by_y[s], "col", Y_SHIFTS[s]) for s in range(1, NY)]
    by_x = small_call(sum_y_kernel, "sum_y", [jax.ShapeDtypeStruct((piece, toks), F32)] * NX, *got)
    got = [by_x[0]] + [lax.ppermute(by_x[t], "col", X_SHIFTS[t]) for t in range(1, NX)]
    return small_call(sum_x_kernel, "sum_x", [jax.ShapeDtypeStruct((piece, toks), BF)], *got)[0]


def tables_kernel(at, mask_ref, owner_ref, listed_ref, slots_ref):
    model_blocks = mask_ref.shape[0]
    count, owners = listed_ref.shape[1], slots_ref.shape[1]
    for s in range(owners):
        slots_ref[0, s] = 0
        slots_ref[1, s] = 0
        slots_ref[2, s] = 0

    def look(i, k):
        hid, mod = lax.div(i, model_blocks), lax.rem(i, model_blocks)
        full = mask_ref[mod, at[0] + hid]
        owner = owner_ref[mod, at[0] + hid]

        @pl.when(full == 1)
        def _():
            listed_ref[0, k] = owner
            listed_ref[1, k] = hid
            listed_ref[2, k] = mod
            slots_ref[0, owner] = hid
            slots_ref[1, owner] = mod
            slots_ref[2, owner] = 1

        return k + full

    lax.fori_loop(0, count * 4, look, 0)


def layout_tables(block_mask, block_owner, group, n_groups, owners):
    hidden_blocks, model_blocks = block_mask.shape
    per_group = hidden_blocks // n_groups
    smem = pl.BlockSpec(memory_space=pltpu.SMEM)
    return pl.pallas_call(
        tables_kernel,
        in_specs=[smem] * 3,
        out_specs=[smem] * 2,
        out_shape=[
            jax.ShapeDtypeStruct((3, per_group * model_blocks // 4), jnp.int32),
            jax.ShapeDtypeStruct((3, owners), jnp.int32),
        ],
        name="layout_tables",
    )((group * per_group).reshape(1).astype(jnp.int32), block_mask.T, block_owner.T)


def spread_kernel(in_ref, out_ref, sems):
    copies = [pltpu.make_async_copy(in_ref, out_ref.at[i], sems.at[i]) for i in range(out_ref.shape[0])]
    for copy in copies:
        copy.start()
    for copy in copies:
        copy.wait()


def spread(x, n):
    return pl.pallas_call(
        spread_kernel,
        in_specs=[pl.BlockSpec(memory_space=pltpu.VMEM)],
        out_specs=pl.BlockSpec(memory_space=pltpu.HBM),
        out_shape=pltpu.HBM((n, *x.shape), x.dtype),
        scratch_shapes=[pltpu.SemaphoreType.DMA((n,))],
        compiler_params=pltpu.CompilerParams(vmem_limit_bytes=4 * MIB),
        name="spread",
    )(x)


def share_y(x):
    half = x.shape[0] // 2
    before = lax.ppermute(x, "col", Y_SHIFTS[1])
    after = lax.ppermute(x, "col", Y_SHIFTS[NY - 1])
    far_lo = lax.ppermute(before[:half], "col", Y_SHIFTS[1])
    far_hi = lax.ppermute(after[half:], "col", Y_SHIFTS[NY - 1])
    return x, before, far_lo, far_hi, after


def per_device(activations, out_grad, weight_slots, block_mask, block_owner):
    blk = weight_slots.shape[2]
    owners, groups = lax.axis_size("row"), lax.axis_size("col")
    group = lax.axis_index("col")
    toks, piece = activations.shape
    hidden = out_grad.shape[1]
    chunk = blk // owners
    rows = hidden // owners
    listed, slots = layout_tables(block_mask, block_owner, group, groups, owners)
    place = jnp.stack([group // (NY * NC), group // NC % NY, group % NC]).astype(jnp.int32)

    w_all = lax.all_gather(weight_slots[0, 0], "row", axis=0)
    act_t = activations.T
    act_all = lax.all_to_all(spread(act_t, groups), "col", 0, 0, tiled=True).reshape(groups * piece, toks)
    act_z = lax.all_gather(act_t, "row", axis=0)

    grad_send = out_grad.T.reshape(-1, owners, chunk, toks).transpose(1, 0, 2, 3)
    grad_send = grad_send.reshape(owners, rows, toks)
    grad_send, act_z, act_all = lax.optimization_barrier((grad_send, act_z, act_all))
    grad_z = lax.all_to_all(grad_send, "row", 0, 0, tiled=True)
    here, before, far_lo, far_hi, after = share_y(act_z)
    grad_z, far_lo, far_hi, listed, slots = lax.optimization_barrier((grad_z, far_lo, far_hi, listed, slots))
    act_own = here, before, far_lo, far_hi, after
    act_oth = [lax.ppermute(a, "col", CORE_SWAP) for a in act_own]
    grad_x = lax.all_to_all(spread(grad_z, NX), "col", 0, 0, tiled=True, axis_index_groups=X_GROUPS)

    prods = wgrad_products(place, grad_x, act_own, act_oth, 1.0 / math.sqrt(toks * owners))
    prods = lax.all_to_all(prods, "col", 0, 0, tiled=True, axis_index_groups=X_GROUPS)
    slot_parts = pick_slots(slots, prods, chunk, blk)

    outputs, in_own, in_oth = tokens_step(listed, place, act_all, out_grad, w_all)
    by_y = sum_pair(in_own, in_oth)
    slot_parts, by_y = lax.optimization_barrier((slot_parts, by_y))
    weight_grad = lax.all_to_all(slot_parts, "row", 0, 0, tiled=True).reshape(1, 1, blk, blk)
    return outputs, sum_plane(by_y).T, weight_grad


def solution(mesh):
    placed = (P("row", "col"), P("row", "col"), P("col", "row", None, None), P(), P())
    return jax.shard_map(
        per_device,
        mesh=mesh,
        in_specs=placed,
        out_specs=(P("row", "col"), P("row", "col"), P("col", "row", None, None)),
        check_vma=False,
    )
```
